32 devices in a mesh: rows: 8 (over z, y), heads: 4 (over x, core).
Axes of the slice: x: 2, y: 2, z: 4, core: 2. Of those that a mesh axis runs over, the one named last changes fastest.
Arguments:
- alignment_embedding: bfloat16 [128, 768, 128], P('rows', 'heads'), may hold values from -6 to 6
- line_group_label: int32 [128], replicated, may hold values from 0 to 3, never falling along the last dimension, each value on 1 to 80 neighbouring positions
- group_site_tally: int32 [4], replicated, may hold values from 32 to 128, as said below
- horizontal_triple_matrix: bfloat16 [3, 768, 768], P(None, 'heads'), may hold values from -0.25 to 0.25
- horizontal_mixing_matrix: bfloat16 [768, 768], P('heads'), may hold values from -0.21875 to 0.21875
- vertical_triple_matrix: bfloat16 [3, 768, 768], P(None, 'heads'), may hold values from -0.25 to 0.25
- vertical_mixing_matrix: bfloat16 [768, 768], P('heads'), may hold values from -0.21875 to 0.21875
- expand_matrix: bfloat16 [768, 3072], P(None, 'heads'), may hold values from -0.21875 to 0.21875
- contract_matrix: bfloat16 [3072, 768], P('heads'), may hold values from -0.109375 to 0.109375
Outputs:
- layer_out: bfloat16 [128, 768, 128], P('rows', 'heads')
The draws below stay inside these ranges and needn't reach their ends.
Inputs may be any that keep to these rules, and one draw needn't show every extreme that they name: `line_group_label`: family ids never fall along the rows; each of the 4 families holds 1 to 80 rows, one family exactly 80. `group_site_tally`: positions at or beyond a family's length are padding; some family has exactly 128.
All inputs are finite; a program needn't handle non-finite values.
Results may differ from the reference program's by a relative error of at most 0.015.
Values may be sent and summed in bfloat16 or wider, within the bound.
No kernel may reach another device: no remote copies, remote signals or barrier semaphores. Data moves between devices by JAX's collectives and lax.ppermute only.
A program may use at most 64 MiB of HBM per device.

```python
import math
import jax
import jax.numpy as jnp
import numpy as np
from jax import lax

EMBED_FEATURES = 768
ATTENTION_PARTS = 12
HIDDEN_UNITS = 3072
SITES_PER_LINE = 128
ALL_ALIGNMENTS = 128
PROTEIN_GROUPS = 4
LARGEST_GROUP = 80
N_HEADS = 4


def draw_group_site_tally(key, part):
    key = jax.random.fold_in(key, 11)
    first_key, second_key = jax.random.split(key)
    drawn = jax.random.randint(first_key, (PROTEIN_GROUPS,), SITES_PER_LINE // 4, SITES_PER_LINE + 1)
    chosen = jax.random.randint(second_key, (), 0, PROTEIN_GROUPS)
    places = jnp.arange(PROTEIN_GROUPS, dtype=jnp.int32)
    return jnp.where(places == chosen, SITES_PER_LINE, drawn).astype(jnp.int32)


def draw_horizontal_triple_matrix(key, part):
    key = jax.random.fold_in(key, 23)
    first_key = jax.random.fold_in(key, 0)
    entries = jax.random.normal(first_key, (3, EMBED_FEATURES, EMBED_FEATURES), jnp.float32) * EMBED_FEATURES ** (-0.5)
    return jnp.clip(entries, -0.25, 0.25).astype(jnp.bfloat16)


def draw_vertical_triple_matrix(key, part):
    key = jax.random.fold_in(key, 37)
    first_key = jax.random.fold_in(key, 0)
    entries = jax.random.normal(first_key, (3, EMBED_FEATURES, EMBED_FEATURES), jnp.float32) * EMBED_FEATURES ** (-0.5)
    return jnp.clip(entries, -0.25, 0.25).astype(jnp.bfloat16)


def shard_levels(own_key, extent, shards, least, top_value):
    level = 1.0
    for position, blocks in shards:
        heights = jax.random.uniform(jax.random.fold_in(jax.random.fold_in(own_key, 6), position), (blocks,), jnp.float32, least / len(shards), top_value / len(shards))
        level = level * jnp.repeat(jnp.exp(heights), extent[position] // blocks).reshape((-1,) + (1,) * (len(extent) - 1 - position))
    return level


def length_profile(amount, total, limit, slope):
    weights = [(1 << 20) // math.isqrt(rank ** slope) + 1 for rank in range(2, amount + 1)]
    rest, holding = total - limit - (amount - 1), [1] * (amount - 1)
    while rest > 0:
        movable = [i for i in range(amount - 1) if holding[i] < limit]
        mass, remaining = sum([weights[i] for i in movable]), rest
        for i in movable:
            extra = min(limit - holding[i], max(1, remaining * weights[i] // mass), rest)
            holding[i] = holding[i] + extra
            rest = rest - extra
    return np.array([limit] + holding)


def ragged_sizes(stream_key, amount, total, bound, lean):
    if amount == 2:
        one = jax.random.randint(stream_key, (), max(1, total - bound), min(bound, total - 1) + 1)
        return jnp.stack([one, total - one])
    sizes = jnp.asarray(length_profile(amount, total, bound, lean), jnp.int32)
    couples = (amount - 1) // 2
    donor, taker = sizes[1:1 + 2 * couples:2], sizes[2:2 + 2 * couples:2]
    margin = jnp.minimum(donor - 1, bound - taker)
    shifted = jax.random.randint(jax.random.fold_in(stream_key, 1), (couples,), 0, 1 << 20) % (margin + 1)
    sizes = sizes.at[1:1 + 2 * couples:2].set(donor - shifted).at[2:2 + 2 * couples:2].set(taker + shifted)
    return sizes[jax.random.permutation(jax.random.fold_in(stream_key, 2), amount)]


def noise(stream_key, dims, scale, limit, pieces=(), kind=jnp.bfloat16):
    values = scale * jax.random.normal(stream_key, dims, jnp.float32)
    if pieces:
        values = values * shard_levels(stream_key, dims, pieces, -0.22, 0.18)
    return jnp.clip(values, -limit, limit).astype(kind)


def setup_inputs(seed: int = 0) -> dict:
    seeds = jax.random.split(jax.random.key(seed), 10)
    return {
        "alignment_embedding": noise(seeds[0], (ALL_ALIGNMENTS, EMBED_FEATURES, SITES_PER_LINE), 1.0, 6.0, ((0, 8), (1, 4))),
        "line_group_label": jnp.searchsorted(jnp.cumsum(ragged_sizes(seeds[1], PROTEIN_GROUPS, ALL_ALIGNMENTS, LARGEST_GROUP, 2)), jnp.arange(ALL_ALIGNMENTS), side="right").astype(jnp.int32),
        "group_site_tally": draw_group_site_tally(jax.random.fold_in(seeds[9], 71), 0),
        "horizontal_triple_matrix": draw_horizontal_triple_matrix(jax.random.fold_in(seeds[9], 71), 0),
        "horizontal_mixing_matrix": noise(seeds[4], (EMBED_FEATURES, EMBED_FEATURES), EMBED_FEATURES ** -0.5, 0.21875, ((0, 4),)),
        "vertical_triple_matrix": draw_vertical_triple_matrix(jax.random.fold_in(seeds[9], 71), 0),
        "vertical_mixing_matrix": noise(seeds[6], (EMBED_FEATURES, EMBED_FEATURES), EMBED_FEATURES ** -0.5, 0.21875, ((0, 4),)),
        "expand_matrix": noise(seeds[7], (EMBED_FEATURES, HIDDEN_UNITS), EMBED_FEATURES ** -0.5, 0.21875, ((1, 4),)),
        "contract_matrix": noise(seeds[8], (HIDDEN_UNITS, EMBED_FEATURES), HIDDEN_UNITS ** -0.5, 0.109375, ((0, 4),)),
    }


def layer_norm(carried_signal):
    values = carried_signal.astype(jnp.float32)
    average = lax.optimization_barrier(jnp.mean(values, axis=-1, keepdims=True))
    centred = values - average
    variance = lax.optimization_barrier(jnp.mean(centred * centred, axis=-1, keepdims=True))
    return (centred * lax.rsqrt(variance + 1e-05)).astype(jnp.bfloat16)

def project_back(carried_signal, mixed, weight):
    inner = weight.shape[0]
    block_size = inner // N_HEADS
    flat = mixed.reshape(-1, inner)
    totals = jnp.zeros((flat.shape[0], weight.shape[1]), jnp.float32)
    for block in range(N_HEADS):
        lower = block * block_size
        partial_sum = jnp.dot(flat[:, lower:lower + block_size], weight[lower:lower + block_size], preferred_element_type=jnp.float32)
        rounded = lax.optimization_barrier(partial_sum.astype(jnp.bfloat16))
        totals = totals + rounded.astype(jnp.float32)
    result = carried_signal.astype(jnp.float32) + totals.reshape(carried_signal.shape)
    return result.astype(jnp.bfloat16)

def project(standardized_vector, attention_probabilities):
    flat = standardized_vector.reshape(-1, standardized_vector.shape[-1])
    outputs = []
    for member in range(3):
        product = jnp.dot(flat, attention_probabilities[member].T, preferred_element_type=jnp.float32)
        outputs.append(product.astype(jnp.bfloat16).reshape(standardized_vector.shape))
    return outputs

def reference(alignment_embedding, line_group_label, group_site_tally, horizontal_triple_matrix, horizontal_mixing_matrix, vertical_triple_matrix, vertical_mixing_matrix, expand_matrix, contract_matrix):
    subspace_dimension = EMBED_FEATURES // ATTENTION_PARTS
    family_range = jnp.arange(PROTEIN_GROUPS, dtype=jnp.int32)
    onehot = (line_group_label[:, None] == family_range[None, :]).astype(jnp.float32)
    counts = lax.optimization_barrier(jnp.sum(onehot, axis=0))
    row_counts = lax.optimization_barrier(jnp.sum(onehot * counts[None, :], axis=1))
    scaling = subspace_dimension ** (-0.5) * lax.rsqrt(row_counts)
    live_keys = jnp.arange(SITES_PER_LINE, dtype=jnp.int32)[None, :] < group_site_tally[:, None]
    carried_signal = jnp.transpose(alignment_embedding, (0, 2, 1))
    standardized_vector = layer_norm(carried_signal)
    queries, key_rows, value_rows = project(standardized_vector, horizontal_triple_matrix)

    def row_head(head):
        lower = (head * subspace_dimension).astype(jnp.int32)
        query_head = lax.dynamic_slice_in_dim(queries, lower, subspace_dimension, 2).astype(jnp.float32)
        key_head = lax.dynamic_slice_in_dim(key_rows, lower, subspace_dimension, 2).astype(jnp.float32)
        value_head = lax.dynamic_slice_in_dim(value_rows, lower, subspace_dimension, 2).astype(jnp.float32)
        logits = jnp.einsum('rid,rjd->rij', query_head, key_head) * scaling[:, None, None]
        family_table = jax.ops.segment_sum(logits, line_group_label, num_segments=PROTEIN_GROUPS)
        family_table = jnp.where(live_keys[:, None, :], family_table, -jnp.inf)
        attention_probabilities = jax.nn.softmax(family_table, axis=-1).astype(jnp.bfloat16)
        row_weights = attention_probabilities[line_group_label].astype(jnp.float32)
        return jnp.einsum('rij,rjd->rid', row_weights, value_head).astype(jnp.bfloat16)
    merged_attention = lax.map(row_head, jnp.arange(ATTENTION_PARTS, dtype=jnp.int32))
    horizontal_mixed = jnp.transpose(merged_attention, (1, 2, 0, 3)).reshape(ALL_ALIGNMENTS, SITES_PER_LINE, EMBED_FEATURES)
    signal_past_horizontal = project_back(carried_signal, horizontal_mixed, horizontal_mixing_matrix)
    standardized_vector = layer_norm(signal_past_horizontal)
    vertical_asks, vertical_keyset, vertical_payload = project(standardized_vector, vertical_triple_matrix)
    same_family = line_group_label[:, None] == line_group_label[None, :]

    def column(site_offset):
        vertical_probe = lax.dynamic_index_in_dim(vertical_asks, site_offset, 1, keepdims=False).reshape(ALL_ALIGNMENTS, ATTENTION_PARTS, subspace_dimension).astype(jnp.float32)
        vertical_lookup = lax.dynamic_index_in_dim(vertical_keyset, site_offset, 1, keepdims=False).reshape(ALL_ALIGNMENTS, ATTENTION_PARTS, subspace_dimension).astype(jnp.float32)
        vertical_payload_slice = lax.dynamic_index_in_dim(vertical_payload, site_offset, 1, keepdims=False).reshape(ALL_ALIGNMENTS, ATTENTION_PARTS, subspace_dimension).astype(jnp.float32)
        scores = jnp.einsum('rhd,shd->hrs', vertical_probe, vertical_lookup) * subspace_dimension ** (-0.5)
        scores = jnp.where(same_family[None], scores, -jnp.inf)
        attention_probabilities = jax.nn.softmax(scores, axis=-1).astype(jnp.bfloat16).astype(jnp.float32)
        return jnp.einsum('ifn,niu->fiu', attention_probabilities, vertical_payload_slice).astype(jnp.bfloat16).reshape(ALL_ALIGNMENTS, EMBED_FEATURES)
    col_mixed = jnp.transpose(lax.map(column, jnp.arange(SITES_PER_LINE, dtype=jnp.int32)), (1, 0, 2))
    after_col = project_back(signal_past_horizontal, col_mixed, vertical_mixing_matrix)
    standardized_vector = layer_norm(after_col)
    expanded_activation = jax.nn.gelu(jnp.dot(standardized_vector.reshape(-1, EMBED_FEATURES), expand_matrix, preferred_element_type=jnp.float32), approximate=False)
    expanded_activation = expanded_activation.astype(jnp.bfloat16).reshape(ALL_ALIGNMENTS, SITES_PER_LINE, HIDDEN_UNITS)
    finished = project_back(after_col, expanded_activation, contract_matrix)
    return jnp.transpose(finished, (0, 2, 1))
```

```python
import jax
import jax.numpy as jnp
from jax import lax
from jax.sharding import Mesh, PartitionSpec as P

HEAD_SIZE = 64
SWAP = [(0, 1), (1, 0)]
BF16 = jnp.bfloat16
F32 = jnp.float32


def other_chip(value):
    return lax.ppermute(value, "chip", SWAP)


def other_core(value):
    return lax.ppermute(value, "core", SWAP)


def in_order(first, second, index, axis):
    forward = jnp.concatenate([first, second], axis=axis)
    backward = jnp.concatenate([second, first], axis=axis)
    return jnp.where(index == 0, forward, backward)


def half_rows(value, index):
    rows = value.shape[0] // 2
    return lax.dynamic_slice_in_dim(value, index * rows, rows)


def own_norm(values, axis):
    values = values.astype(F32)
    average = jnp.mean(values, axis=axis, keepdims=True)
    centred = values - average
    variance = jnp.mean(centred * centred, axis=axis, keepdims=True)
    return (centred * lax.rsqrt(variance + 1e-05)).astype(BF16)


def split_heads(value):
    return value.reshape(value.shape[0], -1, HEAD_SIZE, value.shape[-1])


def masked_softmax(tables, tally):
    live = jnp.arange(tables.shape[-1])[None, :] < tally[:, None]
    tables = jnp.where(live[:, None, None, :], tables, -jnp.inf)
    return jax.nn.softmax(tables, axis=-1).astype(BF16)


def tied_weights(tables, label, tally, first, row_groups):
    sites = tables.shape[-1]
    lines = label.shape[0] // row_groups
    ends = label.reshape(row_groups, lines)[:, jnp.array([0, lines - 1])]
    shared = tables[:2].reshape(2, -1, row_groups, sites // row_groups, sites)
    shared = jnp.transpose(shared, (2, 0, 1, 3, 4)).astype(BF16)
    parts = lax.all_to_all(shared, "rows", 0, 0, tiled=True).astype(F32)
    families = jnp.arange(tally.shape[0])
    member = (ends[:, :, None] == families).astype(F32)
    totals = jnp.einsum("stf,sthij->fhij", member, parts, precision=lax.Precision.HIGHEST)
    weights = masked_softmax(totals, tally)
    back = lax.all_to_all(weights[ends], "rows", 0, 0, tiled=True)
    back = jnp.transpose(back, (1, 2, 0, 3, 4)).reshape(2, -1, sites, sites)
    inner = jnp.clip(first + 1 + jnp.arange(tables.shape[0] - 2), 0, tally.shape[0] - 1)
    return jnp.concatenate([back, masked_softmax(tables[2:], tally[inner])])


def column_attention(queries, keys, values, label):
    same = label[:, None] == label[None, :]
    scores = jnp.einsum("pshd,pthd->phst", queries, keys, preferred_element_type=F32)
    scores = jnp.where(same, scores * HEAD_SIZE**-0.5, -jnp.inf)
    weights = jax.nn.softmax(scores, axis=-1).astype(BF16)
    mixed = jnp.einsum("phst,pthd->pshd", weights, values, preferred_element_type=F32)
    return mixed.astype(BF16)


def core_sum(stream, partial, rows):
    sent = other_core(partial[:, rows:].astype(BF16))
    return (stream.astype(F32) + partial[:, :rows] + sent.astype(F32)).astype(BF16)


def both_cores(stream):
    normed = own_norm(stream, -1)
    return jnp.concatenate([normed, other_core(normed)], axis=1)


def shards(
    alignment_embedding,
    line_group_label,
    group_site_tally,
    horizontal_triple_matrix,
    horizontal_mixing_matrix,
    vertical_triple_matrix,
    vertical_mixing_matrix,
    expand_matrix,
    contract_matrix,
):
    lines, quarter, sites = alignment_embedding.shape
    row_groups = lax.axis_size("rows")
    chips = 2 * row_groups
    place = sites // chips
    chip = lax.axis_index("chip")
    core = lax.axis_index("core")
    label = line_group_label
    tally = group_site_tally
    families = tally.shape[0]

    across = other_chip(alignment_embedding)
    near = in_order(alignment_embedding, other_core(alignment_embedding), core, 1)
    far = in_order(across, other_core(across), core, 1)
    stream = in_order(near, far, chip, 1)
    far_weights = lax.optimization_barrier(
        (
            across,
            horizontal_mixing_matrix,
            vertical_triple_matrix,
            vertical_mixing_matrix,
            expand_matrix,
            contract_matrix,
        )
    )[1:]
    far_mixing, far_triple, far_vertical, far_expand, far_contract = [
        other_chip(weight) for weight in far_weights
    ]
    vertical_triple = jnp.concatenate([vertical_triple_matrix, far_triple], axis=1)
    vertical_mixing = jnp.concatenate([vertical_mixing_matrix, far_vertical], axis=0)
    expand = jnp.concatenate([expand_matrix, far_expand], axis=1)
    contract = jnp.concatenate([contract_matrix, far_contract], axis=0)

    normed = own_norm(stream, 1)
    projected = jnp.einsum(
        "ked,rdi->krei", horizontal_triple_matrix, normed, preferred_element_type=F32
    ).astype(BF16)
    start = lax.axis_index("rows") * lines
    label_here = lax.dynamic_slice_in_dim(label, start, lines)
    first, last = label_here[0], label_here[-1]
    counts = jnp.sum((label[:, None] == jnp.arange(families)).astype(F32), axis=0)
    scaling = HEAD_SIZE**-0.5 * lax.rsqrt(counts)[label_here]
    slots = 2 + max(min(families, lines) - 2, 1)
    slot = jnp.where(
        label_here == first, 0, jnp.where(label_here == last, 1, label_here - first + 1)
    )
    queries, keys, values = [split_heads(member) for member in projected]
    logits = jnp.einsum("rhdi,rhdj->rhij", queries, keys, preferred_element_type=F32)
    logits = logits * scaling[:, None, None, None]
    member = (slot[:, None] == jnp.arange(slots)).astype(F32)
    tables = jnp.einsum("rs,rhij->shij", member, logits, precision=lax.Precision.HIGHEST)
    weights = tied_weights(tables, label, tally, first, row_groups)[slot]
    mixed = jnp.einsum("rhdj,rhij->rhdi", values, weights, preferred_element_type=F32)
    mixed = mixed.astype(BF16).reshape(lines, quarter, sites)

    kept = half_rows(mixed, chip)
    got = other_chip(half_rows(mixed, 1 - chip))
    partial = jnp.einsum("rdi,de->rie", kept, horizontal_mixing_matrix, preferred_element_type=F32)
    partial += jnp.einsum("rdi,de->rie", got, far_mixing, preferred_element_type=F32)
    sent = other_core(half_rows(partial, 1 - core).astype(BF16))
    residual = jnp.transpose(half_rows(half_rows(stream, chip), core), (0, 2, 1))
    after_row = residual.astype(F32) + half_rows(partial, core) + sent.astype(F32)
    after_row = after_row.astype(BF16)

    own = lines // 4
    model = after_row.shape[-1]
    after_row = jnp.transpose(after_row.reshape(own, chips, place, model), (1, 0, 2, 3))
    after_row = lax.all_to_all(after_row, ("rows", "chip"), 0, 0, tiled=True)
    after_row = jnp.transpose(after_row, (2, 0, 1, 3)).reshape(place, chips * own, model)
    rows = chips * own
    label_cores = label.reshape(chips, 2, own)
    label_sites = jnp.concatenate(
        [
            lax.dynamic_index_in_dim(label_cores, index, 1, False).reshape(-1)
            for index in (core, 1 - core)
        ]
    )

    normed = both_cores(after_row)
    projected = jnp.einsum("psd,ked->kpse", normed, vertical_triple, preferred_element_type=F32)
    projected = projected.astype(BF16).reshape(3, place, 2 * rows, -1, HEAD_SIZE)
    mixed = column_attention(projected[0], projected[1], projected[2], label_sites)
    mixed = mixed.reshape(place, 2 * rows, -1)
    partial = jnp.einsum("psd,de->pse", mixed, vertical_mixing, preferred_element_type=F32)
    after_col = core_sum(after_row, partial, rows)

    normed = both_cores(after_col)
    hidden = jnp.einsum("psd,df->psf", normed, expand, preferred_element_type=F32)
    hidden = jax.nn.gelu(hidden, approximate=False).astype(BF16)
    partial = jnp.einsum("psf,fd->psd", hidden, contract, preferred_element_type=F32)
    finished = core_sum(after_col, partial, rows)

    finished = finished.reshape(place, row_groups, 2 * own, model // quarter, quarter)
    finished = jnp.transpose(finished, (1, 3, 2, 0, 4)).reshape(-1, 2 * own, place, quarter)
    finished = lax.all_to_all(finished, ("rows", "chip", "core"), 0, 0, tiled=True)
    finished = finished.reshape(chips, 2, 2, own, place, quarter)
    finished = jnp.transpose(finished, (2, 1, 3, 5, 0, 4))
    return finished.reshape(lines, quarter, sites)


def solution(mesh):
    split = Mesh(mesh.devices.reshape(mesh.shape["rows"], 2, 2), ("rows", "chip", "core"))
    heads = ("chip", "core")
    placed = (
        P("rows", heads, None),
        P(),
        P(),
        P(None, heads, None),
        P(heads, None),
        P(None, heads, None),
        P(heads, None),
        P(None, heads),
        P(heads, None),
    )
    return jax.shard_map(
        shards, mesh=split, in_specs=placed, out_specs=P("rows", heads, None), check_vma=False
    )
```

```python
import jax
import jax.numpy as jnp
from jax import lax
from jax.sharding import Mesh, PartitionSpec as P

HEAD_SIZE = 64
SWAP = [(0, 1), (1, 0)]
ROWS = ("plane", "pair")
BF16 = jnp.bfloat16
F32 = jnp.float32


def other_chip(value):
    return lax.ppermute(value, "chip", SWAP)


def other_pair(value):
    return lax.ppermute(value, "pair", SWAP)


def other_core(value):
    return lax.ppermute(value, "core", SWAP)


def in_order(first, second, index, axis):
    forward = jnp.concatenate([first, second], axis=axis)
    backward = jnp.concatenate([second, first], axis=axis)
    return jnp.where(index == 0, forward, backward)


def half_rows(value, index):
    rows = value.shape[0] // 2
    return lax.dynamic_slice_in_dim(value, index * rows, rows)


def own_norm(values, axis):
    values = values.astype(F32)
    average = jnp.mean(values, axis=axis, keepdims=True)
    centred = values - average
    variance = jnp.mean(centred * centred, axis=axis, keepdims=True)
    return (centred * lax.rsqrt(variance + 1e-05)).astype(BF16)


def split_heads(value):
    return value.reshape(value.shape[0], -1, HEAD_SIZE, value.shape[-1])


def masked_softmax(tables, tally):
    live = jnp.arange(tables.shape[-1])[None, :] < tally[:, None]
    tables = jnp.where(live[:, None, None, :], tables, -jnp.inf)
    return jax.nn.softmax(tables, axis=-1).astype(BF16)


def tied_weights(tables, label, tally, first, row_groups):
    sites = tables.shape[-1]
    lines = label.shape[0] // row_groups
    ends = label.reshape(row_groups, lines)[:, jnp.array([0, lines - 1])]
    shared = tables[:2].reshape(2, -1, row_groups, sites // row_groups, sites)
    shared = jnp.transpose(shared, (2, 0, 1, 3, 4)).astype(BF16)
    parts = lax.all_to_all(shared, ROWS, 0, 0, tiled=True).astype(F32)
    families = jnp.arange(tally.shape[0])
    member = (ends[:, :, None] == families).astype(F32)
    totals = jnp.einsum("stf,sthij->fhij", member, parts, precision=lax.Precision.HIGHEST)
    weights = masked_softmax(totals, tally)
    back = lax.all_to_all(weights[ends], ROWS, 0, 0, tiled=True)
    back = jnp.transpose(back, (1, 2, 0, 3, 4)).reshape(2, -1, sites, sites)
    inner = jnp.clip(first + 1 + jnp.arange(tables.shape[0] - 2), 0, tally.shape[0] - 1)
    return jnp.concatenate([back, masked_softmax(tables[2:], tally[inner])])


def column_attention(queries, keys, values, label):
    same = label[:, None] == label[None, :]
    scores = jnp.einsum("pshd,pthd->phst", queries, keys, preferred_element_type=F32)
    scores = jnp.where(same, scores * HEAD_SIZE**-0.5, -jnp.inf)
    weights = jax.nn.softmax(scores, axis=-1).astype(BF16)
    mixed = jnp.einsum("phst,pthd->pshd", weights, values, preferred_element_type=F32)
    return mixed.astype(BF16)


def core_sum(stream, partial, rows):
    sent = other_core(partial[:, rows:].astype(BF16))
    return (stream.astype(F32) + partial[:, :rows] + sent.astype(F32)).astype(BF16)


def both_cores(stream):
    normed = own_norm(stream, -1)
    return jnp.concatenate([normed, other_core(normed)], axis=1)


def shards(
    alignment_embedding,
    line_group_label,
    group_site_tally,
    horizontal_triple_matrix,
    horizontal_mixing_matrix,
    vertical_triple_matrix,
    vertical_mixing_matrix,
    expand_matrix,
    contract_matrix,
):
    lines, quarter, sites = alignment_embedding.shape
    row_groups = lax.axis_size(ROWS)
    chips = 2 * row_groups
    place = sites // chips
    pair = lax.axis_index("pair")
    chip = lax.axis_index("chip")
    core = lax.axis_index("core")
    label = line_group_label
    tally = group_site_tally
    families = tally.shape[0]

    across = other_chip(alignment_embedding)
    near = in_order(alignment_embedding, other_core(alignment_embedding), core, 1)
    far = in_order(across, other_core(across), core, 1)
    stream = in_order(near, far, chip, 1)
    first_pack = jnp.concatenate(
        [
            horizontal_mixing_matrix,
            vertical_triple_matrix.reshape(-1, vertical_triple_matrix.shape[-1]),
            vertical_mixing_matrix,
        ]
    )
    second_pack = jnp.concatenate([expand_matrix, contract_matrix])
    across, first_pack, second_pack = lax.optimization_barrier((across, first_pack, second_pack))
    first_piece = other_chip(half_rows(first_pack, pair))
    second_piece = other_chip(half_rows(second_pack, pair))
    first_rest = other_pair(first_piece)
    second_rest = other_pair(second_piece)

    normed = own_norm(stream, 1)
    projected = jnp.einsum(
        "ked,rdi->krei", horizontal_triple_matrix, normed, preferred_element_type=F32
    ).astype(BF16)
    start = lax.axis_index(ROWS) * lines
    label_here = lax.dynamic_slice_in_dim(label, start, lines)
    first, last = label_here[0], label_here[-1]
    counts = jnp.sum((label[:, None] == jnp.arange(families)).astype(F32), axis=0)
    scaling = HEAD_SIZE**-0.5 * lax.rsqrt(counts)[label_here]
    slots = 2 + max(min(families, lines) - 2, 1)
    slot = jnp.where(
        label_here == first, 0, jnp.where(label_here == last, 1, label_here - first + 1)
    )
    queries, keys, values = [split_heads(member) for member in projected]
    logits = jnp.einsum("rhdi,rhdj->rhij", queries, keys, preferred_element_type=F32)
    logits = logits * scaling[:, None, None, None]
    member = (slot[:, None] == jnp.arange(slots)).astype(F32)
    tables = jnp.einsum("rs,rhij->shij", member, logits, precision=lax.Precision.HIGHEST)
    tables, first_piece = lax.optimization_barrier((tables, first_piece))
    weights = tied_weights(tables, label, tally, first, row_groups)[slot]
    mixed = jnp.einsum("rhdj,rhij->rhdi", values, weights, preferred_element_type=F32)
    mixed = mixed.astype(BF16).reshape(lines, quarter, sites)

    mixed, first_rest, second_piece = lax.optimization_barrier((mixed, first_rest, second_piece))
    first_far = in_order(first_rest, first_piece, 1 - pair, 0)
    far_mixing = first_far[:quarter]
    vertical_triple = jnp.concatenate(
        [vertical_triple_matrix, first_far[quarter : 4 * quarter].reshape(3, quarter, -1)], axis=1
    )
    vertical_mixing = jnp.concatenate([vertical_mixing_matrix, first_far[4 * quarter :]], axis=0)
    kept = half_rows(mixed, chip)
    got = other_chip(half_rows(mixed, 1 - chip))
    partial = jnp.einsum("rdi,de->rie", kept, horizontal_mixing_matrix, preferred_element_type=F32)
    partial += jnp.einsum("rdi,de->rie", got, far_mixing, preferred_element_type=F32)
    sent = other_core(half_rows(partial, 1 - core).astype(BF16))
    residual = jnp.transpose(half_rows(half_rows(stream, chip), core), (0, 2, 1))
    after_row = residual.astype(F32) + half_rows(partial, core) + sent.astype(F32)
    after_row = after_row.astype(BF16)

    after_row, second_rest = lax.optimization_barrier((after_row, second_rest))
    second_far = in_order(second_rest, second_piece, 1 - pair, 0)
    width = expand_matrix.shape[0]
    expand = jnp.concatenate([expand_matrix, second_far[:width]], axis=1)
    contract = jnp.concatenate([contract_matrix, second_far[width:]], axis=0)
    own = lines // 4
    model = after_row.shape[-1]
    after_row = jnp.transpose(after_row.reshape(own, chips, place, model), (1, 0, 2, 3))
    after_row = lax.all_to_all(after_row, ROWS + ("chip",), 0, 0, tiled=True)
    after_row = jnp.transpose(after_row, (2, 0, 1, 3)).reshape(place, chips * own, model)
    rows = chips * own
    label_cores = label.reshape(chips, 2, own)
    label_sites = jnp.concatenate(
        [
            lax.dynamic_index_in_dim(label_cores, index, 1, False).reshape(-1)
            for index in (core, 1 - core)
        ]
    )

    normed = both_cores(after_row)
    projected = jnp.einsum("psd,ked->kpse", normed, vertical_triple, preferred_element_type=F32)
    projected = projected.astype(BF16).reshape(3, place, 2 * rows, -1, HEAD_SIZE)
    mixed = column_attention(projected[0], projected[1], projected[2], label_sites)
    mixed = mixed.reshape(place, 2 * rows, -1)
    partial = jnp.einsum("psd,de->pse", mixed, vertical_mixing, preferred_element_type=F32)
    after_col = core_sum(after_row, partial, rows)

    normed = both_cores(after_col)
    hidden = jnp.einsum("psd,df->psf", normed, expand, preferred_element_type=F32)
    hidden = lax.optimization_barrier(jax.nn.gelu(hidden, approximate=False).astype(BF16))
    partial = jnp.einsum("psf,fd->psd", hidden, contract, preferred_element_type=F32)
    finished = core_sum(after_col, partial, rows)

    finished = finished.reshape(place, row_groups, 2 * own, model // quarter, quarter)
    finished = jnp.transpose(finished, (1, 3, 2, 0, 4)).reshape(-1, 2 * own, place, quarter)
    finished = lax.all_to_all(finished, ROWS + ("chip", "core"), 0, 0, tiled=True)
    finished = finished.reshape(chips, 2, 2, own, place, quarter)
    finished = jnp.transpose(finished, (2, 1, 3, 5, 0, 4))
    return finished.reshape(lines, quarter, sites)


def solution(mesh):
    planes = mesh.shape["rows"] // 2
    split = Mesh(mesh.devices.reshape(planes, 2, 2, 2), ROWS + ("chip", "core"))
    heads = ("chip", "core")
    placed = (
        P(ROWS, heads, None),
        P(),
        P(),
        P(None, heads, None),
        P(heads, None),
        P(None, heads, None),
        P(heads, None),
        P(None, heads),
        P(heads, None),
    )
    return jax.shard_map(
        shards, mesh=split, in_specs=placed, out_specs=P(ROWS, heads, None), check_vma=False
    )
```

```python
import functools

import jax
import jax.numpy as jnp
from jax import lax
from jax.experimental import pallas as pl
from jax.experimental.pallas import tpu as pltpu
from jax.sharding import Mesh, PartitionSpec as P

HEAD_SIZE = 64
SWAP = [(0, 1), (1, 0)]
ROWS = ("plane", "pair")
BF16 = jnp.bfloat16
F32 = jnp.float32


def other_chip(value):
    return lax.ppermute(value, "chip", SWAP)


def other_pair(value):
    return lax.ppermute(value, "pair", SWAP)


def other_core(value):
    return lax.ppermute(value, "core", SWAP)


def in_order(first, second, index, axis):
    forward = jnp.concatenate([first, second], axis=axis)
    backward = jnp.concatenate([second, first], axis=axis)
    return jnp.where(index == 0, forward, backward)


def half_rows(value, index):
    rows = value.shape[0] // 2
    return lax.dynamic_slice_in_dim(value, index * rows, rows)


def own_norm(values, axis):
    values = values.astype(F32)
    average = jnp.mean(values, axis=axis, keepdims=True)
    centred = values - average
    variance = jnp.mean(centred * centred, axis=axis, keepdims=True)
    return (centred * lax.rsqrt(variance + 1e-05)).astype(BF16)


def masked_softmax(tables, tally):
    live = jnp.arange(tables.shape[-1])[None, :] < tally[:, None]
    tables = jnp.where(live[:, None, None, :], tables, -jnp.inf)
    return jax.nn.softmax(tables, axis=-1).astype(BF16)


def tied_weights(shared, label, tally):
    row_groups, _, rows, sites = shared.shape
    lines = label.shape[0] // row_groups
    ends = label.reshape(row_groups, lines)[:, jnp.array([0, lines - 1])]
    parts = lax.all_to_all(shared, ROWS, 0, 0, tiled=True).astype(F32)
    parts = parts.reshape(row_groups, 2, -1, rows, sites)
    families = jnp.arange(tally.shape[0])
    member = (ends[:, :, None] == families).astype(F32)
    totals = jnp.einsum("stf,sthij->fhij", member, parts, precision=lax.Precision.HIGHEST)
    weights = masked_softmax(totals, tally)
    back = lax.all_to_all(weights[ends], ROWS, 0, 0, tiled=True)
    return jnp.transpose(back, (1, 2, 0, 3, 4)).reshape(2, -1, sites, sites)


CONTRACT_FIRST = (((0,), (0,)), ((), ()))
CONTRACT_LAST = (((1,), (1,)), ((), ()))
IN_VMEM = pl.BlockSpec(memory_space=pltpu.VMEM)
IN_SMEM = pl.BlockSpec(memory_space=pltpu.SMEM)
ANYWHERE = pl.BlockSpec(memory_space=pl.ANY)
GRANT = pltpu.CompilerParams(vmem_limit_bytes=40 * 2**20)


def row_front_kernel(
    count, spot_ref, slot_ref, scale_ref, tally_ref, own, near, far, diagonal, triple,
    table_ref, inner_ref, value_ref, tables, normed,
):
    step = pl.program_id(0)
    group, quarter, sites = own.shape
    heads = quarter // HEAD_SIZE

    @pl.when(step == 0)
    def _():
        tables[...] = jnp.zeros_like(tables)

    pieces = []
    for ref in (own, near, far, diagonal):
        lanes = jnp.concatenate([ref[line] for line in range(group)], axis=-1)
        pieces.append(lanes.astype(F32))
    size = 4 * quarter
    average = sum(jnp.sum(piece, axis=0, keepdims=True) for piece in pieces) / size
    pieces = [piece - average for piece in pieces]
    variance = sum(jnp.sum(piece * piece, axis=0, keepdims=True) for piece in pieces) / size
    inverse = lax.rsqrt(variance + 1e-05)
    for index, piece in enumerate(pieces):
        spot = pl.multiple_of(spot_ref[index] * quarter, quarter)
        normed[pl.ds(spot, quarter), :] = (piece * inverse).astype(BF16)
    projected = jnp.dot(triple[...], normed[...], preferred_element_type=F32).astype(BF16)
    for line in range(group):
        part = projected[:, line * sites : (line + 1) * sites]
        value_ref[line] = part[2 * quarter :]
        slot = slot_ref[step * group + line]
        scale = scale_ref[step * group + line]
        for head in range(heads):
            lower = head * HEAD_SIZE
            queries = part[lower : lower + HEAD_SIZE]
            keys = part[quarter + lower : quarter + lower + HEAD_SIZE]
            logits = lax.dot_general(queries, keys, CONTRACT_FIRST, preferred_element_type=F32)
            tables[slot * heads + head] += logits * scale

    @pl.when(step == count - 1)
    def _():
        for index in range(2 * heads):
            table = tables[index].astype(BF16)
            if len(table_ref.shape) == 4:
                groups, _, rows, _ = table_ref.shape
                table_ref[:, index] = table.reshape(groups, rows, sites)
            else:
                table_ref[index] = table
        site = lax.broadcasted_iota(jnp.int32, (sites, sites), 1)

        def inner(index, carry):
            table = tables[2 * heads + index]
            table = jnp.where(site < tally_ref[index // heads], table, -jnp.inf)
            table = jnp.exp(table - jnp.max(table, axis=-1, keepdims=True))
            table = table / jnp.sum(table, axis=-1, keepdims=True)
            inner_ref[index] = table.astype(BF16)
            return carry

        lax.fori_loop(0, inner_ref.shape[0], inner, 0)


def row_front(pieces, triple, spots, slot, scaling, inner_tally, row_groups):
    lines, quarter, sites = pieces[0].shape
    group = 4
    count = lines // group
    heads = quarter // HEAD_SIZE
    inner = inner_tally.shape[0]
    rows = sites // row_groups
    shape = (row_groups, 2 * heads, rows, sites) if rows % 16 == 0 else (2 * heads, sites, sites)
    block = pl.BlockSpec((group, quarter, sites), lambda step: (step, 0, 0))

    def whole(shape):
        return pl.BlockSpec(shape, lambda step: (0,) * len(shape))

    tables, inner_weights, values = pl.pallas_call(
        functools.partial(row_front_kernel, count),
        grid=(count,),
        out_shape=(
            jax.ShapeDtypeStruct(shape, BF16),
            jax.ShapeDtypeStruct((inner * heads, sites, sites), BF16),
            jax.ShapeDtypeStruct((lines, quarter, sites), BF16),
        ),
        in_specs=[IN_SMEM] * 4 + [block] * 4 + [whole((3 * quarter, 4 * quarter))],
        out_specs=(whole(shape), whole((inner * heads, sites, sites)), block),
        scratch_shapes=[
            pltpu.VMEM(((2 + inner) * heads, sites, sites), F32),
            pltpu.VMEM((4 * quarter, group * sites), BF16),
        ],
        compiler_params=GRANT,
        name="row_front",
    )(spots, slot, scaling, inner_tally, *pieces, triple.reshape(3 * quarter, 4 * quarter))
    if rows % 16:
        tables = jnp.transpose(tables.reshape(-1, row_groups, rows, sites), (1, 0, 2, 3))
    return tables, inner_weights.reshape(inner, heads, sites, sites), values


def column_kernel(
    pair_ref, label_row, label_column, own, other, triple, mixing, piece, rest,
    kept, sent, normed, far, projected, mixed, semaphores,
):
    half = piece.shape[0]
    pair = pair_ref[0]
    copies = []
    for index, (source, place) in enumerate(((piece, pair), (rest, 1 - pair))):
        spot = pl.multiple_of(place * half, half)
        target = far.at[pl.ds(spot, half)]
        copies.append(pltpu.make_async_copy(source, target, semaphores.at[index]))
    for copy in copies:
        copy.start()
    places, rows, model = own.shape
    quarter = mixing.shape[0]
    both = 2 * rows
    normed[:, :rows] = own[...]
    normed[:, rows:] = other[...]
    flat = normed[...].reshape(places * both, model)
    same = label_column[...] == label_row[...]
    scale = HEAD_SIZE**-0.5

    def attend(weights, lower):
        projected[...] = lax.dot_general(
            weights, flat, CONTRACT_LAST, preferred_element_type=F32
        ).astype(BF16)
        for place in range(places):
            lanes = slice(place * both, (place + 1) * both)
            for head in range(quarter // HEAD_SIZE):
                features = slice(head * HEAD_SIZE, (head + 1) * HEAD_SIZE)
                queries = projected[:quarter, lanes][features]
                keys = projected[quarter : 2 * quarter, lanes][features]
                values = projected[2 * quarter :, lanes][features]
                scores = lax.dot_general(
                    keys, queries, CONTRACT_FIRST, preferred_element_type=F32
                )
                scores = jnp.where(same, scores * scale, -jnp.inf)
                scores = jnp.exp(scores - jnp.max(scores, axis=0, keepdims=True))
                total = jnp.sum(scores, axis=0, keepdims=True)
                part = jnp.dot(values, scores.astype(BF16), preferred_element_type=F32)
                target = slice(lower + head * HEAD_SIZE, lower + (head + 1) * HEAD_SIZE)
                mixed[target, lanes] = (part / total).astype(BF16)

    attend(triple[...], 0)
    for copy in copies:
        copy.wait()
    attend(far[quarter : 4 * quarter], quarter)
    for place in range(places):
        lanes = slice(place * both, (place + 1) * both)
        partial = lax.dot_general(
            mixed[:quarter, lanes], mixing[...], CONTRACT_FIRST, preferred_element_type=F32
        )
        partial += lax.dot_general(
            mixed[quarter:, lanes], far[4 * quarter :], CONTRACT_FIRST, preferred_element_type=F32
        )
        kept[place] = partial[:rows]
        sent[place] = partial[rows:].astype(BF16)


def column(own, other, label, triple, mixing, piece, rest, pair):
    places, rows, model = own.shape
    quarter = mixing.shape[0]
    tokens = 2 * places * rows
    return pl.pallas_call(
        column_kernel,
        out_shape=(
            jax.ShapeDtypeStruct(own.shape, F32),
            jax.ShapeDtypeStruct(own.shape, BF16),
        ),
        in_specs=[IN_SMEM] + [IN_VMEM] * 6 + [ANYWHERE] * 2,
        out_specs=(IN_VMEM, IN_VMEM),
        scratch_shapes=[
            pltpu.VMEM((places, 2 * rows, model), BF16),
            pltpu.VMEM((2 * piece.shape[0], model), BF16),
            pltpu.VMEM((3 * quarter, tokens), BF16),
            pltpu.VMEM((2 * quarter, tokens), BF16),
            pltpu.SemaphoreType.DMA((2,)),
        ],
        compiler_params=GRANT,
        name="column",
    )(pair, label[None, :], label[:, None], own, other, triple.reshape(-1, model), mixing, piece, rest)


def feed_forward_kernel(
    pair_ref, normed, expand, contract, piece, rest, out,
    near_expand, near_contract, far_piece, far_rest, hidden, semaphores,
):
    moves = (
        (expand, near_expand), (piece, far_piece), (rest, far_rest), (contract, near_contract)
    )
    copies = [
        pltpu.make_async_copy(source, target, semaphores.at[index])
        for index, (source, target) in enumerate(moves)
    ]
    for copy in copies:
        copy.start()
    width = near_expand.shape[1]
    tile = width // 3
    values = normed[...]
    pair = pair_ref[0]

    def raise_by(weights, lower):
        for start in range(0, width, tile):
            up = jnp.dot(values, weights[:, start : start + tile], preferred_element_type=F32)
            up = 0.5 * up * (1.0 + lax.erf(up * 2.0**-0.5))
            hidden[:, lower + start : lower + start + tile] = up.astype(BF16)

    def lower_by(near_weights, far_weights):
        down = jnp.dot(hidden[:, :width], near_weights[...], preferred_element_type=F32)
        down += jnp.dot(hidden[:, width:], far_weights[...], preferred_element_type=F32)
        out[...] = down.astype(out.dtype)

    copies[0].wait()
    raise_by(near_expand, 0)
    copies[1].wait()
    copies[2].wait()

    @pl.when(pair == 0)
    def _():
        raise_by(far_piece, width)

    @pl.when(pair != 0)
    def _():
        raise_by(far_rest, width)

    copies[3].wait()

    @pl.when(pair == 0)
    def _():
        lower_by(near_contract, far_rest)

    @pl.when(pair != 0)
    def _():
        lower_by(near_contract, far_piece)


def feed_forward(normed, expand, contract, piece, rest, pair, kind):
    places, rows, model = normed.shape
    tokens, width = places * rows, expand.shape[1]
    result = pl.pallas_call(
        feed_forward_kernel,
        out_shape=jax.ShapeDtypeStruct((tokens, model), kind),
        in_specs=[IN_SMEM, IN_VMEM] + [ANYWHERE] * 4,
        out_specs=IN_VMEM,
        scratch_shapes=[
            pltpu.VMEM((model, width), BF16),
            pltpu.VMEM((width, model), BF16),
            pltpu.VMEM((model, width), BF16),
            pltpu.VMEM((model, width), BF16),
            pltpu.VMEM((tokens, 2 * width), BF16),
            pltpu.SemaphoreType.DMA((4,)),
        ],
        compiler_params=GRANT,
        name="feed_forward",
    )(pair, normed.reshape(tokens, model), expand, contract, piece, rest)
    return result.reshape(normed.shape)


def core_sum(stream, kept, sent):
    return (stream.astype(F32) + kept + other_core(sent).astype(F32)).astype(BF16)


def shards(
    alignment_embedding,
    line_group_label,
    group_site_tally,
    horizontal_triple_matrix,
    horizontal_mixing_matrix,
    vertical_triple_matrix,
    vertical_mixing_matrix,
    expand_matrix,
    contract_matrix,
):
    lines, quarter, sites = alignment_embedding.shape
    row_groups = lax.axis_size(ROWS)
    chips = 2 * row_groups
    place = sites // chips
    pair = lax.axis_index("pair")
    chip = lax.axis_index("chip")
    core = lax.axis_index("core")
    label = line_group_label
    tally = group_site_tally
    families = tally.shape[0]

    across = other_chip(alignment_embedding)
    near = other_core(alignment_embedding)
    diagonal = other_core(across)
    pieces = (alignment_embedding, near, across, diagonal)
    spots = jnp.stack(
        [2 * chip + core, 2 * chip + 1 - core, 2 * (1 - chip) + core, 2 * (1 - chip) + 1 - core]
    ).astype(jnp.int32)
    first_pack = jnp.concatenate(
        [
            horizontal_mixing_matrix,
            vertical_triple_matrix.reshape(-1, vertical_triple_matrix.shape[-1]),
            vertical_mixing_matrix,
        ]
    )
    second_pack = jnp.concatenate([expand_matrix, contract_matrix])
    across, first_pack, second_pack = lax.optimization_barrier((across, first_pack, second_pack))
    first_piece = other_chip(half_rows(first_pack, pair))
    second_piece = other_chip(half_rows(second_pack, pair))
    first_rest = other_pair(first_piece)
    second_rest = other_pair(second_piece)

    start = lax.axis_index(ROWS) * lines
    label_here = lax.dynamic_slice_in_dim(label, start, lines)
    first, last = label_here[0], label_here[-1]
    counts = jnp.sum((label[:, None] == jnp.arange(families)).astype(F32), axis=0)
    scaling = HEAD_SIZE**-0.5 * lax.rsqrt(counts)[label_here]
    slots = 2 + max(min(families, lines) - 2, 1)
    slot = jnp.where(
        label_here == first, 0, jnp.where(label_here == last, 1, label_here - first + 1)
    )
    inner = jnp.clip(first + 1 + jnp.arange(slots - 2), 0, families - 1)
    tables, inner_weights, values = row_front(
        pieces, horizontal_triple_matrix, spots, slot, scaling, tally[inner], row_groups
    )
    tables, first_piece = lax.optimization_barrier((tables, first_piece))
    weights = jnp.concatenate([tied_weights(tables, label, tally), inner_weights])[slot]
    values = values.reshape(lines, -1, HEAD_SIZE, sites)
    mixed = jnp.einsum("rhdj,rhij->rhdi", values, weights, preferred_element_type=F32)
    mixed = mixed.astype(BF16).reshape(lines, quarter, sites)

    mixed, first_rest, second_piece = lax.optimization_barrier((mixed, first_rest, second_piece))
    far_mixing = jnp.where(pair == 0, first_piece[:quarter], first_rest[:quarter])
    kept = half_rows(mixed, chip)
    got = other_chip(half_rows(mixed, 1 - chip))
    partial = jnp.einsum("rdi,de->rie", kept, horizontal_mixing_matrix, preferred_element_type=F32)
    partial += jnp.einsum("rdi,de->rie", got, far_mixing, preferred_element_type=F32)
    sent = other_core(half_rows(partial, 1 - core).astype(BF16))
    ours = [half_rows(half_rows(piece, chip), core) for piece in pieces]
    stream = in_order(
        in_order(ours[0], ours[1], core, 1), in_order(ours[2], ours[3], core, 1), chip, 1
    )
    residual = jnp.transpose(stream, (0, 2, 1))
    after_row = residual.astype(F32) + half_rows(partial, core) + sent.astype(F32)
    after_row = after_row.astype(BF16)

    after_row, second_rest = lax.optimization_barrier((after_row, second_rest))
    own = lines // 4
    model = after_row.shape[-1]
    after_row = jnp.transpose(after_row.reshape(own, chips, place, model), (1, 0, 2, 3))
    after_row = lax.all_to_all(after_row, ROWS + ("chip",), 0, 0, tiled=True)
    after_row = jnp.transpose(after_row, (2, 0, 1, 3)).reshape(place, chips * own, model)
    rows = chips * own
    label_cores = label.reshape(chips, 2, own)
    label_sites = jnp.concatenate(
        [
            lax.dynamic_index_in_dim(label_cores, index, 1, False).reshape(-1)
            for index in (core, 1 - core)
        ]
    )

    parity = pair.astype(jnp.int32).reshape(1)
    normed = own_norm(after_row, -1)
    kept, sent = column(
        normed,
        other_core(normed),
        label_sites,
        vertical_triple_matrix,
        vertical_mixing_matrix,
        first_piece,
        first_rest,
        parity,
    )
    after_col = core_sum(after_row, kept, sent)

    normed = own_norm(after_col, -1)
    feed = (expand_matrix, contract_matrix, second_piece, second_rest, parity)
    kept = feed_forward(normed, *feed, F32)
    sent = feed_forward(other_core(normed), *feed, BF16)
    finished = core_sum(after_col, kept, sent)

    finished = finished.reshape(place, row_groups, 2 * own, model // quarter, quarter)
    finished = jnp.transpose(finished, (1, 3, 2, 0, 4)).reshape(-1, 2 * own * place, quarter)
    parts, wide = 2 * own * place // 2, quarter // 3 * 2
    finished = jnp.concatenate(
        [
            finished[:, :, :wide],
            jnp.concatenate([finished[:, :parts, wide:], finished[:, parts:, wide:]], axis=2),
        ],
        axis=1,
    )
    finished = lax.all_to_all(finished, ROWS + ("chip", "core"), 0, 0, tiled=True)
    narrow = finished[:, 2 * parts :]
    narrow = jnp.concatenate([narrow[:, :, : wide // 2], narrow[:, :, wide // 2 :]], axis=1)
    finished = jnp.concatenate([finished[:, : 2 * parts], narrow], axis=2)
    finished = finished.reshape(chips, 2, 2, own, place, quarter)
    finished = jnp.transpose(finished, (2, 1, 3, 5, 0, 4))
    return finished.reshape(lines, quarter, sites)


def solution(mesh):
    planes = mesh.shape["rows"] // 2
    split = Mesh(mesh.devices.reshape(planes, 2, 2, 2), ROWS + ("chip", "core"))
    heads = ("chip", "core")
    placed = (
        P(ROWS, heads, None),
        P(),
        P(),
        P(None, heads, None),
        P(heads, None),
        P(None, heads, None),
        P(heads, None),
        P(None, heads),
        P(heads, None),
    )
    return jax.shard_map(
        shards, mesh=split, in_specs=placed, out_specs=P(ROWS, heads, None), check_vma=False
    )
```

```python
import functools

import jax
import jax.numpy as jnp
from jax import lax
from jax.experimental import pallas as pl
from jax.experimental.pallas import tpu as pltpu
from jax.sharding import Mesh, PartitionSpec as P

HEAD_SIZE = 64
SWAP = [(0, 1), (1, 0)]
ROWS = ("plane", "pair")
BF16 = jnp.bfloat16
F32 = jnp.float32


def other_chip(value):
    return lax.ppermute(value, "chip", SWAP)


def other_pair(value):
    return lax.ppermute(value, "pair", SWAP)


def other_core(value):
    return lax.ppermute(value, "core", SWAP)


def in_order(first, second, index, axis):
    forward = jnp.concatenate([first, second], axis=axis)
    backward = jnp.concatenate([second, first], axis=axis)
    return jnp.where(index == 0, forward, backward)


def half_rows(value, index):
    rows = value.shape[0] // 2
    return lax.dynamic_slice_in_dim(value, index * rows, rows)


def own_norm(values, axis):
    values = values.astype(F32)
    average = jnp.mean(values, axis=axis, keepdims=True)
    centred = values - average
    variance = jnp.mean(centred * centred, axis=axis, keepdims=True)
    return (centred * lax.rsqrt(variance + 1e-05)).astype(BF16)


def masked_softmax(tables, tally):
    live = jnp.arange(tables.shape[-1])[None, :] < tally[:, None]
    tables = jnp.where(live[:, None, None, :], tables, -jnp.inf)
    return jax.nn.softmax(tables, axis=-1).astype(BF16)


CONTRACT_FIRST = (((0,), (0,)), ((), ()))
CONTRACT_LAST = (((1,), (1,)), ((), ()))
IN_VMEM = pl.BlockSpec(memory_space=pltpu.VMEM)
IN_SMEM = pl.BlockSpec(memory_space=pltpu.SMEM)
ANYWHERE = pl.BlockSpec(memory_space=pl.ANY)
GRANT = pltpu.CompilerParams(vmem_limit_bytes=40 * 2**20)


def row_front_kernel(
    count, spot_ref, slot_ref, scale_ref, tally_ref, own, near, far, diagonal, triple,
    table_ref, inner_ref, value_ref, tables, normed,
):
    step = pl.program_id(0)
    group, quarter, sites = own.shape
    heads = quarter // HEAD_SIZE

    @pl.when(step == 0)
    def _():
        tables[...] = jnp.zeros_like(tables)

    pieces = []
    for ref in (own, near, far, diagonal):
        lanes = jnp.concatenate([ref[line] for line in range(group)], axis=-1)
        pieces.append(lanes.astype(F32))
    size = 4 * quarter
    average = sum(jnp.sum(piece, axis=0, keepdims=True) for piece in pieces) / size
    pieces = [piece - average for piece in pieces]
    variance = sum(jnp.sum(piece * piece, axis=0, keepdims=True) for piece in pieces) / size
    inverse = lax.rsqrt(variance + 1e-05)
    for index, piece in enumerate(pieces):
        spot = pl.multiple_of(spot_ref[index] * quarter, quarter)
        normed[pl.ds(spot, quarter), :] = (piece * inverse).astype(BF16)
    projected = jnp.dot(triple[...], normed[...], preferred_element_type=F32).astype(BF16)
    for line in range(group):
        part = projected[:, line * sites : (line + 1) * sites]
        value_ref[line] = part[2 * quarter :]
        slot = slot_ref[step * group + line]
        scale = scale_ref[step * group + line]
        for head in range(heads):
            lower = head * HEAD_SIZE
            queries = part[lower : lower + HEAD_SIZE]
            keys = part[quarter + lower : quarter + lower + HEAD_SIZE]
            logits = lax.dot_general(queries, keys, CONTRACT_FIRST, preferred_element_type=F32)
            tables[slot * heads + head] += logits * scale

    @pl.when(step == count - 1)
    def _():
        for index in range(2 * heads):
            table = tables[index].astype(BF16)
            if len(table_ref.shape) == 4:
                groups, _, rows, _ = table_ref.shape
                table_ref[:, index] = table.reshape(groups, rows, sites)
            else:
                table_ref[index] = table
        site = lax.broadcasted_iota(jnp.int32, (sites, sites), 1)

        def inner(index, carry):
            table = tables[2 * heads + index]
            table = jnp.where(site < tally_ref[index // heads], table, -jnp.inf)
            table = jnp.exp(table - jnp.max(table, axis=-1, keepdims=True))
            table = table / jnp.sum(table, axis=-1, keepdims=True)
            inner_ref[index] = table.astype(BF16)
            return carry

        lax.fori_loop(0, inner_ref.shape[0], inner, 0)


def row_front(pieces, triple, spots, slot, scaling, inner_tally, row_groups):
    lines, quarter, sites = pieces[0].shape
    group = 4
    count = lines // group
    heads = quarter // HEAD_SIZE
    inner = inner_tally.shape[0]
    rows = sites // row_groups
    shape = (row_groups, 2 * heads, rows, sites) if rows % 16 == 0 else (2 * heads, sites, sites)
    block = pl.BlockSpec((group, quarter, sites), lambda step: (step, 0, 0))

    def whole(shape):
        return pl.BlockSpec(shape, lambda step: (0,) * len(shape))

    tables, inner_weights, values = pl.pallas_call(
        functools.partial(row_front_kernel, count),
        grid=(count,),
        out_shape=(
            jax.ShapeDtypeStruct(shape, BF16),
            jax.ShapeDtypeStruct((inner * heads, sites, sites), BF16),
            jax.ShapeDtypeStruct((lines, quarter, sites), BF16),
        ),
        in_specs=[IN_SMEM] * 4 + [block] * 4 + [whole((3 * quarter, 4 * quarter))],
        out_specs=(whole(shape), whole((inner * heads, sites, sites)), block),
        scratch_shapes=[
            pltpu.VMEM(((2 + inner) * heads, sites, sites), F32),
            pltpu.VMEM((4 * quarter, group * sites), BF16),
        ],
        compiler_params=GRANT,
        name="row_front",
    )(spots, slot, scaling, inner_tally, *pieces, triple.reshape(3 * quarter, 4 * quarter))
    if rows % 16:
        tables = jnp.transpose(tables.reshape(-1, row_groups, rows, sites), (1, 0, 2, 3))
    return tables, inner_weights, values


def tie_kernel(end_ref, tally_ref, parts, out, weights):
    groups, pairs, rows, sites = parts.shape
    heads = pairs // 2
    site = lax.broadcasted_iota(jnp.int32, (heads, rows, sites), 2)
    for family in range(weights.shape[0]):
        total = jnp.zeros((heads, rows, sites), F32)
        for group in range(groups):
            for end in range(2):
                part = parts[group, end * heads : (end + 1) * heads].astype(F32)
                total += jnp.where(end_ref[2 * group + end] == family, part, 0.0)
        total = jnp.where(site < tally_ref[family], total, -jnp.inf)
        total = jnp.exp(total - jnp.max(total, axis=-1, keepdims=True))
        total = total / jnp.sum(total, axis=-1, keepdims=True)
        weights[family] = total.astype(BF16)
    for group in range(groups):
        for end in range(2):
            chosen = weights[end_ref[2 * group + end]]
            out[group, end * heads : (end + 1) * heads] = chosen


def tie(parts, ends, tally):
    groups, pairs, rows, sites = parts.shape
    if rows % 16 == 0:
        return pl.pallas_call(
            tie_kernel,
            out_shape=jax.ShapeDtypeStruct(parts.shape, BF16),
            in_specs=[IN_SMEM, IN_SMEM, IN_VMEM],
            out_specs=IN_VMEM,
            scratch_shapes=[pltpu.VMEM((tally.shape[0], pairs // 2, rows, sites), BF16)],
            compiler_params=GRANT,
            name="tie",
        )(ends, tally, parts)
    ends = ends.reshape(groups, 2)
    parts = parts.astype(F32).reshape(groups, 2, -1, rows, sites)
    member = (ends[:, :, None] == jnp.arange(tally.shape[0])).astype(F32)
    totals = jnp.einsum("stf,sthij->fhij", member, parts, precision=lax.Precision.HIGHEST)
    return masked_softmax(totals, tally)[ends].reshape(groups, pairs, rows, sites)


def mix_kernel(spot_ref, slot_ref, shared, inner, values, kept, sent):
    pairs, sites = shared.shape[1], values.shape[2]
    heads = pairs // 2
    half = kept.shape[0]

    def run(weights):
        weights[: 2 * heads] = jnp.stack(
            [shared[:, index].reshape(sites, sites) for index in range(2 * heads)]
        )
        weights[2 * heads :] = inner[...]
        for target, chip in ((sent, 1 - spot_ref[0]), (kept, spot_ref[0])):
            for line in range(half):
                row = chip * half + line
                slot = slot_ref[row]
                value = values[row]
                for head in range(heads):
                    features = slice(head * HEAD_SIZE, (head + 1) * HEAD_SIZE)
                    target[line, features] = lax.dot_general(
                        value[features],
                        weights[slot * heads + head],
                        CONTRACT_LAST,
                        preferred_element_type=F32,
                    ).astype(BF16)

    pl.run_scoped(run, pltpu.VMEM((2 * heads + inner.shape[0], sites, sites), BF16))


def mix(shared, inner, values, slot, chip):
    groups, pairs, rows, sites = shared.shape
    lines, quarter, _ = values.shape
    if rows % 16 == 0:
        half = jax.ShapeDtypeStruct((lines // 2, quarter, sites), BF16)
        return pl.pallas_call(
            mix_kernel,
            out_shape=(half, half),
            in_specs=[IN_SMEM, IN_SMEM] + [IN_VMEM] * 3,
            out_specs=(IN_VMEM, IN_VMEM),
            compiler_params=GRANT,
            name="mix",
        )(chip.astype(jnp.int32).reshape(1), slot, shared, inner, values)
    ends = jnp.transpose(shared, (1, 0, 2, 3)).reshape(2, pairs // 2, sites, sites)
    weights = jnp.concatenate([ends, inner.reshape(-1, *ends.shape[1:])])[slot]
    values = values.reshape(lines, -1, HEAD_SIZE, sites)
    mixed = jnp.einsum("rhdj,rhij->rhdi", values, weights, preferred_element_type=F32)
    mixed = mixed.astype(BF16).reshape(lines, quarter, sites)
    return half_rows(mixed, chip), half_rows(mixed, 1 - chip)


def project_kernel(
    spot_ref, line_ref, mixed, got, mixing, piece, rest, own, near, across, diagonal,
    kept, sent, stream, far, semaphores,
):
    lines, _, sites = stream.shape
    quarter = mixing.shape[0]
    copies = []
    for index, source in enumerate((own, near, across, diagonal)):
        spot = pl.multiple_of(spot_ref[index] * quarter, quarter)
        copies.append(
            pltpu.make_async_copy(
                source.at[pl.ds(line_ref[0], lines)],
                stream.at[:, pl.ds(spot, quarter)],
                semaphores.at[index],
            )
        )
    for copy in copies:
        copy.start()
    pair, core = line_ref[1], line_ref[2]

    @pl.when(pair == 0)
    def _():
        far[...] = piece[:quarter]

    @pl.when(pair != 0)
    def _():
        far[...] = rest[:quarter]

    def partial(row):
        near_part = lax.dot_general(
            mixed[row], mixing[...], CONTRACT_FIRST, preferred_element_type=F32
        )
        return near_part + lax.dot_general(
            got[row], far[...], CONTRACT_FIRST, preferred_element_type=F32
        )

    for line in range(lines):
        sent[line] = partial((1 - core) * lines + line).astype(BF16)
    for copy in copies:
        copy.wait()
    for line in range(lines):
        kept[line] = partial(core * lines + line) + stream[line].astype(F32).T


def project(mixed, got, mixing, piece, rest, pieces, spots, place):
    half, quarter, sites = mixed.shape
    lines, model = half // 2, mixing.shape[1]
    out = (lines, sites, model)
    return pl.pallas_call(
        project_kernel,
        out_shape=(jax.ShapeDtypeStruct(out, F32), jax.ShapeDtypeStruct(out, BF16)),
        in_specs=[IN_SMEM, IN_SMEM] + [IN_VMEM] * 5 + [ANYWHERE] * 4,
        out_specs=(IN_VMEM, IN_VMEM),
        scratch_shapes=[
            pltpu.VMEM((lines, model, sites), BF16),
            pltpu.VMEM((quarter, model), BF16),
            pltpu.SemaphoreType.DMA((4,)),
        ],
        compiler_params=GRANT,
        name="project",
    )(spots, place, mixed, got, mixing, piece, rest, *pieces)


def settle_kernel(kept, got, out):
    lines, sites, model = kept.shape
    chips = out.shape[0]
    parts = []
    for line in range(lines):
        total = kept[line] + got[line].astype(F32)
        parts.append(total.reshape(chips, sites // chips, model))
    out[...] = jnp.concatenate(parts, axis=1).astype(BF16)


def settle(kept, got, chips):
    lines, sites, model = kept.shape
    place = sites // chips
    if place % 8 == 0:
        return pl.pallas_call(
            settle_kernel,
            out_shape=jax.ShapeDtypeStruct((chips, lines * place, model), BF16),
            in_specs=[IN_VMEM, IN_VMEM],
            out_specs=IN_VMEM,
            compiler_params=GRANT,
            name="settle",
        )(kept, got)
    total = (kept + got.astype(F32)).astype(BF16).reshape(lines, chips, place, model)
    return jnp.transpose(total, (1, 0, 2, 3)).reshape(chips, lines * place, model)


def arrive_kernel(blocks, normed, stream, tokens):
    chips, count, model = blocks.shape
    places, rows, _ = normed.shape
    lanes = tokens.shape[-1]
    flat = blocks[...].reshape(chips * count, model).astype(F32)
    for index in range(tokens.shape[0]):
        tokens[index] = flat[:, index * lanes : (index + 1) * lanes]
    for place in range(places):
        values = [
            tokens[index, pl.ds(place, rows, stride=places), :] for index in range(tokens.shape[0])
        ]
        values = jnp.concatenate(values, axis=-1)
        stream[place] = values.astype(BF16)
        centred = values - jnp.mean(values, axis=-1, keepdims=True)
        variance = jnp.mean(centred * centred, axis=-1, keepdims=True)
        normed[place] = (centred * lax.rsqrt(variance + 1e-05)).astype(BF16)


def arrive(blocks, place):
    chips, count, model = blocks.shape
    rows = chips * count // place
    if place % 8 == 0:
        shape = jax.ShapeDtypeStruct((place, rows, model), BF16)
        return pl.pallas_call(
            arrive_kernel,
            out_shape=(shape, shape),
            in_specs=[IN_VMEM],
            out_specs=(IN_VMEM, IN_VMEM),
            scratch_shapes=[pltpu.VMEM((model // 128, chips * count, 128), F32)],
            compiler_params=GRANT,
            name="arrive",
        )(blocks)
    stream = jnp.transpose(blocks.reshape(rows, place, model), (1, 0, 2))
    return own_norm(stream, -1), stream


def column_kernel(
    pair_ref, label_row, label_column, own, other, triple, mixing, piece, rest,
    kept, sent, normed, far, projected, mixed, semaphores,
):
    half = piece.shape[0]
    pair = pair_ref[0]
    copies = []
    for index, (source, place) in enumerate(((piece, pair), (rest, 1 - pair))):
        spot = pl.multiple_of(place * half, half)
        target = far.at[pl.ds(spot, half)]
        copies.append(pltpu.make_async_copy(source, target, semaphores.at[index]))
    for copy in copies:
        copy.start()
    places, rows, model = own.shape
    quarter = mixing.shape[0]
    both = 2 * rows
    normed[:, :rows] = own[...]
    normed[:, rows:] = other[...]
    flat = normed[...].reshape(places * both, model)
    same = label_column[...] == label_row[...]
    scale = HEAD_SIZE**-0.5

    def attend(weights, lower):
        projected[...] = lax.dot_general(
            weights, flat, CONTRACT_LAST, preferred_element_type=F32
        ).astype(BF16)
        for place in range(places):
            lanes = slice(place * both, (place + 1) * both)
            for head in range(quarter // HEAD_SIZE):
                features = slice(head * HEAD_SIZE, (head + 1) * HEAD_SIZE)
                queries = projected[:quarter, lanes][features]
                keys = projected[quarter : 2 * quarter, lanes][features]
                values = projected[2 * quarter :, lanes][features]
                scores = lax.dot_general(
                    keys, queries, CONTRACT_FIRST, preferred_element_type=F32
                )
                scores = jnp.where(same, scores * scale, -jnp.inf)
                scores = jnp.exp(scores - jnp.max(scores, axis=0, keepdims=True))
                total = jnp.sum(scores, axis=0, keepdims=True)
                part = jnp.dot(values, scores.astype(BF16), preferred_element_type=F32)
                target = slice(lower + head * HEAD_SIZE, lower + (head + 1) * HEAD_SIZE)
                mixed[target, lanes] = (part / total).astype(BF16)

    attend(triple[...], 0)
    for copy in copies:
        copy.wait()
    attend(far[quarter : 4 * quarter], quarter)
    for place in range(places):
        lanes = slice(place * both, (place + 1) * both)
        partial = lax.dot_general(
            mixed[:quarter, lanes], mixing[...], CONTRACT_FIRST, preferred_element_type=F32
        )
        partial += lax.dot_general(
            mixed[quarter:, lanes], far[4 * quarter :], CONTRACT_FIRST, preferred_element_type=F32
        )
        kept[place] = partial[:rows]
        sent[place] = partial[rows:].astype(BF16)


def column(own, other, label, triple, mixing, piece, rest, pair):
    places, rows, model = own.shape
    quarter = mixing.shape[0]
    tokens = 2 * places * rows
    return pl.pallas_call(
        column_kernel,
        out_shape=(
            jax.ShapeDtypeStruct(own.shape, F32),
            jax.ShapeDtypeStruct(own.shape, BF16),
        ),
        in_specs=[IN_SMEM] + [IN_VMEM] * 6 + [ANYWHERE] * 2,
        out_specs=(IN_VMEM, IN_VMEM),
        scratch_shapes=[
            pltpu.VMEM((places, 2 * rows, model), BF16),
            pltpu.VMEM((2 * piece.shape[0], model), BF16),
            pltpu.VMEM((3 * quarter, tokens), BF16),
            pltpu.VMEM((2 * quarter, tokens), BF16),
            pltpu.SemaphoreType.DMA((2,)),
        ],
        compiler_params=GRANT,
        name="column",
    )(pair, label[None, :], label[:, None], own, other, triple.reshape(-1, model), mixing, piece, rest)


def feed_forward_kernel(
    pair_ref, normed, expand, contract, piece, rest, out,
    near_expand, near_contract, far_piece, far_rest, hidden, semaphores,
):
    moves = (
        (expand, near_expand), (piece, far_piece), (rest, far_rest), (contract, near_contract)
    )
    copies = [
        pltpu.make_async_copy(source, target, semaphores.at[index])
        for index, (source, target) in enumerate(moves)
    ]
    for copy in copies:
        copy.start()
    width = near_expand.shape[1]
    tile = width // 3
    values = normed[...]
    pair = pair_ref[0]

    def raise_by(weights, lower):
        for start in range(0, width, tile):
            up = jnp.dot(values, weights[:, start : start + tile], preferred_element_type=F32)
            up = 0.5 * up * (1.0 + lax.erf(up * 2.0**-0.5))
            hidden[:, lower + start : lower + start + tile] = up.astype(BF16)

    def lower_by(near_weights, far_weights):
        down = jnp.dot(hidden[:, :width], near_weights[...], preferred_element_type=F32)
        down += jnp.dot(hidden[:, width:], far_weights[...], preferred_element_type=F32)
        out[...] = down.astype(out.dtype)

    copies[0].wait()
    raise_by(near_expand, 0)
    copies[1].wait()
    copies[2].wait()

    @pl.when(pair == 0)
    def _():
        raise_by(far_piece, width)

    @pl.when(pair != 0)
    def _():
        raise_by(far_rest, width)

    copies[3].wait()

    @pl.when(pair == 0)
    def _():
        lower_by(near_contract, far_rest)

    @pl.when(pair != 0)
    def _():
        lower_by(near_contract, far_piece)


def feed_forward(normed, expand, contract, piece, rest, pair, kind):
    places, rows, model = normed.shape
    tokens, width = places * rows, expand.shape[1]
    result = pl.pallas_call(
        feed_forward_kernel,
        out_shape=jax.ShapeDtypeStruct((tokens, model), kind),
        in_specs=[IN_SMEM, IN_VMEM] + [ANYWHERE] * 4,
        out_specs=IN_VMEM,
        scratch_shapes=[
            pltpu.VMEM((model, width), BF16),
            pltpu.VMEM((width, model), BF16),
            pltpu.VMEM((model, width), BF16),
            pltpu.VMEM((model, width), BF16),
            pltpu.VMEM((tokens, 2 * width), BF16),
            pltpu.SemaphoreType.DMA((4,)),
        ],
        compiler_params=GRANT,
        name="feed_forward",
    )(pair, normed.reshape(tokens, model), expand, contract, piece, rest)
    return result.reshape(normed.shape)


def core_sum(stream, kept, sent):
    return (stream.astype(F32) + kept + other_core(sent).astype(F32)).astype(BF16)


def shards(
    alignment_embedding,
    line_group_label,
    group_site_tally,
    horizontal_triple_matrix,
    horizontal_mixing_matrix,
    vertical_triple_matrix,
    vertical_mixing_matrix,
    expand_matrix,
    contract_matrix,
):
    lines, quarter, sites = alignment_embedding.shape
    row_groups = lax.axis_size(ROWS)
    chips = 2 * row_groups
    place = sites // chips
    pair = lax.axis_index("pair")
    chip = lax.axis_index("chip")
    core = lax.axis_index("core")
    label = line_group_label
    tally = group_site_tally
    families = tally.shape[0]

    across = other_chip(alignment_embedding)
    near = other_core(alignment_embedding)
    diagonal = other_core(across)
    pieces = (alignment_embedding, near, across, diagonal)
    spots = jnp.stack(
        [2 * chip + core, 2 * chip + 1 - core, 2 * (1 - chip) + core, 2 * (1 - chip) + 1 - core]
    ).astype(jnp.int32)
    first_pack = jnp.concatenate(
        [
            horizontal_mixing_matrix,
            vertical_triple_matrix.reshape(-1, vertical_triple_matrix.shape[-1]),
            vertical_mixing_matrix,
        ]
    )
    second_pack = jnp.concatenate([expand_matrix, contract_matrix])
    across, first_pack, second_pack = lax.optimization_barrier((across, first_pack, second_pack))
    first_piece = other_chip(half_rows(first_pack, pair))
    second_piece = other_chip(half_rows(second_pack, pair))
    first_rest = other_pair(first_piece)
    second_rest = other_pair(second_piece)

    start = lax.axis_index(ROWS) * lines
    label_here = lax.dynamic_slice_in_dim(label, start, lines)
    first, last = label_here[0], label_here[-1]
    counts = jnp.sum((label[:, None] == jnp.arange(families)).astype(F32), axis=0)
    scaling = HEAD_SIZE**-0.5 * lax.rsqrt(counts)[label_here]
    slots = 2 + max(min(families, lines) - 2, 1)
    slot = jnp.where(
        label_here == first, 0, jnp.where(label_here == last, 1, label_here - first + 1)
    )
    inner = jnp.clip(first + 1 + jnp.arange(slots - 2), 0, families - 1)
    tables, inner_weights, values = row_front(
        pieces, horizontal_triple_matrix, spots, slot, scaling, tally[inner], row_groups
    )
    tables, first_piece = lax.optimization_barrier((tables, first_piece))
    ends = label.reshape(row_groups, lines)[:, jnp.array([0, lines - 1])].reshape(-1)
    shared = tie(lax.all_to_all(tables, ROWS, 0, 0, tiled=True), ends, tally)
    shared = lax.all_to_all(shared, ROWS, 0, 0, tiled=True)
    mixed, sent = mix(shared, inner_weights, values, slot, chip)

    sent, first_rest, second_piece = lax.optimization_barrier((sent, first_rest, second_piece))
    own = lines // 4
    rows = chips * own
    here = jnp.stack([(2 * chip + core) * own, pair, core]).astype(jnp.int32)
    kept, sent = project(
        mixed,
        other_chip(sent),
        horizontal_mixing_matrix,
        first_piece,
        first_rest,
        pieces,
        spots,
        here,
    )

    blocks = settle(kept, other_core(sent), chips)
    blocks, second_rest = lax.optimization_barrier((blocks, second_rest))
    blocks = lax.all_to_all(blocks, ROWS + ("chip",), 0, 0, tiled=True)
    normed, after_row = arrive(blocks, place)
    label_cores = label.reshape(chips, 2, own)
    label_sites = jnp.concatenate(
        [
            lax.dynamic_index_in_dim(label_cores, index, 1, False).reshape(-1)
            for index in (core, 1 - core)
        ]
    )

    parity = pair.astype(jnp.int32).reshape(1)
    kept, sent = column(
        normed,
        other_core(normed),
        label_sites,
        vertical_triple_matrix,
        vertical_mixing_matrix,
        first_piece,
        first_rest,
        parity,
    )
    after_col = core_sum(after_row, kept, sent)

    normed = own_norm(after_col, -1)
    feed = (expand_matrix, contract_matrix, second_piece, second_rest, parity)
    kept = feed_forward(normed, *feed, F32)
    sent = feed_forward(other_core(normed), *feed, BF16)
    finished = core_sum(after_col, kept, sent)

    heads = after_col.shape[-1] // quarter
    finished = finished.reshape(place, row_groups, 2 * own, heads, quarter)
    finished = jnp.transpose(finished, (1, 3, 2, 0, 4)).reshape(-1, 2 * own * place, quarter)
    parts, wide = 2 * own * place // 2, quarter // 3 * 2
    finished = jnp.concatenate(
        [
            finished[:, :, :wide],
            jnp.concatenate([finished[:, :parts, wide:], finished[:, parts:, wide:]], axis=2),
        ],
        axis=1,
    )
    finished = lax.all_to_all(finished, ROWS + ("chip", "core"), 0, 0, tiled=True)
    narrow = finished[:, 2 * parts :]
    narrow = jnp.concatenate([narrow[:, :, : wide // 2], narrow[:, :, wide // 2 :]], axis=1)
    finished = jnp.concatenate([finished[:, : 2 * parts], narrow], axis=2)
    finished = finished.reshape(chips, 2, 2, own, place, quarter)
    finished = jnp.transpose(finished, (2, 1, 3, 5, 0, 4))
    return finished.reshape(lines, quarter, sites)


def solution(mesh):
    planes = mesh.shape["rows"] // 2
    split = Mesh(mesh.devices.reshape(planes, 2, 2, 2), ROWS + ("chip", "core"))
    heads = ("chip", "core")
    placed = (
        P(ROWS, heads, None),
        P(),
        P(),
        P(None, heads, None),
        P(heads, None),
        P(None, heads, None),
        P(heads, None),
        P(None, heads),
        P(heads, None),
    )
    return jax.shard_map(
        shards, mesh=split, in_specs=placed, out_specs=P(ROWS, heads, None), check_vma=False
    )
```

```python
import functools

import jax
import jax.numpy as jnp
from jax import lax
from jax.experimental import pallas as pl
from jax.experimental.pallas import tpu as pltpu
from jax.sharding import Mesh, PartitionSpec as P

HEAD_SIZE = 64
SWAP = [(0, 1), (1, 0)]
ROWS = ("plane", "pair")
BF16 = jnp.bfloat16
F32 = jnp.float32


def other_chip(value):
    return lax.ppermute(value, "chip", SWAP)


def other_pair(value):
    return lax.ppermute(value, "pair", SWAP)


def other_core(value):
    return lax.ppermute(value, "core", SWAP)


def in_order(first, second, index, axis):
    forward = jnp.concatenate([first, second], axis=axis)
    backward = jnp.concatenate([second, first], axis=axis)
    return jnp.where(index == 0, forward, backward)


def half_rows(value, index):
    rows = value.shape[0] // 2
    return lax.dynamic_slice_in_dim(value, index * rows, rows)


def own_norm(values, axis):
    values = values.astype(F32)
    average = jnp.mean(values, axis=axis, keepdims=True)
    centred = values - average
    variance = jnp.mean(centred * centred, axis=axis, keepdims=True)
    return (centred * lax.rsqrt(variance + 1e-05)).astype(BF16)


def masked_softmax(tables, tally):
    live = jnp.arange(tables.shape[-1])[None, :] < tally[:, None]
    tables = jnp.where(live[:, None, None, :], tables, -jnp.inf)
    return jax.nn.softmax(tables, axis=-1).astype(BF16)


CONTRACT_FIRST = (((0,), (0,)), ((), ()))
CONTRACT_LAST = (((1,), (1,)), ((), ()))
IN_VMEM = pl.BlockSpec(memory_space=pltpu.VMEM)
IN_SMEM = pl.BlockSpec(memory_space=pltpu.SMEM)
ANYWHERE = pl.BlockSpec(memory_space=pl.ANY)
GRANT = pltpu.CompilerParams(vmem_limit_bytes=40 * 2**20)


def slot_of(label_ref, start, lines, line):
    first, last = label_ref[start], label_ref[start + lines - 1]
    family = label_ref[start + line]
    return jnp.where(family == first, 0, jnp.where(family == last, 1, family - first + 1))


def quarter_spots(me_ref):
    chip, core = me_ref[1], me_ref[2]
    return (
        2 * chip + core, 2 * chip + 1 - core, 2 * (1 - chip) + core, 2 * (1 - chip) + 1 - core
    )


def row_front_kernel(
    start, lines, me_ref, label_ref, starts_ref, tally_ref, own, near, far, diagonal, triple, *refs
):
    if len(refs) == 3:
        value_ref, tables, normed = refs
        before = table_ref = None
    else:
        before, table_ref, inner_ref, value_ref, tables, normed = refs
    step = pl.program_id(0)
    group, quarter, sites = own.shape
    heads = quarter // HEAD_SIZE

    @pl.when(step == 0)
    def _():
        tables[...] = jnp.zeros_like(tables) if before is None else before[...]

    pieces = []
    for ref in (own, near, far, diagonal):
        lanes = jnp.concatenate([ref[line] for line in range(group)], axis=-1)
        pieces.append(lanes.astype(F32))
    size = 4 * quarter
    average = sum(jnp.sum(piece, axis=0, keepdims=True) for piece in pieces) / size
    pieces = [piece - average for piece in pieces]
    variance = sum(jnp.sum(piece * piece, axis=0, keepdims=True) for piece in pieces) / size
    inverse = lax.rsqrt(variance + 1e-05)
    for spot, piece in zip(quarter_spots(me_ref), pieces):
        spot = pl.multiple_of(spot * quarter, quarter)
        normed[pl.ds(spot, quarter), :] = (piece * inverse).astype(BF16)
    projected = jnp.dot(triple[...], normed[...], preferred_element_type=F32).astype(BF16)
    base = me_ref[0] * lines
    for line in range(group):
        part = projected[:, line * sites : (line + 1) * sites]
        value_ref[line] = part[2 * quarter :]
        place = start + step * group + line
        slot = slot_of(label_ref, base, lines, place)
        family = label_ref[base + place]
        members = jnp.full((1, sites), starts_ref[family + 1] - starts_ref[family], jnp.int32)
        scale = HEAD_SIZE**-0.5 * lax.rsqrt(members.astype(F32))
        for head in range(heads):
            lower = head * HEAD_SIZE
            queries = part[lower : lower + HEAD_SIZE]
            keys = part[quarter + lower : quarter + lower + HEAD_SIZE]
            logits = lax.dot_general(queries, keys, CONTRACT_FIRST, preferred_element_type=F32)
            tables[slot * heads + head] += logits * scale

    if table_ref is None:
        return

    @pl.when(step == pl.num_programs(0) - 1)
    def _():
        for index in range(2 * heads):
            table = tables[index].astype(BF16)
            if len(table_ref.shape) == 4:
                groups, _, rows, _ = table_ref.shape
                table_ref[:, index] = table.reshape(groups, rows, sites)
            else:
                table_ref[index] = table
        site = lax.broadcasted_iota(jnp.int32, (sites, sites), 1)

        def inner(index, carry):
            table = tables[2 * heads + index]
            family = label_ref[base] + 1 + index // heads
            family = jnp.minimum(family, tally_ref.shape[0] - 1)
            table = jnp.where(site < tally_ref[family], table, -jnp.inf)
            table = jnp.exp(table - jnp.max(table, axis=-1, keepdims=True))
            table = table / jnp.sum(table, axis=-1, keepdims=True)
            inner_ref[index] = table.astype(BF16)
            return carry

        lax.fori_loop(0, inner_ref.shape[0], inner, 0)


def row_front(pieces, triple, plan, slots, row_groups, start, lines_here, before=None):
    lines, quarter, sites = pieces[0].shape
    group = 4
    count = lines // group
    heads = quarter // HEAD_SIZE
    inner = slots - 2
    rows = sites // row_groups
    shape = (row_groups, 2 * heads, rows, sites) if rows % 16 == 0 else (2 * heads, sites, sites)
    block = pl.BlockSpec((group, quarter, sites), lambda step: (step, 0, 0))
    every = ((2 + inner) * heads, sites, sites)

    def whole(shape):
        return pl.BlockSpec(shape, lambda step: (0,) * len(shape))

    operands = (*pieces, triple.reshape(3 * quarter, 4 * quarter))
    in_specs = [IN_SMEM] * 4 + [block] * 4 + [whole((3 * quarter, 4 * quarter))]
    values = jax.ShapeDtypeStruct((lines, quarter, sites), BF16)
    normed = pltpu.VMEM((4 * quarter, group * sites), BF16)
    name = "row_front"
    if before is None:
        values, tables = pl.pallas_call(
            functools.partial(row_front_kernel, start, lines_here),
            grid=(count,),
            out_shape=(values, jax.ShapeDtypeStruct(every, F32)),
            in_specs=in_specs,
            out_specs=(block, whole(every)),
            scratch_shapes=[normed],
            compiler_params=GRANT,
            name=name,
        )(*plan, *operands)
        return tables, values
    tables, inner_weights, values = pl.pallas_call(
        functools.partial(row_front_kernel, start, lines_here),
        grid=(count,),
        out_shape=(
            jax.ShapeDtypeStruct(shape, BF16),
            jax.ShapeDtypeStruct((inner * heads, sites, sites), BF16),
            values,
        ),
        in_specs=in_specs + [whole(every)],
        out_specs=(whole(shape), whole((inner * heads, sites, sites)), block),
        scratch_shapes=[pltpu.VMEM(every, F32), normed],
        compiler_params=GRANT,
        name=name,
    )(*plan, *operands, before)
    if rows % 16:
        tables = jnp.transpose(tables.reshape(-1, row_groups, rows, sites), (1, 0, 2, 3))
    return tables, inner_weights, values


def tie_kernel(me_ref, label_ref, starts_ref, tally_ref, parts, out, weights):
    groups, pairs, rows, sites = parts.shape
    lines = label_ref.shape[0] // groups
    ends = [label_ref[g * lines + e * (lines - 1)] for g in range(groups) for e in range(2)]
    heads = pairs // 2
    site = lax.broadcasted_iota(jnp.int32, (heads, rows, sites), 2)
    for family in range(weights.shape[0]):
        total = jnp.zeros((heads, rows, sites), F32)
        for group in range(groups):
            for end in range(2):
                part = parts[group, end * heads : (end + 1) * heads].astype(F32)
                total += jnp.where(ends[2 * group + end] == family, part, 0.0)
        total = jnp.where(site < tally_ref[family], total, -jnp.inf)
        total = jnp.exp(total - jnp.max(total, axis=-1, keepdims=True))
        total = total / jnp.sum(total, axis=-1, keepdims=True)
        weights[family] = total.astype(BF16)
    for group in range(groups):
        for end in range(2):
            chosen = weights[ends[2 * group + end]]
            out[group, end * heads : (end + 1) * heads] = chosen


def tie(parts, plan):
    groups, pairs, rows, sites = parts.shape
    _, label, _, tally = plan
    if rows % 16 == 0:
        return pl.pallas_call(
            tie_kernel,
            out_shape=jax.ShapeDtypeStruct(parts.shape, BF16),
            in_specs=[IN_SMEM] * 4 + [IN_VMEM],
            out_specs=IN_VMEM,
            scratch_shapes=[pltpu.VMEM((tally.shape[0], pairs // 2, rows, sites), BF16)],
            compiler_params=GRANT,
            name="tie",
        )(*plan, parts)
    ends = jnp.stack([label.reshape(groups, -1)[:, 0], label.reshape(groups, -1)[:, -1]], axis=1)
    parts = parts.astype(F32).reshape(groups, 2, -1, rows, sites)
    member = (ends[:, :, None] == jnp.arange(tally.shape[0])).astype(F32)
    totals = jnp.einsum("stf,sthij->fhij", member, parts, precision=lax.Precision.HIGHEST)
    return masked_softmax(totals, tally)[ends].reshape(groups, pairs, rows, sites)


def mix_kernel(me_ref, label_ref, starts_ref, tally_ref, shared, inner, first, second, kept, sent):
    pairs, sites = shared.shape[1], first.shape[2]
    heads = pairs // 2
    half = kept.shape[0]

    def run(weights):
        weights[: 2 * heads] = jnp.stack(
            [shared[:, index].reshape(sites, sites) for index in range(2 * heads)]
        )
        weights[2 * heads :] = inner[...]
        chip = me_ref[1]

        @pl.when(chip == 0)
        def _():
            spread(weights, second, half, sent)
            spread(weights, first, 0, kept)

        @pl.when(chip != 0)
        def _():
            spread(weights, first, 0, sent)
            spread(weights, second, half, kept)

    def spread(weights, values, start, target):
        for line in range(half):
            slot = slot_of(label_ref, me_ref[0] * 2 * half, 2 * half, start + line)
            value = values[line]
            for head in range(heads):
                features = slice(head * HEAD_SIZE, (head + 1) * HEAD_SIZE)
                target[line, features] = lax.dot_general(
                    value[features],
                    weights[slot * heads + head],
                    CONTRACT_LAST,
                    preferred_element_type=F32,
                ).astype(BF16)

    pl.run_scoped(run, pltpu.VMEM((2 * heads + inner.shape[0], sites, sites), BF16))


def mix(shared, inner, first, second, plan):
    groups, pairs, rows, sites = shared.shape
    lines, quarter, _ = first.shape
    if rows % 16 == 0:
        half = jax.ShapeDtypeStruct(first.shape, BF16)
        return pl.pallas_call(
            mix_kernel,
            out_shape=(half, half),
            in_specs=[IN_SMEM] * 4 + [IN_VMEM] * 4,
            out_specs=(IN_VMEM, IN_VMEM),
            compiler_params=GRANT,
            name="mix",
        )(*plan, shared, inner, first, second)
    me, label = plan[:2]
    chip = me[1]
    label = lax.dynamic_slice_in_dim(label, me[0] * 2 * lines, 2 * lines)
    slot = slot_of(label, 0, 2 * lines, jnp.arange(2 * lines))
    ends = jnp.transpose(shared, (1, 0, 2, 3)).reshape(2, pairs // 2, sites, sites)
    weights = jnp.concatenate([ends, inner.reshape(-1, *ends.shape[1:])])[slot]
    values = jnp.concatenate([first, second]).reshape(2 * lines, -1, HEAD_SIZE, sites)
    mixed = jnp.einsum("rhdj,rhij->rhdi", values, weights, preferred_element_type=F32)
    mixed = mixed.astype(BF16).reshape(2 * lines, quarter, sites)
    return half_rows(mixed, chip), half_rows(mixed, 1 - chip)


def project_kernel(
    me_ref, mixed, got, mixing, piece, *refs
):
    halves = refs[:4], refs[4:8]
    kept, sent, stream, far, semaphores = refs[8:]
    lines, _, sites = stream.shape
    quarter = mixing.shape[0]
    chip, core = me_ref[1], me_ref[2]

    def copies(half):
        result = []
        for index, (spot, source) in enumerate(zip(quarter_spots(me_ref), half)):
            spot = pl.multiple_of(spot * quarter, quarter)
            result.append(
                pltpu.make_async_copy(
                    source.at[pl.ds(core * lines, lines)],
                    stream.at[:, pl.ds(spot, quarter)],
                    semaphores.at[index],
                )
            )
        return result

    for index, half in enumerate(halves):

        @pl.when(chip == index)
        def _(half=half):
            for copy in copies(half):
                copy.start()

    fetch = pltpu.make_async_copy(piece.at[pl.ds(2 * quarter, quarter)], far, semaphores.at[4])
    fetch.start()

    def partial(row):
        near_part = lax.dot_general(
            mixed[row], mixing[...], CONTRACT_FIRST, preferred_element_type=F32
        )
        return near_part + lax.dot_general(
            got[row], far[...], CONTRACT_FIRST, preferred_element_type=F32
        )

    fetch.wait()
    for line in range(lines):
        sent[line] = partial((1 - core) * lines + line).astype(BF16)
    for copy in copies(halves[0]):
        copy.wait()
    for line in range(lines):
        kept[line] = partial(core * lines + line) + stream[line].astype(F32).T


def project(mixed, got, mixing, piece, halves, me):
    half, quarter, sites = mixed.shape
    lines, model = half // 2, mixing.shape[1]
    out = (lines, sites, model)
    return pl.pallas_call(
        project_kernel,
        out_shape=(jax.ShapeDtypeStruct(out, F32), jax.ShapeDtypeStruct(out, BF16)),
        in_specs=[IN_SMEM] + [IN_VMEM] * 3 + [ANYWHERE] * 9,
        out_specs=(IN_VMEM, IN_VMEM),
        scratch_shapes=[
            pltpu.VMEM((lines, model, sites), BF16),
            pltpu.VMEM((quarter, model), BF16),
            pltpu.SemaphoreType.DMA((5,)),
        ],
        compiler_params=GRANT,
        name="project",
    )(me, mixed, got, mixing, piece, *halves[0], *halves[1])


def settle_kernel(kept, got, out):
    lines, sites, model = kept.shape
    chips = out.shape[0]
    parts = []
    for line in range(lines):
        total = kept[line] + got[line].astype(F32)
        parts.append(total.reshape(chips, sites // chips, model))
    out[...] = jnp.concatenate(parts, axis=1).astype(BF16)


def settle(kept, got, chips):
    lines, sites, model = kept.shape
    place = sites // chips
    if place % 8 == 0:
        return pl.pallas_call(
            settle_kernel,
            out_shape=jax.ShapeDtypeStruct((chips, lines * place, model), BF16),
            in_specs=[IN_VMEM, IN_VMEM],
            out_specs=IN_VMEM,
            compiler_params=GRANT,
            name="settle",
        )(kept, got)
    total = (kept + got.astype(F32)).astype(BF16).reshape(lines, chips, place, model)
    return jnp.transpose(total, (1, 0, 2, 3)).reshape(chips, lines * place, model)


def arrive_kernel(blocks, normed, stream, tokens):
    chips, count, model = blocks.shape
    places, rows, _ = normed.shape
    lanes = tokens.shape[-1]
    flat = blocks[...].reshape(chips * count, model).astype(F32)
    for index in range(tokens.shape[0]):
        tokens[index] = flat[:, index * lanes : (index + 1) * lanes]
    for place in range(places):
        values = [
            tokens[index, pl.ds(place, rows, stride=places), :] for index in range(tokens.shape[0])
        ]
        values = jnp.concatenate(values, axis=-1)
        stream[place] = values.astype(BF16)
        centred = values - jnp.mean(values, axis=-1, keepdims=True)
        variance = jnp.mean(centred * centred, axis=-1, keepdims=True)
        normed[place] = (centred * lax.rsqrt(variance + 1e-05)).astype(BF16)


def arrive(blocks, place):
    chips, count, model = blocks.shape
    rows = chips * count // place
    if place % 8 == 0:
        shape = jax.ShapeDtypeStruct((place, rows, model), BF16)
        return pl.pallas_call(
            arrive_kernel,
            out_shape=(shape, shape),
            in_specs=[IN_VMEM],
            out_specs=(IN_VMEM, IN_VMEM),
            scratch_shapes=[pltpu.VMEM((model // 128, chips * count, 128), F32)],
            compiler_params=GRANT,
            name="arrive",
        )(blocks)
    stream = jnp.transpose(blocks.reshape(rows, place, model), (1, 0, 2))
    return own_norm(stream, -1), stream


def column_kernel(
    lines, me_ref, starts_ref, own, other, triple, mixing, piece, rest,
    kept, sent, normed, far, projected, mixed, semaphores,
):
    half = far.shape[0] // 2
    core, pair = me_ref[2], me_ref[3]
    copies = []
    for index, (source, place) in enumerate(((piece, pair), (rest, 1 - pair))):
        spot = pl.multiple_of(place * half, half)
        target = far.at[pl.ds(spot, half)]
        copies.append(
            pltpu.make_async_copy(source.at[pl.ds(0, half)], target, semaphores.at[index])
        )
    for copy in copies:
        copy.start()
    places, rows, model = own.shape
    quarter = mixing.shape[0]
    both = 2 * rows
    normed[:, :rows] = own[...]
    normed[:, rows:] = other[...]
    flat = normed[...].reshape(places * both, model)

    def families(axis):
        shape = (both, 1) if axis == 0 else (1, both)
        index = lax.broadcasted_iota(jnp.int32, shape, axis)
        line = jnp.where(index < rows, core * lines, (1 - core) * lines)
        index = jnp.where(index < rows, index, index - rows)
        line += index // lines * (2 * lines) + index % lines
        return sum(
            (line >= starts_ref[family]).astype(jnp.int32)
            for family in range(1, starts_ref.shape[0] - 1)
        )

    same = families(0) == families(1)
    scale = HEAD_SIZE**-0.5

    def attend(weights, lower):
        projected[...] = lax.dot_general(
            weights, flat, CONTRACT_LAST, preferred_element_type=F32
        ).astype(BF16)
        for place in range(places):
            lanes = slice(place * both, (place + 1) * both)
            for head in range(quarter // HEAD_SIZE):
                features = slice(head * HEAD_SIZE, (head + 1) * HEAD_SIZE)
                queries = projected[:quarter, lanes][features]
                keys = projected[quarter : 2 * quarter, lanes][features]
                values = projected[2 * quarter :, lanes][features]
                scores = lax.dot_general(
                    keys, queries, CONTRACT_FIRST, preferred_element_type=F32
                )
                scores = jnp.where(same, scores * scale, -jnp.inf)
                scores = jnp.exp(scores - jnp.max(scores, axis=0, keepdims=True))
                total = jnp.sum(scores, axis=0, keepdims=True)
                part = jnp.dot(values, scores.astype(BF16), preferred_element_type=F32)
                target = slice(lower + head * HEAD_SIZE, lower + (head + 1) * HEAD_SIZE)
                mixed[target, lanes] = (part / total).astype(BF16)

    attend(triple[...], 0)
    for copy in copies:
        copy.wait()
    attend(far[: 3 * quarter], quarter)
    for place in range(places):
        lanes = slice(place * both, (place + 1) * both)
        partial = lax.dot_general(
            mixed[:quarter, lanes], mixing[...], CONTRACT_FIRST, preferred_element_type=F32
        )
        partial += lax.dot_general(
            mixed[quarter:, lanes], far[3 * quarter :], CONTRACT_FIRST, preferred_element_type=F32
        )
        kept[place] = partial[:rows]
        sent[place] = partial[rows:].astype(BF16)


def column(own, other, triple, mixing, piece, rest, plan, lines):
    places, rows, model = own.shape
    quarter = mixing.shape[0]
    tokens = 2 * places * rows
    return pl.pallas_call(
        functools.partial(column_kernel, lines),
        out_shape=(
            jax.ShapeDtypeStruct(own.shape, F32),
            jax.ShapeDtypeStruct(own.shape, BF16),
        ),
        in_specs=[IN_SMEM] * 2 + [IN_VMEM] * 4 + [ANYWHERE] * 2,
        out_specs=(IN_VMEM, IN_VMEM),
        scratch_shapes=[
            pltpu.VMEM((places, 2 * rows, model), BF16),
            pltpu.VMEM((4 * quarter, model), BF16),
            pltpu.VMEM((3 * quarter, tokens), BF16),
            pltpu.VMEM((2 * quarter, tokens), BF16),
            pltpu.SemaphoreType.DMA((2,)),
        ],
        compiler_params=GRANT,
        name="column",
    )(plan[0], plan[2], own, other, triple.reshape(-1, model), mixing, piece, rest)


def feed_forward_kernel(
    me_ref, normed, expand, contract, piece, rest, late, out,
    near_expand, near_contract, far_piece, far_rest, hidden, semaphores,
):
    shared, direct = rest.shape[0], late.shape[0] // 2
    pair = me_ref[3]
    moves = (
        (expand, near_expand),
        (contract, near_contract),
        (piece.at[pl.ds(piece.shape[0] - shared, shared)], far_piece.at[pl.ds(0, shared)]),
        (rest, far_rest.at[pl.ds(0, shared)]),
    )
    copies = [
        pltpu.make_async_copy(source, target, semaphores.at[index])
        for index, (source, target) in enumerate(moves)
    ]

    def tails(first, second):
        return [
            pltpu.make_async_copy(
                late.at[pl.ds(index * direct, direct)],
                target.at[pl.ds(shared, direct)],
                semaphores.at[4 + index],
            )
            for index, target in enumerate((first, second))
        ]

    for copy in copies:
        copy.start()

    @pl.when(pair == 0)
    def _():
        for copy in tails(far_piece, far_rest):
            copy.start()

    @pl.when(pair != 0)
    def _():
        for copy in tails(far_rest, far_piece):
            copy.start()

    width = near_expand.shape[1]
    tile = width // 3
    values = normed[...]

    def raise_by(weights, lower):
        for start in range(0, width, tile):
            up = jnp.dot(values, weights[:, start : start + tile], preferred_element_type=F32)
            up = 0.5 * up * (1.0 + lax.erf(up * 2.0**-0.5))
            hidden[:, lower + start : lower + start + tile] = up.astype(BF16)

    def lower_by(near_weights, far_weights):
        down = jnp.dot(hidden[:, :width], near_weights[...], preferred_element_type=F32)
        down += jnp.dot(hidden[:, width:], far_weights[...], preferred_element_type=F32)
        out[...] = down.astype(out.dtype)

    copies[0].wait()
    raise_by(near_expand, 0)
    for copy in copies[2:] + tails(far_piece, far_rest):
        copy.wait()

    @pl.when(pair == 0)
    def _():
        raise_by(far_piece, width)

    @pl.when(pair != 0)
    def _():
        raise_by(far_rest, width)

    copies[1].wait()

    @pl.when(pair == 0)
    def _():
        lower_by(near_contract, far_rest)

    @pl.when(pair != 0)
    def _():
        lower_by(near_contract, far_piece)


def feed_forward(normed, expand, contract, piece, rest, late, me, kind):
    places, rows, model = normed.shape
    tokens, width = places * rows, expand.shape[1]
    result = pl.pallas_call(
        feed_forward_kernel,
        out_shape=jax.ShapeDtypeStruct((tokens, model), kind),
        in_specs=[IN_SMEM, IN_VMEM] + [ANYWHERE] * 5,
        out_specs=IN_VMEM,
        scratch_shapes=[
            pltpu.VMEM((model, width), BF16),
            pltpu.VMEM((width, model), BF16),
            pltpu.VMEM((model, width), BF16),
            pltpu.VMEM((model, width), BF16),
            pltpu.VMEM((tokens, 2 * width), BF16),
            pltpu.SemaphoreType.DMA((6,)),
        ],
        compiler_params=GRANT,
        name="feed_forward",
    )(me, normed.reshape(tokens, model), expand, contract, piece, rest, late)
    return result.reshape(normed.shape)


def core_sum(stream, kept, sent):
    return (stream.astype(F32) + kept + other_core(sent).astype(F32)).astype(BF16)


def shards(
    alignment_embedding,
    line_group_label,
    group_site_tally,
    horizontal_triple_matrix,
    horizontal_mixing_matrix,
    vertical_triple_matrix,
    vertical_mixing_matrix,
    expand_matrix,
    contract_matrix,
):
    lines, quarter, sites = alignment_embedding.shape
    row_groups = lax.axis_size(ROWS)
    own = lines // 4
    chips = 2 * row_groups
    place = sites // chips
    pair = lax.axis_index("pair")
    chip = lax.axis_index("chip")
    core = lax.axis_index("core")
    label = line_group_label
    tally = group_site_tally
    families = tally.shape[0]

    starts = jnp.sum(label[:, None] < jnp.arange(families + 1), axis=0, dtype=jnp.int32)
    me = jnp.stack([lax.axis_index(ROWS), chip, core, pair]).astype(jnp.int32)

    halves = (alignment_embedding[: lines // 2], alignment_embedding[lines // 2 :])
    across = [other_chip(half) for half in halves]
    near = [other_core(half) for half in halves]
    first_pack = jnp.concatenate(
        [
            vertical_triple_matrix.reshape(-1, vertical_triple_matrix.shape[-1]),
            vertical_mixing_matrix,
        ]
    )
    second_pack = jnp.concatenate([expand_matrix, contract_matrix])
    column_rows = first_pack.shape[0] // 2
    shared_rows = expand_matrix.shape[0] * 3 // 4
    feed_pack = half_rows(second_pack, pair)[:shared_rows]
    pack = jnp.concatenate([half_rows(first_pack, pair), horizontal_mixing_matrix, feed_pack])
    late_pack = jnp.concatenate([expand_matrix[shared_rows:], contract_matrix[shared_rows:]])
    across[0], pack, late_pack, starts, me = lax.optimization_barrier(
        (across[0], pack, late_pack, starts, me)
    )
    plan = (me, label, starts, tally)
    diagonal = [other_core(across[0])]
    across[1], pack = lax.optimization_barrier((across[1], pack))
    diagonal.append(other_core(across[1]))
    piece = other_chip(pack)

    tables, values = None, []
    for index in range(2):
        *tables, value = row_front(
            (halves[index], near[index], across[index], diagonal[index]),
            horizontal_triple_matrix,
            plan,
            2 + max(min(families, lines) - 2, 1),
            row_groups,
            index * lines // 2,
            lines,
            before=tables[0] if index else None,
        )
        values.append(value)
    shared, inner_weights = tables
    parts = lax.all_to_all(shared, ROWS, 0, 0, tiled=True)
    shared = lax.all_to_all(tie(parts, plan), ROWS, 0, 0, tiled=True)
    mixed, sent = mix(shared, inner_weights, *values, plan)
    sent, piece, late_pack = lax.optimization_barrier((sent, piece, late_pack))
    first_rest = other_pair(piece[:column_rows])
    second_rest = other_pair(piece[column_rows + quarter :])
    late_piece = other_chip(late_pack)

    got, first_rest = lax.optimization_barrier((other_chip(sent), first_rest))
    kept, sent = project(
        mixed,
        got,
        horizontal_mixing_matrix,
        piece,
        list(zip(halves, near, across, diagonal)),
        me,
    )

    blocks = settle(kept, other_core(sent), chips)
    blocks = lax.all_to_all(blocks, ROWS + ("chip",), 0, 0, tiled=True)
    normed, after_row = arrive(blocks, place)
    normed, second_rest, late_piece = lax.optimization_barrier((normed, second_rest, late_piece))
    kept, sent = column(
        normed,
        other_core(normed),
        vertical_triple_matrix,
        vertical_mixing_matrix,
        piece,
        first_rest,
        plan,
        lines // 4,
    )
    after_col = core_sum(after_row, kept, sent)

    normed = own_norm(after_col, -1)
    feed = (expand_matrix, contract_matrix, piece, second_rest, late_piece, me)
    kept = feed_forward(normed, *feed, F32)
    sent = feed_forward(other_core(normed), *feed, BF16)
    finished = core_sum(after_col, kept, sent)

    heads = after_col.shape[-1] // quarter
    finished = finished.reshape(place, row_groups, 2 * own, heads, quarter)
    finished = jnp.transpose(finished, (1, 3, 2, 0, 4)).reshape(-1, 2 * own * place, quarter)
    parts, wide = 2 * own * place // 2, quarter // 3 * 2
    finished = jnp.concatenate(
        [
            finished[:, :, :wide],
            jnp.concatenate([finished[:, :parts, wide:], finished[:, parts:, wide:]], axis=2),
        ],
        axis=1,
    )
    finished = lax.all_to_all(finished, ROWS + ("chip", "core"), 0, 0, tiled=True)
    narrow = finished[:, 2 * parts :]
    narrow = jnp.concatenate([narrow[:, :, : wide // 2], narrow[:, :, wide // 2 :]], axis=1)
    finished = jnp.concatenate([finished[:, : 2 * parts], narrow], axis=2)
    finished = finished.reshape(chips, 2, 2, own, place, quarter)
    finished = jnp.transpose(finished, (2, 1, 3, 5, 0, 4))
    return finished.reshape(lines, quarter, sites)


def solution(mesh):
    planes = mesh.shape["rows"] // 2
    split = Mesh(mesh.devices.reshape(planes, 2, 2, 2), ROWS + ("chip", "core"))
    heads = ("chip", "core")
    placed = (
        P(ROWS, heads, None),
        P(),
        P(),
        P(None, heads, None),
        P(heads, None),
        P(None, heads, None),
        P(heads, None),
        P(None, heads),
        P(heads, None),
    )
    return jax.shard_map(
        shards, mesh=split, in_specs=placed, out_specs=P(ROWS, heads, None), check_vma=False
    )
```

```python
import functools

import jax
import jax.numpy as jnp
from jax import lax
from jax.experimental import pallas as pl
from jax.experimental.pallas import tpu as pltpu
from jax.sharding import Mesh, PartitionSpec as P

HEAD_SIZE = 64
SWAP = [(0, 1), (1, 0)]
ROWS = ("far", "plane", "pair")
BF16 = jnp.bfloat16
F32 = jnp.float32


def other_chip(value):
    return lax.ppermute(value, "chip", SWAP)


def other_pair(value):
    return lax.ppermute(value, "pair", SWAP)


def other_plane(value):
    return lax.ppermute(value, "plane", SWAP)


def other_core(value):
    return lax.ppermute(value, "core", SWAP)


def in_order(first, second, index, axis):
    forward = jnp.concatenate([first, second], axis=axis)
    backward = jnp.concatenate([second, first], axis=axis)
    return jnp.where(index == 0, forward, backward)


def half_rows(value, index):
    rows = value.shape[0] // 2
    return lax.dynamic_slice_in_dim(value, index * rows, rows)


def own_norm(values, axis):
    values = values.astype(F32)
    average = jnp.mean(values, axis=axis, keepdims=True)
    centred = values - average
    variance = jnp.mean(centred * centred, axis=axis, keepdims=True)
    return (centred * lax.rsqrt(variance + 1e-05)).astype(BF16)


def masked_softmax(tables, tally):
    live = jnp.arange(tables.shape[-1])[None, :] < tally[:, None]
    tables = jnp.where(live[:, None, None, :], tables, -jnp.inf)
    return jax.nn.softmax(tables, axis=-1).astype(BF16)


CONTRACT_FIRST = (((0,), (0,)), ((), ()))
CONTRACT_LAST = (((1,), (1,)), ((), ()))
IN_VMEM = pl.BlockSpec(memory_space=pltpu.VMEM)
IN_SMEM = pl.BlockSpec(memory_space=pltpu.SMEM)
IN_HBM = pl.BlockSpec(memory_space=pltpu.HBM)
GRANT = pltpu.CompilerParams(vmem_limit_bytes=40 * 2**20)


def slot_of(label_ref, start, lines, line):
    first, last = label_ref[start], label_ref[start + lines - 1]
    family = label_ref[start + line]
    return jnp.where(family == first, 0, jnp.where(family == last, 1, family - first + 1))


def quarter_spots(me_ref):
    chip, core = me_ref[1], me_ref[2]
    return (
        2 * chip + core, 2 * chip + 1 - core, 2 * (1 - chip) + core, 2 * (1 - chip) + 1 - core
    )


def row_front_kernel(
    lines, me_ref, label_ref, starts_ref, tally_ref, own, near, far, diagonal, triple,
    table_ref, inner_ref, value_ref, tables, normed,
):
    step = pl.program_id(0)
    group, quarter, sites = own.shape
    heads = quarter // HEAD_SIZE

    @pl.when(step == 0)
    def _():
        tables[...] = jnp.zeros_like(tables)

    pieces = []
    for ref in (own, near, far, diagonal):
        lanes = jnp.concatenate([ref[line] for line in range(group)], axis=-1)
        pieces.append(lanes.astype(F32))
    size = 4 * quarter
    average = sum(jnp.sum(piece, axis=0, keepdims=True) for piece in pieces) / size
    pieces = [piece - average for piece in pieces]
    variance = sum(jnp.sum(piece * piece, axis=0, keepdims=True) for piece in pieces) / size
    inverse = lax.rsqrt(variance + 1e-05)
    for spot, piece in zip(quarter_spots(me_ref), pieces):
        spot = pl.multiple_of(spot * quarter, quarter)
        normed[pl.ds(spot, quarter), :] = (piece * inverse).astype(BF16)
    projected = jnp.dot(triple[...], normed[...], preferred_element_type=F32).astype(BF16)
    base = me_ref[0] * lines
    jobs = []
    for line in range(group):
        part = projected[:, line * sites : (line + 1) * sites]
        value_ref[line] = part[2 * quarter :]
        place = step * group + line
        slot = slot_of(label_ref, base, lines, place)
        family = label_ref[base + place]
        members = jnp.full((1, sites), starts_ref[family + 1] - starts_ref[family], jnp.int32)
        scale = HEAD_SIZE**-0.5 * lax.rsqrt(members.astype(F32))
        for head in range(heads):
            lower = head * HEAD_SIZE
            queries = part[lower : lower + HEAD_SIZE]
            keys = part[quarter + lower : quarter + lower + HEAD_SIZE]
            logits = lax.dot_general(queries, keys, CONTRACT_FIRST, preferred_element_type=F32)
            jobs.append((slot * heads + head, logits, scale))
    for index, logits, scale in jobs:
        tables[index] += logits * scale

    @pl.when(step == pl.num_programs(0) - 1)
    def _():
        for index in range(2 * heads):
            table = tables[index].astype(BF16)
            if len(table_ref.shape) == 4:
                groups, _, rows, _ = table_ref.shape
                table_ref[:, index] = table.reshape(groups, rows, sites)
            else:
                table_ref[index] = table
        site = lax.broadcasted_iota(jnp.int32, (sites, sites), 1)

        def inner(index, carry):
            table = tables[2 * heads + index]
            family = label_ref[base] + 1 + index // heads
            family = jnp.minimum(family, tally_ref.shape[0] - 1)
            table = jnp.where(site < tally_ref[family], table, -jnp.inf)
            table = jnp.exp(table - jnp.max(table, axis=-1, keepdims=True))
            table = table / jnp.sum(table, axis=-1, keepdims=True)
            inner_ref[index] = table.astype(BF16)
            return carry

        lax.fori_loop(0, inner_ref.shape[0], inner, 0)


def row_front(pieces, triple, plan, slots, row_groups):
    lines, quarter, sites = pieces[0].shape
    group = 4
    heads = quarter // HEAD_SIZE
    inner = slots - 2
    rows = sites // row_groups
    shape = (row_groups, 2 * heads, rows, sites) if rows % 16 == 0 else (2 * heads, sites, sites)
    block = pl.BlockSpec((group, quarter, sites), lambda step: (step, 0, 0))

    def whole(shape):
        return pl.BlockSpec(shape, lambda step: (0,) * len(shape))

    tables, inner_weights, values = pl.pallas_call(
        functools.partial(row_front_kernel, lines),
        grid=(lines // group,),
        out_shape=(
            jax.ShapeDtypeStruct(shape, BF16),
            jax.ShapeDtypeStruct((inner * heads, sites, sites), BF16),
            jax.ShapeDtypeStruct((lines, quarter, sites), BF16),
        ),
        in_specs=[IN_SMEM] * 4 + [block] * 4 + [whole((3 * quarter, 4 * quarter))],
        out_specs=(whole(shape), whole((inner * heads, sites, sites)), block),
        scratch_shapes=[
            pltpu.VMEM((slots * heads, sites, sites), F32),
            pltpu.VMEM((4 * quarter, group * sites), BF16),
        ],
        compiler_params=GRANT,
        name="row_front",
    )(*plan, *pieces, triple.reshape(3 * quarter, 4 * quarter))
    if rows % 16:
        tables = jnp.transpose(tables.reshape(-1, row_groups, rows, sites), (1, 0, 2, 3))
    return tables, inner_weights, values


def tie_kernel(me_ref, label_ref, starts_ref, tally_ref, parts, out, weights):
    groups, pairs, rows, sites = parts.shape
    lines = label_ref.shape[0] // groups
    ends = [label_ref[g * lines + e * (lines - 1)] for g in range(groups) for e in range(2)]
    heads = pairs // 2
    site = lax.broadcasted_iota(jnp.int32, (heads, rows, sites), 2)
    for family in range(weights.shape[0]):
        total = jnp.zeros((heads, rows, sites), F32)
        for group in range(groups):
            for end in range(2):
                part = parts[group, end * heads : (end + 1) * heads].astype(F32)
                total += jnp.where(ends[2 * group + end] == family, part, 0.0)
        total = jnp.where(site < tally_ref[family], total, -jnp.inf)
        total = jnp.exp(total - jnp.max(total, axis=-1, keepdims=True))
        total = total / jnp.sum(total, axis=-1, keepdims=True)
        weights[family] = total.astype(BF16)
    for group in range(groups):
        for end in range(2):
            chosen = weights[ends[2 * group + end]]
            out[group, end * heads : (end + 1) * heads] = chosen


def tie(parts, plan):
    groups, pairs, rows, sites = parts.shape
    _, label, _, tally = plan
    if rows % 16 == 0:
        return pl.pallas_call(
            tie_kernel,
            out_shape=jax.ShapeDtypeStruct(parts.shape, BF16),
            in_specs=[IN_SMEM] * 4 + [IN_VMEM],
            out_specs=IN_VMEM,
            scratch_shapes=[pltpu.VMEM((tally.shape[0], pairs // 2, rows, sites), BF16)],
            compiler_params=GRANT,
            name="tie",
        )(*plan, parts)
    ends = jnp.stack([label.reshape(groups, -1)[:, 0], label.reshape(groups, -1)[:, -1]], axis=1)
    parts = parts.astype(F32).reshape(groups, 2, -1, rows, sites)
    member = (ends[:, :, None] == jnp.arange(tally.shape[0])).astype(F32)
    totals = jnp.einsum("stf,sthij->fhij", member, parts, precision=lax.Precision.HIGHEST)
    return masked_softmax(totals, tally)[ends].reshape(groups, pairs, rows, sites)


def mix_kernel(
    me_ref, label_ref, starts_ref, tally_ref, shared, inner, values, kept, sent, weights
):
    heads, sites = shared.shape[1] // 2, values.shape[2]
    half = kept.shape[0]
    for index in range(2 * heads):
        weights[index] = shared[:, index].reshape(sites, sites)
    weights[2 * heads :] = inner[...]
    for target, chip in ((sent, 1 - me_ref[1]), (kept, me_ref[1])):
        jobs = []
        for line in range(half):
            row = chip * half + line
            slot = slot_of(label_ref, me_ref[0] * 2 * half, 2 * half, row)
            value = values[row]
            for head in range(heads):
                features = slice(head * HEAD_SIZE, (head + 1) * HEAD_SIZE)
                result = lax.dot_general(
                    value[features],
                    weights[slot * heads + head],
                    CONTRACT_LAST,
                    preferred_element_type=F32,
                )
                jobs.append((line, features, result))
        for line, features, result in jobs:
            target[line, features] = result.astype(BF16)


def mix(shared, inner, values, plan):
    groups, pairs, rows, sites = shared.shape
    lines, quarter, _ = values.shape
    if rows % 16 == 0:
        half = jax.ShapeDtypeStruct((lines // 2, quarter, sites), BF16)
        return pl.pallas_call(
            mix_kernel,
            out_shape=(half, half),
            in_specs=[IN_SMEM] * 4 + [IN_VMEM] * 3,
            out_specs=(IN_VMEM, IN_VMEM),
            scratch_shapes=[pltpu.VMEM((pairs + inner.shape[0], sites, sites), BF16)],
            compiler_params=GRANT,
            name="mix",
        )(*plan, shared, inner, values)
    me, label = plan[:2]
    chip = me[1]
    label = lax.dynamic_slice_in_dim(label, me[0] * lines, lines)
    slot = slot_of(label, 0, lines, jnp.arange(lines))
    ends = jnp.transpose(shared, (1, 0, 2, 3)).reshape(2, pairs // 2, sites, sites)
    weights = jnp.concatenate([ends, inner.reshape(-1, *ends.shape[1:])])[slot]
    values = values.reshape(lines, -1, HEAD_SIZE, sites)
    mixed = jnp.einsum("rhdj,rhij->rhdi", values, weights, preferred_element_type=F32)
    mixed = mixed.astype(BF16).reshape(lines, quarter, sites)
    return half_rows(mixed, chip), half_rows(mixed, 1 - chip)


def project_kernel(
    me_ref, mixed, got, mixing, piece, *refs
):
    pieces = refs[:4]
    kept, sent, stream, far, semaphores = refs[4:]
    lines, _, sites = stream.shape
    quarter = mixing.shape[0]
    chip, core = me_ref[1], me_ref[2]
    copies = []
    for index, (spot, source) in enumerate(zip(quarter_spots(me_ref), pieces)):
        spot = pl.multiple_of(spot * quarter, quarter)
        copies.append(
            pltpu.make_async_copy(
                source.at[pl.ds((2 * chip + core) * lines, lines)],
                stream.at[:, pl.ds(spot, quarter)],
                semaphores.at[index],
            )
        )
    for copy in copies:
        copy.start()
    fetch = pltpu.make_async_copy(piece.at[pl.ds(7 * quarter // 2, quarter)], far, semaphores.at[4])
    fetch.start()

    def partial(row):
        near_part = lax.dot_general(
            mixed[row], mixing[...], CONTRACT_FIRST, preferred_element_type=F32
        )
        return near_part + lax.dot_general(
            got[row], far[...], CONTRACT_FIRST, preferred_element_type=F32
        )

    fetch.wait()
    for line in range(lines):
        sent[line] = partial((1 - core) * lines + line).astype(BF16)
    for copy in copies:
        copy.wait()
    for line in range(lines):
        kept[line] = partial(core * lines + line) + stream[line].astype(F32).T


def project(mixed, got, mixing, piece, pieces, me):
    half, quarter, sites = mixed.shape
    lines, model = half // 2, mixing.shape[1]
    out = (lines, sites, model)
    return pl.pallas_call(
        project_kernel,
        out_shape=(jax.ShapeDtypeStruct(out, F32), jax.ShapeDtypeStruct(out, BF16)),
        in_specs=[IN_SMEM] + [IN_VMEM] * 3 + [IN_HBM] * 5,
        out_specs=(IN_VMEM, IN_VMEM),
        scratch_shapes=[
            pltpu.VMEM((lines, model, sites), BF16),
            pltpu.VMEM((quarter, model), BF16),
            pltpu.SemaphoreType.DMA((5,)),
        ],
        compiler_params=GRANT,
        name="project",
    )(me, mixed, got, mixing, piece, *pieces)


def settle_kernel(kept, got, out):
    lines, sites, model = kept.shape
    chips = out.shape[0]
    parts = []
    for line in range(lines):
        total = kept[line] + got[line].astype(F32)
        parts.append(total.reshape(chips, sites // chips, model))
    out[...] = jnp.concatenate(parts, axis=1).astype(BF16)


def settle(kept, got, chips):
    lines, sites, model = kept.shape
    place = sites // chips
    if place % 8 == 0:
        return pl.pallas_call(
            settle_kernel,
            out_shape=jax.ShapeDtypeStruct((chips, lines * place, model), BF16),
            in_specs=[IN_VMEM, IN_VMEM],
            out_specs=IN_VMEM,
            compiler_params=GRANT,
            name="settle",
        )(kept, got)
    total = (kept + got.astype(F32)).astype(BF16).reshape(lines, chips, place, model)
    return jnp.transpose(total, (1, 0, 2, 3)).reshape(chips, lines * place, model)


def arrive_kernel(blocks, normed, stream, tokens):
    chips, count, model = blocks.shape
    places, rows, _ = normed.shape
    lanes = tokens.shape[-1]
    flat = blocks[...].reshape(chips * count, model).astype(F32)
    for index in range(tokens.shape[0]):
        tokens[index] = flat[:, index * lanes : (index + 1) * lanes]
    for place in range(places):
        values = [
            tokens[index, pl.ds(place, rows, stride=places), :] for index in range(tokens.shape[0])
        ]
        values = jnp.concatenate(values, axis=-1)
        stream[place] = values.astype(BF16)
        centred = values - jnp.mean(values, axis=-1, keepdims=True)
        variance = jnp.mean(centred * centred, axis=-1, keepdims=True)
        normed[place] = (centred * lax.rsqrt(variance + 1e-05)).astype(BF16)


def arrive(blocks, place):
    chips, count, model = blocks.shape
    rows = chips * count // place
    if place % 8 == 0:
        shape = jax.ShapeDtypeStruct((place, rows, model), BF16)
        return pl.pallas_call(
            arrive_kernel,
            out_shape=(shape, shape),
            in_specs=[IN_VMEM],
            out_specs=(IN_VMEM, IN_VMEM),
            scratch_shapes=[pltpu.VMEM((model // 128, chips * count, 128), F32)],
            compiler_params=GRANT,
            name="arrive",
        )(blocks)
    stream = jnp.transpose(blocks.reshape(rows, place, model), (1, 0, 2))
    return own_norm(stream, -1), stream


def column_kernel(
    lines, me_ref, starts_ref, own, other, triple, mixing, piece, pair_rest, plane_rest,
    kept, sent, normed, near, far, projected, mixed, semaphores,
):
    quarter = mixing.shape[0]
    eighth = quarter // 2
    core, pair, plane = me_ref[2], me_ref[3], me_ref[4]

    def rows_of(ref, start):
        return ref.at[pl.ds(start, quarter)]

    def spot(index):
        return pl.multiple_of(index * quarter, quarter)

    moves = (
        (triple, near.at[pl.ds(0, 3 * quarter)]),
        (mixing, near.at[pl.ds(3 * quarter, quarter)]),
        (rows_of(piece, 5 * eighth), rows_of(far, spot(pair))),
        (rows_of(piece, 9 * eighth), rows_of(far, spot(2 + plane))),
        (rows_of(pair_rest, eighth), rows_of(far, spot(1 - pair))),
        (rows_of(plane_rest, 0), rows_of(far, spot(3 - plane))),
    )
    copies = [
        pltpu.make_async_copy(source, target, semaphores.at[index])
        for index, (source, target) in enumerate(moves)
    ]
    for copy in copies:
        copy.start()
    places, rows, model = own.shape
    both = 2 * rows
    normed[:, :rows] = own[...]
    normed[:, rows:] = other[...]
    flat = normed[...].reshape(places * both, model)

    def families(axis):
        shape = (both, 1) if axis == 0 else (1, both)
        index = lax.broadcasted_iota(jnp.int32, shape, axis)
        line = jnp.where(index < rows, core * lines, (1 - core) * lines)
        index = jnp.where(index < rows, index, index - rows)
        line += index // lines * (2 * lines) + index % lines
        return sum(
            (line >= starts_ref[family]).astype(jnp.int32)
            for family in range(1, starts_ref.shape[0] - 1)
        )

    same = families(0) == families(1)
    scale = HEAD_SIZE**-0.5

    def attend(weights, lower):
        projected[...] = lax.dot_general(
            weights, flat, CONTRACT_LAST, preferred_element_type=F32
        ).astype(BF16)
        heads = quarter // HEAD_SIZE
        jobs = [(place, head) for place in range(places) for head in range(heads)]
        group = min(len(jobs), max(1, 12 * 128 // both))
        for first in range(0, len(jobs), group):
            batch = jobs[first : first + group]
            scores = []
            for place, head in batch:
                lanes = slice(place * both, (place + 1) * both)
                features = slice(head * HEAD_SIZE, (head + 1) * HEAD_SIZE)
                queries = projected[:quarter, lanes][features]
                keys = projected[quarter : 2 * quarter, lanes][features]
                scores.append(
                    lax.dot_general(keys, queries, CONTRACT_FIRST, preferred_element_type=F32)
                )
            scores = [jnp.where(same, part * scale, -jnp.inf) for part in scores]
            scores = [jnp.exp(part - jnp.max(part, axis=0, keepdims=True)) for part in scores]
            totals = [jnp.sum(part, axis=0, keepdims=True) for part in scores]
            scores = [part.astype(BF16) for part in scores]
            results = []
            for (place, head), part in zip(batch, scores):
                lanes = slice(place * both, (place + 1) * both)
                features = slice(head * HEAD_SIZE, (head + 1) * HEAD_SIZE)
                values = projected[2 * quarter :, lanes][features]
                results.append(jnp.dot(values, part, preferred_element_type=F32))
            for (place, head), part, total in zip(batch, results, totals):
                lanes = slice(place * both, (place + 1) * both)
                target = slice(lower + head * HEAD_SIZE, lower + (head + 1) * HEAD_SIZE)
                mixed[target, lanes] = (part / total).astype(BF16)

    copies[0].wait()
    attend(near[: 3 * quarter], 0)
    for copy in copies[1:]:
        copy.wait()
    attend(far[: 3 * quarter], quarter)
    for place in range(places):
        lanes = slice(place * both, (place + 1) * both)
        partial = lax.dot_general(
            mixed[:quarter, lanes], near[3 * quarter :], CONTRACT_FIRST, preferred_element_type=F32
        )
        partial += lax.dot_general(
            mixed[quarter:, lanes], far[3 * quarter :], CONTRACT_FIRST, preferred_element_type=F32
        )
        kept[place] = partial[:rows]
        sent[place] = partial[rows:].astype(BF16)


def column(own, other, triple, mixing, piece, pair_rest, plane_rest, plan, lines):
    places, rows, model = own.shape
    quarter = mixing.shape[0]
    tokens = 2 * places * rows
    return pl.pallas_call(
        functools.partial(column_kernel, lines),
        out_shape=(
            jax.ShapeDtypeStruct(own.shape, F32),
            jax.ShapeDtypeStruct(own.shape, BF16),
        ),
        in_specs=[IN_SMEM] * 2 + [IN_VMEM] * 2 + [IN_HBM] * 5,
        out_specs=(IN_VMEM, IN_VMEM),
        scratch_shapes=[
            pltpu.VMEM((places, 2 * rows, model), BF16),
            pltpu.VMEM((4 * quarter, model), BF16),
            pltpu.VMEM((4 * quarter, model), BF16),
            pltpu.VMEM((3 * quarter, tokens), BF16),
            pltpu.VMEM((2 * quarter, tokens), BF16),
            pltpu.SemaphoreType.DMA((6,)),
        ],
        compiler_params=GRANT,
        name="column",
    )(plan[0], plan[2], own, other, triple.reshape(-1, model), mixing, piece, pair_rest, plane_rest)


def finish_kernel(stream, kept, got, out):
    places, rows, model = stream.shape
    parts, wide = out.shape[1] // 3, out.shape[2]
    quarter = wide // 2 * 3
    heads = model // quarter
    groups = out.shape[0] // heads
    lines = rows // groups
    for group in range(groups):
        these = slice(group * lines, (group + 1) * lines)
        total = stream[:, these].astype(F32) + kept[:, these] + got[:, these].astype(F32)
        total = total.reshape(places * lines, model)
        for head in range(heads):
            block = total[:, head * quarter : (head + 1) * quarter]
            narrow = jnp.concatenate([block[:parts, wide:], block[parts:, wide:]], axis=1)
            block = jnp.concatenate([block[:, :wide], narrow], axis=0)
            out[group * heads + head] = block.astype(BF16)


def finish(stream, kept, got, groups, quarter):
    places, rows, model = stream.shape
    heads, lines = model // quarter, rows // groups
    parts, wide = places * lines // 2, quarter // 3 * 2
    shape = (groups * heads, 3 * parts, wide)
    if parts % 16 == 0 and lines % 8 == 0:
        return pl.pallas_call(
            finish_kernel,
            out_shape=jax.ShapeDtypeStruct(shape, BF16),
            in_specs=[IN_VMEM] * 3,
            out_specs=IN_VMEM,
            compiler_params=GRANT,
            name="finish",
        )(stream, kept, got)
    total = (stream.astype(F32) + kept + got.astype(F32)).astype(BF16)
    total = total.reshape(places, groups, lines, heads, quarter)
    total = jnp.transpose(total, (1, 3, 0, 2, 4)).reshape(-1, places * lines, quarter)
    narrow = jnp.concatenate([total[:, :parts, wide:], total[:, parts:, wide:]], axis=2)
    return jnp.concatenate([total[:, :, :wide], narrow], axis=1)


def feed_forward_kernel(
    me_ref, normed, expand, contract, piece, pair_rest, column_rest, plane_rest, late, out,
    near_expand, near_contract, far_expand, far_contract, hidden, semaphores,
):
    width = near_expand.shape[1]
    quarter = late.shape[0] // 2
    pair, plane = me_ref[3], me_ref[4]
    eighth = quarter // 2

    def move(source, start, count, target, place, index):
        return pltpu.make_async_copy(
            source.at[pl.ds(start, count)], target.at[pl.ds(place, count)], semaphores.at[index]
        )

    def own_weights():
        return [
            move(expand, 0, width, near_expand, 0, 0),
            move(contract, 0, width, near_contract, 0, 1),
            move(late, 0, quarter, far_expand, 3 * quarter, 2),
            move(late, quarter, quarter, far_contract, 3 * quarter, 3),
        ]

    def by_pair(first, second):
        return [
            move(piece, 0, 5 * eighth, first, 0, 4),
            move(pair_rest, 0, 4 * eighth, second, 0, 5),
            move(column_rest, 0, eighth, second, 4 * eighth, 8),
        ]

    def by_plane(first, second):
        return [
            move(piece, 11 * eighth, eighth, first, 5 * eighth, 6),
            move(plane_rest, 2 * eighth, eighth, second, 5 * eighth, 7),
        ]

    for copy in own_weights():
        copy.start()
    for index, moves in ((pair, by_pair), (plane, by_plane)):

        @pl.when(index == 0)
        def _(moves=moves):
            for copy in moves(far_expand, far_contract):
                copy.start()

        @pl.when(index != 0)
        def _(moves=moves):
            for copy in moves(far_contract, far_expand):
                copy.start()

    tile = width // 3
    values = normed[...]

    def raise_by(weights, lower):
        for start in range(0, width, tile):
            up = jnp.dot(values, weights[:, start : start + tile], preferred_element_type=F32)
            up = 0.5 * up * (1.0 + lax.erf(up * 2.0**-0.5))
            hidden[:, lower + start : lower + start + tile] = up.astype(BF16)

    copies = own_weights() + by_pair(far_expand, far_contract) + by_plane(far_expand, far_contract)
    copies[0].wait()
    raise_by(near_expand, 0)
    for copy in copies[1:]:
        copy.wait()
    raise_by(far_expand, width)
    down = jnp.dot(hidden[:, :width], near_contract[...], preferred_element_type=F32)
    down += jnp.dot(hidden[:, width:], far_contract[...], preferred_element_type=F32)
    out[...] = down.astype(out.dtype)


def feed_forward(normed, expand, contract, pieces, me, kind):
    places, rows, model = normed.shape
    tokens, width = places * rows, expand.shape[1]
    result = pl.pallas_call(
        feed_forward_kernel,
        out_shape=jax.ShapeDtypeStruct((tokens, model), kind),
        in_specs=[IN_SMEM, IN_VMEM] + [IN_HBM] * 7,
        out_specs=IN_VMEM,
        scratch_shapes=[
            pltpu.VMEM((model, width), BF16),
            pltpu.VMEM((width, model), BF16),
            pltpu.VMEM((model, width), BF16),
            pltpu.VMEM((model, width), BF16),
            pltpu.VMEM((tokens, 2 * width), BF16),
            pltpu.SemaphoreType.DMA((9,)),
        ],
        compiler_params=GRANT,
        name="feed_forward",
    )(me, normed.reshape(tokens, model), expand, contract, *pieces)
    return result.reshape(normed.shape)


def core_sum(stream, kept, sent):
    return (stream.astype(F32) + kept + other_core(sent).astype(F32)).astype(BF16)


def shards(
    alignment_embedding,
    line_group_label,
    group_site_tally,
    horizontal_triple_matrix,
    horizontal_mixing_matrix,
    vertical_triple_matrix,
    vertical_mixing_matrix,
    expand_matrix,
    contract_matrix,
):
    lines, quarter, sites = alignment_embedding.shape
    row_groups = lax.axis_size(ROWS)
    own = lines // 4
    chips = 2 * row_groups
    place = sites // chips
    pair = lax.axis_index("pair")
    chip = lax.axis_index("chip")
    core = lax.axis_index("core")
    label = line_group_label
    tally = group_site_tally
    families = tally.shape[0]

    starts = jnp.sum(label[:, None] < jnp.arange(families + 1), axis=0, dtype=jnp.int32)
    plane = lax.axis_index("plane")
    me = jnp.stack([lax.axis_index(ROWS), chip, core, pair, plane]).astype(jnp.int32)

    across = other_chip(alignment_embedding)
    near = other_core(alignment_embedding)
    width, eighth = expand_matrix.shape[0], quarter // 2
    column_pack = jnp.concatenate(
        [
            vertical_triple_matrix.reshape(-1, vertical_triple_matrix.shape[-1]),
            vertical_mixing_matrix,
        ]
    )
    feed = jnp.stack([expand_matrix, contract_matrix])

    def chosen(options, index):
        return lax.dynamic_index_in_dim(options, index, 0, False)

    quarters = column_pack.reshape(4, quarter, -1)
    pack = jnp.concatenate(
        [
            chosen(feed[:, : 5 * eighth], pair),
            chosen(quarters, pair),
            horizontal_mixing_matrix,
            chosen(quarters, 2 + plane),
            chosen(feed[:, 5 * eighth : 6 * eighth], plane),
        ]
    )
    late_pack = feed[:, 6 * eighth :].reshape(2 * (width - 6 * eighth), -1)
    across, near, pack, late_pack, starts, me = lax.optimization_barrier(
        (across, near, pack, late_pack, starts, me)
    )
    plan = (me, label, starts, tally)
    streams = (alignment_embedding, near, across, other_core(across))
    piece = other_chip(pack)

    shared, inner_weights, values = row_front(
        streams,
        horizontal_triple_matrix,
        plan,
        2 + max(min(families, lines) - 2, 1),
        row_groups,
    )
    parts = lax.all_to_all(shared, ROWS, 0, 0, tiled=True)
    shared = lax.all_to_all(tie(parts, plan), ROWS, 0, 0, tiled=True)
    mixed, sent = mix(shared, inner_weights, values, plan)
    sent, piece, late_pack = lax.optimization_barrier((sent, piece, late_pack))
    column_rest = other_pair(piece[4 * eighth : 7 * eighth])
    plane_rest = other_plane(piece[9 * eighth :])
    feed_rest = other_pair(piece[: 4 * eighth])
    late_piece = other_chip(late_pack)

    got, column_rest, plane_rest = lax.optimization_barrier(
        (other_chip(sent), column_rest, plane_rest)
    )
    kept, sent = project(
        mixed,
        got,
        horizontal_mixing_matrix,
        piece,
        streams,
        me,
    )

    blocks = settle(kept, other_core(sent), chips)
    blocks = lax.all_to_all(blocks, ROWS + ("chip",), 0, 0, tiled=True)
    normed, after_row = arrive(blocks, place)
    normed, feed_rest, late_piece = lax.optimization_barrier((normed, feed_rest, late_piece))
    kept, sent = column(
        normed,
        other_core(normed),
        vertical_triple_matrix,
        vertical_mixing_matrix,
        piece,
        column_rest,
        plane_rest,
        plan,
        lines // 4,
    )
    after_col = core_sum(after_row, kept, sent)

    normed = own_norm(after_col, -1)
    pieces = (piece, feed_rest, column_rest, plane_rest, late_piece)
    weights = (expand_matrix, contract_matrix, pieces, me)
    kept = feed_forward(normed, *weights, F32)
    sent = feed_forward(other_core(normed), *weights, BF16)
    blocks = finish(after_col, kept, other_core(sent), row_groups, quarter)

    blocks = lax.all_to_all(blocks, ROWS + ("chip", "core"), 0, 0, tiled=True)
    parts, wide = 2 * own * place // 2, quarter // 3 * 2
    narrow = blocks[:, 2 * parts :]
    narrow = jnp.concatenate([narrow[:, :, : wide // 2], narrow[:, :, wide // 2 :]], axis=1)
    finished = jnp.concatenate([blocks[:, : 2 * parts], narrow], axis=2)
    finished = finished.reshape(chips, 2, place, 2, own, quarter)
    finished = jnp.transpose(finished, (3, 1, 4, 5, 0, 2))
    return finished.reshape(lines, quarter, sites)


def solution(mesh):
    far = mesh.shape["rows"] // 4
    split = Mesh(mesh.devices.reshape(far, 2, 2, 2, 2), ROWS + ("chip", "core"))
    heads = ("chip", "core")
    placed = (
        P(ROWS, heads, None),
        P(),
        P(),
        P(None, heads, None),
        P(heads, None),
        P(None, heads, None),
        P(heads, None),
        P(None, heads),
        P(heads, None),
    )
    return jax.shard_map(
        shards, mesh=split, in_specs=placed, out_specs=P(ROWS, heads, None), check_vma=False
    )
```

```python
import functools

import jax
import jax.numpy as jnp
from jax import lax
from jax.experimental import pallas as pl
from jax.experimental.pallas import tpu as pltpu
from jax.sharding import Mesh, PartitionSpec as P

HEAD_SIZE = 64
SWAP = [(0, 1), (1, 0)]
ROWS = ("plane", "pair")
BF16 = jnp.bfloat16
F32 = jnp.float32


def other_chip(value):
    return lax.ppermute(value, "chip", SWAP)


def other_pair(value):
    return lax.ppermute(value, "pair", SWAP)


def other_core(value):
    return lax.ppermute(value, "core", SWAP)


def in_order(first, second, index, axis):
    forward = jnp.concatenate([first, second], axis=axis)
    backward = jnp.concatenate([second, first], axis=axis)
    return jnp.where(index == 0, forward, backward)


def half_rows(value, index):
    rows = value.shape[0] // 2
    return lax.dynamic_slice_in_dim(value, index * rows, rows)


def own_norm(values, axis):
    values = values.astype(F32)
    average = jnp.mean(values, axis=axis, keepdims=True)
    centred = values - average
    variance = jnp.mean(centred * centred, axis=axis, keepdims=True)
    return (centred * lax.rsqrt(variance + 1e-05)).astype(BF16)


def masked_softmax(tables, tally):
    live = jnp.arange(tables.shape[-1])[None, :] < tally[:, None]
    tables = jnp.where(live[:, None, None, :], tables, -jnp.inf)
    return jax.nn.softmax(tables, axis=-1).astype(BF16)


CONTRACT_FIRST = (((0,), (0,)), ((), ()))
CONTRACT_LAST = (((1,), (1,)), ((), ()))
IN_VMEM = pl.BlockSpec(memory_space=pltpu.VMEM)
IN_SMEM = pl.BlockSpec(memory_space=pltpu.SMEM)
IN_HBM = pl.BlockSpec(memory_space=pltpu.HBM)
GRANT = pltpu.CompilerParams(vmem_limit_bytes=40 * 2**20)


def slot_of(label_ref, start, lines, line):
    first, last = label_ref[start], label_ref[start + lines - 1]
    family = label_ref[start + line]
    return jnp.where(family == first, 0, jnp.where(family == last, 1, family - first + 1))


def quarter_spots(me_ref):
    chip, core = me_ref[1], me_ref[2]
    return (
        2 * chip + core, 2 * chip + 1 - core, 2 * (1 - chip) + core, 2 * (1 - chip) + 1 - core
    )


def pack_kernel(me_ref, mixing, triple, vertical, expand, contract, pack, late, semaphores):
    quarter = mixing.shape[0]
    half, pair = 2 * quarter, me_ref[3]

    def move(index, source, start, count, target, place):
        return pltpu.make_async_copy(
            source.at[pl.ds(start, count)], target.at[pl.ds(place, count)], semaphores.at[index]
        )

    fixed = [
        move(0, mixing, 0, quarter, pack, 2 * half),
        move(1, expand, half, half, late, 0),
        move(2, contract, half, half, late, half),
    ]
    options = (
        [
            move(3, expand, 0, half, pack, 0),
            move(4, triple, 0, quarter, pack, half),
            move(5, triple, quarter, quarter, pack, half + quarter),
        ],
        [
            move(3, contract, 0, half, pack, 0),
            move(4, triple, half, quarter, pack, half),
            move(5, vertical, 0, quarter, pack, half + quarter),
        ],
    )
    for copy in fixed:
        copy.start()
    for index, copies in enumerate(options):

        @pl.when(pair == index)
        def _(copies=copies):
            for copy in copies:
                copy.start()

    for copy in fixed + options[0]:
        copy.wait()


def pack_weights(me, mixing, triple, vertical, expand, contract):
    quarter, model = mixing.shape
    return pl.pallas_call(
        pack_kernel,
        out_shape=(
            jax.ShapeDtypeStruct((5 * quarter, model), BF16),
            jax.ShapeDtypeStruct((4 * quarter, model), BF16),
        ),
        in_specs=[IN_SMEM] + [IN_HBM] * 5,
        out_specs=(IN_HBM, IN_HBM),
        scratch_shapes=[pltpu.SemaphoreType.DMA((6,))],
        compiler_params=GRANT,
        name="pack",
    )(me, mixing, triple.reshape(-1, model), vertical, expand, contract)


def spread_kernel(stream, out):
    lines, quarter, sites = stream.shape
    chips = out.shape[0] // 2
    place, own = sites // chips, lines // 2
    wide = out.shape[2]
    for core in range(2):
        values = [stream[core * own + line].astype(F32).T for line in range(own)]
        values = [value.reshape(chips, place, quarter) for value in values]
        values = jnp.concatenate(values, axis=1)
        parts = own * place // 2
        narrow = jnp.concatenate([values[:, :parts, wide:], values[:, parts:, wide:]], axis=2)
        values = jnp.concatenate([values[:, :, :wide], narrow], axis=1).astype(BF16)
        for chip in range(chips):
            out[2 * chip + core] = values[chip]


def spread(stream, chips):
    lines, quarter, sites = stream.shape
    place, own = sites // chips, lines // 2
    if place % 8 == 0:
        shape = (2 * chips, 3 * own * place // 2, quarter // 3 * 2)
        return pl.pallas_call(
            spread_kernel,
            out_shape=jax.ShapeDtypeStruct(shape, BF16),
            in_specs=[IN_VMEM],
            out_specs=IN_VMEM,
            compiler_params=GRANT,
            name="spread",
        )(stream)
    stream = jnp.transpose(stream.reshape(2, own, quarter, chips, place), (3, 0, 1, 4, 2))
    return stream.reshape(2 * chips, own * place, quarter)


def row_front_kernel(
    lines, me_ref, label_ref, starts_ref, tally_ref, own, near, far, diagonal, triple,
    table_ref, inner_ref, value_ref, tables, normed,
):
    step = pl.program_id(0)
    group, quarter, sites = own.shape
    heads = quarter // HEAD_SIZE

    @pl.when(step == 0)
    def _():
        tables[...] = jnp.zeros_like(tables)

    pieces = []
    for ref in (own, near, far, diagonal):
        lanes = jnp.concatenate([ref[line] for line in range(group)], axis=-1)
        pieces.append(lanes.astype(F32))
    size = 4 * quarter
    average = sum(jnp.sum(piece, axis=0, keepdims=True) for piece in pieces) / size
    pieces = [piece - average for piece in pieces]
    variance = sum(jnp.sum(piece * piece, axis=0, keepdims=True) for piece in pieces) / size
    inverse = lax.rsqrt(variance + 1e-05)
    for spot, piece in zip(quarter_spots(me_ref), pieces):
        spot = pl.multiple_of(spot * quarter, quarter)
        normed[pl.ds(spot, quarter), :] = (piece * inverse).astype(BF16)
    projected = jnp.dot(triple[...], normed[...], preferred_element_type=F32).astype(BF16)
    base = me_ref[0] * lines
    jobs = []
    for line in range(group):
        part = projected[:, line * sites : (line + 1) * sites]
        value_ref[line] = part[2 * quarter :]
        place = step * group + line
        slot = slot_of(label_ref, base, lines, place)
        family = label_ref[base + place]
        members = jnp.full((1, sites), starts_ref[family + 1] - starts_ref[family], jnp.int32)
        scale = HEAD_SIZE**-0.5 * lax.rsqrt(members.astype(F32))
        for head in range(heads):
            lower = head * HEAD_SIZE
            queries = part[lower : lower + HEAD_SIZE]
            keys = part[quarter + lower : quarter + lower + HEAD_SIZE]
            logits = lax.dot_general(queries, keys, CONTRACT_FIRST, preferred_element_type=F32)
            jobs.append((slot * heads + head, logits, scale))
    for index, logits, scale in jobs:
        tables[index] += logits * scale

    @pl.when(step == pl.num_programs(0) - 1)
    def _():
        for index in range(2 * heads):
            table = tables[index].astype(BF16)
            if len(table_ref.shape) == 4:
                groups, _, rows, _ = table_ref.shape
                table_ref[:, index] = table.reshape(groups, rows, sites)
            else:
                table_ref[index] = table
        site = lax.broadcasted_iota(jnp.int32, (sites, sites), 1)

        def inner(index, carry):
            table = tables[2 * heads + index]
            family = label_ref[base] + 1 + index // heads
            family = jnp.minimum(family, tally_ref.shape[0] - 1)
            table = jnp.where(site < tally_ref[family], table, -jnp.inf)
            table = jnp.exp(table - jnp.max(table, axis=-1, keepdims=True))
            table = table / jnp.sum(table, axis=-1, keepdims=True)
            inner_ref[index] = table.astype(BF16)
            return carry

        lax.fori_loop(0, inner_ref.shape[0], inner, 0)


def row_front(pieces, triple, plan, slots, row_groups):
    lines, quarter, sites = pieces[0].shape
    group = 4
    heads = quarter // HEAD_SIZE
    inner = slots - 2
    rows = sites // row_groups
    shape = (row_groups, 2 * heads, rows, sites) if rows % 16 == 0 else (2 * heads, sites, sites)
    block = pl.BlockSpec((group, quarter, sites), lambda step: (step, 0, 0))

    def whole(shape):
        return pl.BlockSpec(shape, lambda step: (0,) * len(shape))

    tables, inner_weights, values = pl.pallas_call(
        functools.partial(row_front_kernel, lines),
        grid=(lines // group,),
        out_shape=(
            jax.ShapeDtypeStruct(shape, BF16),
            jax.ShapeDtypeStruct((inner * heads, sites, sites), BF16),
            jax.ShapeDtypeStruct((lines, quarter, sites), BF16),
        ),
        in_specs=[IN_SMEM] * 4 + [block] * 4 + [whole((3 * quarter, 4 * quarter))],
        out_specs=(whole(shape), whole((inner * heads, sites, sites)), block),
        scratch_shapes=[
            pltpu.VMEM((slots * heads, sites, sites), F32),
            pltpu.VMEM((4 * quarter, group * sites), BF16),
        ],
        compiler_params=GRANT,
        name="row_front",
    )(*plan, *pieces, triple.reshape(3 * quarter, 4 * quarter))
    if rows % 16:
        tables = jnp.transpose(tables.reshape(-1, row_groups, rows, sites), (1, 0, 2, 3))
    return tables, inner_weights, values


def tie_kernel(me_ref, label_ref, starts_ref, tally_ref, parts, out, weights):
    groups, pairs, rows, sites = parts.shape
    lines = label_ref.shape[0] // groups
    ends = [label_ref[g * lines + e * (lines - 1)] for g in range(groups) for e in range(2)]
    heads = pairs // 2
    site = lax.broadcasted_iota(jnp.int32, (heads, rows, sites), 2)
    for family in range(weights.shape[0]):
        total = jnp.zeros((heads, rows, sites), F32)
        for group in range(groups):
            for end in range(2):
                part = parts[group, end * heads : (end + 1) * heads].astype(F32)
                total += jnp.where(ends[2 * group + end] == family, part, 0.0)
        total = jnp.where(site < tally_ref[family], total, -jnp.inf)
        total = jnp.exp(total - jnp.max(total, axis=-1, keepdims=True))
        total = total / jnp.sum(total, axis=-1, keepdims=True)
        weights[family] = total.astype(BF16)
    for group in range(groups):
        for end in range(2):
            chosen = weights[ends[2 * group + end]]
            out[group, end * heads : (end + 1) * heads] = chosen


def tie(parts, plan):
    groups, pairs, rows, sites = parts.shape
    _, label, _, tally = plan
    if rows % 16 == 0:
        return pl.pallas_call(
            tie_kernel,
            out_shape=jax.ShapeDtypeStruct(parts.shape, BF16),
            in_specs=[IN_SMEM] * 4 + [IN_VMEM],
            out_specs=IN_VMEM,
            scratch_shapes=[pltpu.VMEM((tally.shape[0], pairs // 2, rows, sites), BF16)],
            compiler_params=GRANT,
            name="tie",
        )(*plan, parts)
    ends = jnp.stack([label.reshape(groups, -1)[:, 0], label.reshape(groups, -1)[:, -1]], axis=1)
    parts = parts.astype(F32).reshape(groups, 2, -1, rows, sites)
    member = (ends[:, :, None] == jnp.arange(tally.shape[0])).astype(F32)
    totals = jnp.einsum("stf,sthij->fhij", member, parts, precision=lax.Precision.HIGHEST)
    return masked_softmax(totals, tally)[ends].reshape(groups, pairs, rows, sites)


def mix_kernel(me_ref, label_ref, starts_ref, tally_ref, shared, inner, values, out, weights):
    heads, sites = shared.shape[1] // 2, values.shape[2]
    lines, chips = values.shape[0], out.shape[0]
    place = sites // chips
    for index in range(2 * heads):
        weights[index] = shared[:, index].reshape(sites, sites)
    weights[2 * heads :] = inner[...]
    mixed = []
    for line in range(lines):
        slot = slot_of(label_ref, me_ref[0] * lines, lines, line)
        value = values[line]
        mixed.append(
            [
                lax.dot_general(
                    weights[slot * heads + head],
                    value[head * HEAD_SIZE : (head + 1) * HEAD_SIZE],
                    CONTRACT_LAST,
                    preferred_element_type=F32,
                )
                for head in range(heads)
            ]
        )
    pairs = [(part[0], part[1]) for part in mixed]
    pairs += [(mixed[line][2], mixed[line + lines // 2][2]) for line in range(lines // 2)]
    for index in range(0, len(pairs), 2):
        block = [
            jnp.concatenate(pair, axis=1).reshape(chips, place, 2 * HEAD_SIZE)
            for pair in pairs[index : index + 2]
        ]
        out[:, index * place : (index + 2) * place] = jnp.concatenate(block, axis=1).astype(BF16)


def mix(shared, inner, values, plan, chips):
    groups, pairs, rows, sites = shared.shape
    lines, quarter, _ = values.shape
    place = sites // chips
    if rows % 16 == 0 and place % 8 == 0:
        shape = (chips, 3 * lines * place // 2, 2 * HEAD_SIZE)
        return pl.pallas_call(
            mix_kernel,
            out_shape=jax.ShapeDtypeStruct(shape, BF16),
            in_specs=[IN_SMEM] * 4 + [IN_VMEM] * 3,
            out_specs=IN_VMEM,
            scratch_shapes=[pltpu.VMEM((pairs + inner.shape[0], sites, sites), BF16)],
            compiler_params=GRANT,
            name="mix",
        )(*plan, shared, inner, values)
    me, label = plan[:2]
    label = lax.dynamic_slice_in_dim(label, me[0] * lines, lines)
    slot = slot_of(label, 0, lines, jnp.arange(lines))
    ends = jnp.transpose(shared, (1, 0, 2, 3)).reshape(2, pairs // 2, sites, sites)
    weights = jnp.concatenate([ends, inner.reshape(-1, *ends.shape[1:])])[slot]
    values = values.reshape(lines, -1, HEAD_SIZE, sites)
    mixed = jnp.einsum("rhdj,rhij->rihd", values, weights, preferred_element_type=F32)
    mixed = mixed.astype(BF16).reshape(lines, chips, place, quarter)
    return jnp.transpose(mixed, (1, 0, 2, 3)).reshape(chips, lines * place, quarter)


def project_kernel(me_ref, blocks, mixing, piece, kept, sent, wide, first, second, semaphores):
    chips, count, lanes = blocks.shape
    quarter, model = mixing.shape
    tokens = count * 2 // 3
    groups, own = chips // 2, tokens // 2
    chip, core = me_ref[1], me_ref[2]
    start = piece.shape[0] - quarter
    tail = quarter - lanes
    first[...] = jnp.zeros_like(first)
    second[...] = jnp.zeros_like(second)
    copies = []
    for index, (source, place, side) in enumerate(((mixing, 0, chip), (piece, start, 1 - chip))):
        spot = pl.multiple_of(side * lanes, lanes)
        end = source.at[pl.ds(place + lanes, tail)]
        moves = (
            (source.at[pl.ds(place, lanes)], wide.at[pl.ds(spot, lanes)]),
            (end, first.at[pl.ds(spot, tail)]),
            (end, second.at[pl.ds(pl.multiple_of(spot + tail, tail), tail)]),
        )
        for number, (origin, target) in enumerate(moves):
            copies.append(
                pltpu.make_async_copy(origin, target, semaphores.at[3 * index + number])
            )
    for copy in copies:
        copy.start()
    values = blocks[...].reshape(groups, 2, count, lanes)
    values = jnp.concatenate([values[:, 0], values[:, 1]], axis=-1)
    whole = values[:, :tokens].reshape(groups * tokens, 2 * lanes)
    narrow = values[:, tokens:].reshape(groups * own, 2 * lanes)
    for copy in copies:
        copy.wait()
    total = jnp.dot(whole, wide[...], preferred_element_type=F32)
    total = total.reshape(groups, tokens, model)
    ends = [
        jnp.dot(narrow, weights[...], preferred_element_type=F32).reshape(groups, own, model)
        for weights in (first, second)
    ]
    halves = [total[:, :own] + ends[0], total[:, own:] + ends[1]]
    for index in range(2):

        @pl.when(core == index)
        def _(index=index):
            kept[...] = halves[index]
            sent[...] = halves[1 - index].astype(BF16)


def project(blocks, mixing, piece, me, lines):
    chips, count, lanes = blocks.shape
    quarter, model = mixing.shape
    groups = chips // 2
    if lanes != quarter:
        out = (groups, count // 3, model)
        return pl.pallas_call(
            project_kernel,
            out_shape=(jax.ShapeDtypeStruct(out, F32), jax.ShapeDtypeStruct(out, BF16)),
            in_specs=[IN_SMEM, IN_VMEM, IN_HBM, IN_HBM],
            out_specs=(IN_VMEM, IN_VMEM),
            scratch_shapes=[pltpu.VMEM((2 * lanes, model), BF16)] * 3
            + [pltpu.SemaphoreType.DMA((6,))],
            compiler_params=GRANT,
            name="project",
        )(me, blocks, mixing, piece)
    weights = in_order(mixing[None], piece[None, -quarter:], me[1], 0)
    values = blocks.reshape(groups, 2, 2, count // 2, quarter)
    partial = jnp.einsum("gxctd,xde->cgte", values, weights, preferred_element_type=F32)
    kept = lax.dynamic_index_in_dim(partial, me[2], 0, False)
    sent = lax.dynamic_index_in_dim(partial, 1 - me[2], 0, False)
    return kept, sent.astype(BF16)


def arrive_kernel(kept, got, blocks, normed, stream, tokens):
    groups, own, model = kept.shape
    places, rows, _ = normed.shape
    count, lanes = blocks.shape[1], blocks.shape[2]
    heads = blocks.shape[0] // groups
    parts = count // 3
    total = kept[...] + got[...].astype(F32)
    for group in range(groups):
        features = []
        for head in range(heads):
            block = blocks[group * heads + head].astype(F32)
            narrow = block[2 * parts :]
            narrow = jnp.concatenate([narrow[:, : lanes // 2], narrow[:, lanes // 2 :]], axis=0)
            features += [block[: 2 * parts], narrow]
        values = total[group] + jnp.concatenate(features, axis=1)
        for index in range(tokens.shape[0]):
            lower = index * tokens.shape[2]
            part = values[:, lower : lower + tokens.shape[2]]
            tokens[index, group * own : (group + 1) * own] = part
    for place in range(places):
        values = [
            tokens[index, pl.ds(place, rows, stride=places), :] for index in range(tokens.shape[0])
        ]
        values = jnp.concatenate(values, axis=-1).astype(BF16)
        stream[place] = values
        values = values.astype(F32)
        centred = values - jnp.mean(values, axis=-1, keepdims=True)
        variance = jnp.mean(centred * centred, axis=-1, keepdims=True)
        normed[place] = (centred * lax.rsqrt(variance + 1e-05)).astype(BF16)


def arrive(kept, got, blocks, place):
    groups, own, model = kept.shape
    rows = groups * own // place
    if place % 8 == 0:
        shape = jax.ShapeDtypeStruct((place, rows, model), BF16)
        return pl.pallas_call(
            arrive_kernel,
            out_shape=(shape, shape),
            in_specs=[IN_VMEM] * 3,
            out_specs=(IN_VMEM, IN_VMEM),
            scratch_shapes=[pltpu.VMEM((model // 128, groups * own, 128), F32)],
            compiler_params=GRANT,
            name="arrive",
        )(kept, got, blocks)
    heads = blocks.shape[0] // groups
    stream = jnp.transpose(blocks.reshape(groups, heads, own, -1), (0, 2, 1, 3))
    stream = stream.reshape(groups, own, model).astype(F32) + kept + got.astype(F32)
    stream = jnp.transpose(stream.reshape(rows, place, model), (1, 0, 2)).astype(BF16)
    return own_norm(stream, -1), stream


def column_kernel(
    lines, me_ref, starts_ref, own, other, triple, mixing, piece, rest,
    kept, sent, normed, near, far, projected, mixed, semaphores,
):
    quarter = mixing.shape[0]
    core, pair = me_ref[2], me_ref[3]
    half = rest.shape[0] // 2

    def spot(index):
        return far.at[pl.ds(pl.multiple_of(index * half, half), half)]

    moves = (
        (triple, near.at[pl.ds(0, 3 * quarter)]),
        (mixing, near.at[pl.ds(3 * quarter, quarter)]),
        (piece.at[pl.ds(half, half)], spot(pair)),
        (rest.at[pl.ds(half, half)], spot(1 - pair)),
    )
    copies = [
        pltpu.make_async_copy(source, target, semaphores.at[index])
        for index, (source, target) in enumerate(moves)
    ]
    for copy in copies:
        copy.start()
    places, rows, model = own.shape
    both = 2 * rows
    normed[:, :rows] = own[...]
    normed[:, rows:] = other[...]
    flat = normed[...].reshape(places * both, model)

    def families(axis):
        shape = (both, 1) if axis == 0 else (1, both)
        index = lax.broadcasted_iota(jnp.int32, shape, axis)
        line = jnp.where(index < rows, core * lines, (1 - core) * lines)
        index = jnp.where(index < rows, index, index - rows)
        line += index // lines * (2 * lines) + index % lines
        return sum(
            (line >= starts_ref[family]).astype(jnp.int32)
            for family in range(1, starts_ref.shape[0] - 1)
        )

    same = families(0) == families(1)
    scale = HEAD_SIZE**-0.5

    def attend(weights, lower):
        projected[...] = lax.dot_general(
            weights, flat, CONTRACT_LAST, preferred_element_type=F32
        ).astype(BF16)
        heads = quarter // HEAD_SIZE
        jobs = [(place, head) for place in range(places) for head in range(heads)]
        group = min(len(jobs), max(1, 12 * 128 // both))
        for first in range(0, len(jobs), group):
            batch = jobs[first : first + group]
            scores = []
            for place, head in batch:
                lanes = slice(place * both, (place + 1) * both)
                features = slice(head * HEAD_SIZE, (head + 1) * HEAD_SIZE)
                queries = projected[:quarter, lanes][features]
                keys = projected[quarter : 2 * quarter, lanes][features]
                scores.append(
                    lax.dot_general(keys, queries, CONTRACT_FIRST, preferred_element_type=F32)
                )
            scores = [jnp.where(same, part * scale, -jnp.inf) for part in scores]
            scores = [jnp.exp(part - jnp.max(part, axis=0, keepdims=True)) for part in scores]
            totals = [jnp.sum(part, axis=0, keepdims=True) for part in scores]
            scores = [part.astype(BF16) for part in scores]
            results = []
            for (place, head), part in zip(batch, scores):
                lanes = slice(place * both, (place + 1) * both)
                features = slice(head * HEAD_SIZE, (head + 1) * HEAD_SIZE)
                values = projected[2 * quarter :, lanes][features]
                results.append(jnp.dot(values, part, preferred_element_type=F32))
            for (place, head), part, total in zip(batch, results, totals):
                lanes = slice(place * both, (place + 1) * both)
                target = slice(lower + head * HEAD_SIZE, lower + (head + 1) * HEAD_SIZE)
                mixed[target, lanes] = (part / total).astype(BF16)

    copies[0].wait()
    attend(near[: 3 * quarter], 0)
    for copy in copies[1:]:
        copy.wait()
    attend(far[: 3 * quarter], quarter)
    for place in range(places):
        lanes = slice(place * both, (place + 1) * both)
        partial = lax.dot_general(
            mixed[:quarter, lanes], near[3 * quarter :], CONTRACT_FIRST, preferred_element_type=F32
        )
        partial += lax.dot_general(
            mixed[quarter:, lanes], far[3 * quarter :], CONTRACT_FIRST, preferred_element_type=F32
        )
        kept[place] = partial[:rows]
        sent[place] = partial[rows:].astype(BF16)


def column(own, other, triple, mixing, piece, rest, plan, lines):
    places, rows, model = own.shape
    quarter = mixing.shape[0]
    tokens = 2 * places * rows
    return pl.pallas_call(
        functools.partial(column_kernel, lines),
        out_shape=(
            jax.ShapeDtypeStruct(own.shape, F32),
            jax.ShapeDtypeStruct(own.shape, BF16),
        ),
        in_specs=[IN_SMEM] * 2 + [IN_VMEM] * 2 + [IN_HBM] * 4,
        out_specs=(IN_VMEM, IN_VMEM),
        scratch_shapes=[
            pltpu.VMEM((places, 2 * rows, model), BF16),
            pltpu.VMEM((4 * quarter, model), BF16),
            pltpu.VMEM((4 * quarter, model), BF16),
            pltpu.VMEM((3 * quarter, tokens), BF16),
            pltpu.VMEM((2 * quarter, tokens), BF16),
            pltpu.SemaphoreType.DMA((4,)),
        ],
        compiler_params=GRANT,
        name="column",
    )(plan[0], plan[2], own, other, triple.reshape(-1, model), mixing, piece, rest)


def finish_kernel(stream, kept, got, out):
    places, rows, model = stream.shape
    parts, wide = out.shape[1] // 3, out.shape[2]
    quarter = wide // 2 * 3
    heads = model // quarter
    groups = out.shape[0] // heads
    lines = rows // groups
    for group in range(groups):
        these = slice(group * lines, (group + 1) * lines)
        total = stream[:, these].astype(F32) + kept[:, these] + got[:, these].astype(F32)
        total = total.reshape(places * lines, model)
        for head in range(heads):
            block = total[:, head * quarter : (head + 1) * quarter]
            narrow = jnp.concatenate([block[:parts, wide:], block[parts:, wide:]], axis=1)
            block = jnp.concatenate([block[:, :wide], narrow], axis=0)
            out[group * heads + head] = block.astype(BF16)


def finish(stream, kept, got, groups, quarter):
    places, rows, model = stream.shape
    heads, lines = model // quarter, rows // groups
    parts, wide = places * lines // 2, quarter // 3 * 2
    shape = (groups * heads, 3 * parts, wide)
    if parts % 16 == 0 and lines % 8 == 0:
        return pl.pallas_call(
            finish_kernel,
            out_shape=jax.ShapeDtypeStruct(shape, BF16),
            in_specs=[IN_VMEM] * 3,
            out_specs=IN_VMEM,
            compiler_params=GRANT,
            name="finish",
        )(stream, kept, got)
    total = (stream.astype(F32) + kept + got.astype(F32)).astype(BF16)
    total = total.reshape(places, groups, lines, heads, quarter)
    total = jnp.transpose(total, (1, 3, 0, 2, 4)).reshape(-1, places * lines, quarter)
    narrow = jnp.concatenate([total[:, :parts, wide:], total[:, parts:, wide:]], axis=2)
    return jnp.concatenate([total[:, :, :wide], narrow], axis=1)


def feed_forward_kernel(
    me_ref, normed, expand, contract, piece, rest, late, out,
    near_expand, near_contract, far_expand, far_contract, hidden, semaphores,
):
    width = near_expand.shape[1]
    half, pair = rest.shape[0] // 2, me_ref[3]

    def move(source, start, count, target, place, index):
        return pltpu.make_async_copy(
            source.at[pl.ds(start, count)], target.at[pl.ds(place, count)], semaphores.at[index]
        )

    def shared(first, second):
        return [
            move(piece, 0, half, first, 0, 4),
            move(rest, 0, half, second, 0, 5),
        ]

    copies = [
        move(expand, 0, width, near_expand, 0, 0),
        move(contract, 0, width, near_contract, 0, 1),
        move(late, 0, half, far_expand, half, 2),
        move(late, half, half, far_contract, half, 3),
    ]
    for copy in copies:
        copy.start()

    @pl.when(pair == 0)
    def _():
        for copy in shared(far_expand, far_contract):
            copy.start()

    @pl.when(pair != 0)
    def _():
        for copy in shared(far_contract, far_expand):
            copy.start()

    tile = width // 3
    values = normed[...]

    def raise_by(weights, lower):
        for start in range(0, width, tile):
            up = jnp.dot(values, weights[:, start : start + tile], preferred_element_type=F32)
            up = 0.5 * up * (1.0 + lax.erf(up * 2.0**-0.5))
            hidden[:, lower + start : lower + start + tile] = up.astype(BF16)

    copies += shared(far_expand, far_contract)
    copies[0].wait()
    raise_by(near_expand, 0)
    for copy in copies[1:]:
        copy.wait()
    raise_by(far_expand, width)
    down = jnp.dot(hidden[:, :width], near_contract[...], preferred_element_type=F32)
    down += jnp.dot(hidden[:, width:], far_contract[...], preferred_element_type=F32)
    out[...] = down.astype(out.dtype)


def feed_forward(normed, expand, contract, pieces, me, kind):
    places, rows, model = normed.shape
    tokens, width = places * rows, expand.shape[1]
    result = pl.pallas_call(
        feed_forward_kernel,
        out_shape=jax.ShapeDtypeStruct((tokens, model), kind),
        in_specs=[IN_SMEM, IN_VMEM] + [IN_HBM] * 5,
        out_specs=IN_VMEM,
        scratch_shapes=[
            pltpu.VMEM((model, width), BF16),
            pltpu.VMEM((width, model), BF16),
            pltpu.VMEM((model, width), BF16),
            pltpu.VMEM((model, width), BF16),
            pltpu.VMEM((tokens, 2 * width), BF16),
            pltpu.SemaphoreType.DMA((6,)),
        ],
        compiler_params=GRANT,
        name="feed_forward",
    )(me, normed.reshape(tokens, model), expand, contract, *pieces)
    return result.reshape(normed.shape)


def core_sum(stream, kept, sent):
    return (stream.astype(F32) + kept + other_core(sent).astype(F32)).astype(BF16)


def shards(
    alignment_embedding,
    line_group_label,
    group_site_tally,
    horizontal_triple_matrix,
    horizontal_mixing_matrix,
    vertical_triple_matrix,
    vertical_mixing_matrix,
    expand_matrix,
    contract_matrix,
):
    lines, quarter, sites = alignment_embedding.shape
    row_groups = lax.axis_size(ROWS)
    own = lines // 2
    chips = 2 * row_groups
    place = sites // chips
    pair = lax.axis_index("pair")
    chip = lax.axis_index("chip")
    core = lax.axis_index("core")
    label, tally = line_group_label, group_site_tally
    families = tally.shape[0]
    starts = jnp.sum(label[:, None] < jnp.arange(families + 1), axis=0, dtype=jnp.int32)
    me = jnp.stack([lax.axis_index(ROWS), chip, core, pair]).astype(jnp.int32)

    across = other_chip(alignment_embedding)
    near = other_core(alignment_embedding)
    pack, late = pack_weights(
        me,
        horizontal_mixing_matrix,
        vertical_triple_matrix,
        vertical_mixing_matrix,
        expand_matrix,
        contract_matrix,
    )
    stream, pack, late = lax.optimization_barrier((alignment_embedding, pack, late))
    stream = spread(stream, chips)
    stream = lax.all_to_all(stream, ROWS + ("chip", "core"), 0, 0, tiled=True)
    across, near, pack, late, starts, me = lax.optimization_barrier(
        (across, near, pack, late, starts, me)
    )
    plan = (me, label, starts, tally)
    piece = other_chip(pack)

    shared, inner_weights, values = row_front(
        (alignment_embedding, near, across, other_core(across)),
        horizontal_triple_matrix,
        plan,
        2 + max(min(families, lines) - 2, 1),
        row_groups,
    )
    shared, stream = lax.optimization_barrier((shared, stream))
    parts = lax.all_to_all(shared, ROWS, 0, 0, tiled=True)
    shared = lax.all_to_all(tie(parts, plan), ROWS, 0, 0, tiled=True)
    blocks = mix(shared, inner_weights, values, plan, chips)

    blocks, piece, late = lax.optimization_barrier((blocks, piece, late))
    half = expand_matrix.shape[0] // 2
    rest = other_pair(piece[: 2 * half])
    late = other_chip(late)
    blocks = lax.all_to_all(blocks, ROWS + ("chip",), 0, 0, tiled=True)
    kept, sent = project(blocks, horizontal_mixing_matrix, piece, me, lines)
    normed, after_row = arrive(kept, other_core(sent), stream, place)
    normed, rest, late = lax.optimization_barrier((normed, rest, late))

    kept, sent = column(
        normed,
        other_core(normed),
        vertical_triple_matrix,
        vertical_mixing_matrix,
        piece,
        rest,
        plan,
        own,
    )
    after_col = core_sum(after_row, kept, sent)

    normed = own_norm(after_col, -1)
    weights = (expand_matrix, contract_matrix, (piece, rest, late), me)
    kept = feed_forward(normed, *weights, F32)
    sent = feed_forward(other_core(normed), *weights, BF16)
    blocks = finish(after_col, kept, other_core(sent), row_groups, quarter)

    blocks = lax.all_to_all(blocks, ROWS + ("chip", "core"), 0, 0, tiled=True)
    parts, wide = own * place // 2, quarter // 3 * 2
    narrow = blocks[:, 2 * parts :]
    narrow = jnp.concatenate([narrow[:, :, : wide // 2], narrow[:, :, wide // 2 :]], axis=1)
    finished = jnp.concatenate([blocks[:, : 2 * parts], narrow], axis=2)
    finished = finished.reshape(chips, 2, place, own, quarter)
    finished = jnp.transpose(finished, (1, 3, 4, 0, 2))
    return finished.reshape(lines, quarter, sites)


def solution(mesh):
    planes = mesh.shape["rows"] // 2
    split = Mesh(mesh.devices.reshape(planes, 2, 2, 2), ROWS + ("chip", "core"))
    heads = ("chip", "core")
    placed = (
        P(ROWS, heads, None),
        P(),
        P(),
        P(None, heads, None),
        P(heads, None),
        P(None, heads, None),
        P(heads, None),
        P(None, heads),
        P(heads, None),
    )
    return jax.shard_map(
        shards, mesh=split, in_specs=placed, out_specs=P(ROWS, heads, None), check_vma=False
    )
```

```python
import functools

import jax
import jax.numpy as jnp
from jax import lax
from jax.experimental import pallas as pl
from jax.experimental.pallas import tpu as pltpu
from jax.sharding import Mesh, PartitionSpec as P

HEAD_SIZE = 64
SWAP = [(0, 1), (1, 0)]
ROWS = ("plane", "pair")
BF16 = jnp.bfloat16
F32 = jnp.float32


def other_chip(value):
    return lax.ppermute(value, "chip", SWAP)


def other_pair(value):
    return lax.ppermute(value, "pair", SWAP)


def other_core(value):
    return lax.ppermute(value, "core", SWAP)


def in_order(first, second, index, axis):
    forward = jnp.concatenate([first, second], axis=axis)
    backward = jnp.concatenate([second, first], axis=axis)
    return jnp.where(index == 0, forward, backward)


def half_rows(value, index):
    rows = value.shape[0] // 2
    return lax.dynamic_slice_in_dim(value, index * rows, rows)


def own_norm(values, axis):
    values = values.astype(F32)
    average = jnp.mean(values, axis=axis, keepdims=True)
    centred = values - average
    variance = jnp.mean(centred * centred, axis=axis, keepdims=True)
    return (centred * lax.rsqrt(variance + 1e-05)).astype(BF16)


def masked_softmax(tables, tally):
    live = jnp.arange(tables.shape[-1])[None, :] < tally[:, None]
    tables = jnp.where(live[:, None, None, :], tables, -jnp.inf)
    return jax.nn.softmax(tables, axis=-1).astype(BF16)


CONTRACT_FIRST = (((0,), (0,)), ((), ()))
CONTRACT_LAST = (((1,), (1,)), ((), ()))
IN_VMEM = pl.BlockSpec(memory_space=pltpu.VMEM)
IN_SMEM = pl.BlockSpec(memory_space=pltpu.SMEM)
IN_HBM = pl.BlockSpec(memory_space=pltpu.HBM)
GRANT = pltpu.CompilerParams(vmem_limit_bytes=40 * 2**20)


def slot_of(label_ref, start, lines, line):
    first, last = label_ref[start], label_ref[start + lines - 1]
    family = label_ref[start + line]
    return jnp.where(family == first, 0, jnp.where(family == last, 1, family - first + 1))


def quarter_spots(me_ref):
    chip, core = me_ref[1], me_ref[2]
    return (
        2 * chip + core, 2 * chip + 1 - core, 2 * (1 - chip) + core, 2 * (1 - chip) + 1 - core
    )


def pack_kernel(me_ref, mixing, triple, vertical, expand, contract, pack, late, semaphores):
    quarter = mixing.shape[0]
    half, pair = 2 * quarter, me_ref[3]

    def move(index, source, start, count, target, place):
        return pltpu.make_async_copy(
            source.at[pl.ds(start, count)], target.at[pl.ds(place, count)], semaphores.at[index]
        )

    fixed = [
        move(0, mixing, 0, quarter, pack, 2 * half),
        move(1, expand, half, half, late, 0),
        move(2, contract, half, half, late, half),
    ]
    options = (
        [
            move(3, expand, 0, half, pack, 0),
            move(4, triple, 0, quarter, pack, half),
            move(5, triple, quarter, quarter, pack, half + quarter),
        ],
        [
            move(3, contract, 0, half, pack, 0),
            move(4, triple, half, quarter, pack, half),
            move(5, vertical, 0, quarter, pack, half + quarter),
        ],
    )
    for copy in fixed:
        copy.start()
    for index, copies in enumerate(options):

        @pl.when(pair == index)
        def _(copies=copies):
            for copy in copies:
                copy.start()

    for copy in fixed + options[0]:
        copy.wait()


def pack_weights(me, mixing, triple, vertical, expand, contract):
    quarter, model = mixing.shape
    return pl.pallas_call(
        pack_kernel,
        out_shape=(
            jax.ShapeDtypeStruct((5 * quarter, model), BF16),
            jax.ShapeDtypeStruct((4 * quarter, model), BF16),
        ),
        in_specs=[IN_SMEM] + [IN_HBM] * 5,
        out_specs=(IN_HBM, IN_HBM),
        scratch_shapes=[pltpu.SemaphoreType.DMA((6,))],
        compiler_params=GRANT,
        name="pack",
    )(me, mixing, triple.reshape(-1, model), vertical, expand, contract)


def spread_kernel(stream, out):
    lines, quarter, sites = stream.shape
    chips = out.shape[0] // 2
    place, own = sites // chips, lines // 2
    wide = out.shape[2]
    for core in range(2):
        values = [stream[core * own + line].astype(F32).T for line in range(own)]
        values = [value.reshape(chips, place, quarter) for value in values]
        values = jnp.concatenate(values, axis=1)
        parts = own * place // 2
        narrow = jnp.concatenate([values[:, :parts, wide:], values[:, parts:, wide:]], axis=2)
        values = jnp.concatenate([values[:, :, :wide], narrow], axis=1).astype(BF16)
        for chip in range(chips):
            out[2 * chip + core] = values[chip]


def spread(stream, chips):
    lines, quarter, sites = stream.shape
    place, own = sites // chips, lines // 2
    if place % 8 == 0:
        shape = (2 * chips, 3 * own * place // 2, quarter // 3 * 2)
        return pl.pallas_call(
            spread_kernel,
            out_shape=jax.ShapeDtypeStruct(shape, BF16),
            in_specs=[IN_VMEM],
            out_specs=IN_VMEM,
            compiler_params=GRANT,
            name="spread",
        )(stream)
    stream = jnp.transpose(stream.reshape(2, own, quarter, chips, place), (3, 0, 1, 4, 2))
    return stream.reshape(2 * chips, own * place, quarter)


def row_front_kernel(
    lines, me_ref, label_ref, starts_ref, tally_ref, own, near, far, diagonal, triple,
    table_ref, inner_ref, value_ref, tables, normed,
):
    step = pl.program_id(0)
    group, quarter, sites = own.shape
    heads = quarter // HEAD_SIZE

    @pl.when(step == 0)
    def _():
        tables[...] = jnp.zeros_like(tables)

    pieces = []
    for ref in (own, near, far, diagonal):
        lanes = jnp.concatenate([ref[line] for line in range(group)], axis=-1)
        pieces.append(lanes.astype(F32))
    size = 4 * quarter
    average = sum(jnp.sum(piece, axis=0, keepdims=True) for piece in pieces) / size
    pieces = [piece - average for piece in pieces]
    variance = sum(jnp.sum(piece * piece, axis=0, keepdims=True) for piece in pieces) / size
    inverse = lax.rsqrt(variance + 1e-05)
    for spot, piece in zip(quarter_spots(me_ref), pieces):
        spot = pl.multiple_of(spot * quarter, quarter)
        normed[pl.ds(spot, quarter), :] = (piece * inverse).astype(BF16)
    projected = jnp.dot(triple[...], normed[...], preferred_element_type=F32).astype(BF16)
    base = me_ref[0] * lines
    jobs = []
    for line in range(group):
        part = projected[:, line * sites : (line + 1) * sites]
        value_ref[line] = part[2 * quarter :]
        place = step * group + line
        slot = slot_of(label_ref, base, lines, place)
        family = label_ref[base + place]
        members = jnp.full((1, sites), starts_ref[family + 1] - starts_ref[family], jnp.int32)
        scale = HEAD_SIZE**-0.5 * lax.rsqrt(members.astype(F32))
        for head in range(heads):
            lower = head * HEAD_SIZE
            queries = part[lower : lower + HEAD_SIZE]
            keys = part[quarter + lower : quarter + lower + HEAD_SIZE]
            logits = lax.dot_general(queries, keys, CONTRACT_FIRST, preferred_element_type=F32)
            jobs.append((slot * heads + head, logits, scale))
    for index, logits, scale in jobs:
        tables[index] += logits * scale

    @pl.when(step == pl.num_programs(0) - 1)
    def _():
        for index in range(2 * heads):
            table = tables[index].astype(BF16)
            if len(table_ref.shape) == 4:
                groups, _, rows, _ = table_ref.shape
                table_ref[:, index] = table.reshape(groups, rows, sites)
            else:
                table_ref[index] = table
        site = lax.broadcasted_iota(jnp.int32, (sites, sites), 1)

        def inner(index, carry):
            table = tables[2 * heads + index]
            family = label_ref[base] + 1 + index // heads
            family = jnp.minimum(family, tally_ref.shape[0] - 1)
            table = jnp.where(site < tally_ref[family], table, -jnp.inf)
            table = jnp.exp(table - jnp.max(table, axis=-1, keepdims=True))
            table = table / jnp.sum(table, axis=-1, keepdims=True)
            inner_ref[index] = table.astype(BF16)
            return carry

        lax.fori_loop(0, inner_ref.shape[0], inner, 0)


def row_front(pieces, triple, plan, slots, row_groups):
    lines, quarter, sites = pieces[0].shape
    group = 4
    heads = quarter // HEAD_SIZE
    inner = slots - 2
    rows = sites // row_groups
    shape = (row_groups, 2 * heads, rows, sites) if rows % 16 == 0 else (2 * heads, sites, sites)
    block = pl.BlockSpec((group, quarter, sites), lambda step: (step, 0, 0))

    def whole(shape):
        return pl.BlockSpec(shape, lambda step: (0,) * len(shape))

    tables, inner_weights, values = pl.pallas_call(
        functools.partial(row_front_kernel, lines),
        grid=(lines // group,),
        out_shape=(
            jax.ShapeDtypeStruct(shape, BF16),
            jax.ShapeDtypeStruct((inner * heads, sites, sites), BF16),
            jax.ShapeDtypeStruct((lines, quarter, sites), BF16),
        ),
        in_specs=[IN_SMEM] * 4 + [block] * 4 + [whole((3 * quarter, 4 * quarter))],
        out_specs=(whole(shape), whole((inner * heads, sites, sites)), block),
        scratch_shapes=[
            pltpu.VMEM((slots * heads, sites, sites), F32),
            pltpu.VMEM((4 * quarter, group * sites), BF16),
        ],
        compiler_params=GRANT,
        name="row_front",
    )(*plan, *pieces, triple.reshape(3 * quarter, 4 * quarter))
    if rows % 16:
        tables = jnp.transpose(tables.reshape(-1, row_groups, rows, sites), (1, 0, 2, 3))
    return tables, inner_weights, values


def tie_kernel(me_ref, label_ref, starts_ref, tally_ref, parts, out, weights):
    groups, pairs, rows, sites = parts.shape
    lines = label_ref.shape[0] // groups
    ends = [label_ref[g * lines + e * (lines - 1)] for g in range(groups) for e in range(2)]
    heads = pairs // 2
    site = lax.broadcasted_iota(jnp.int32, (heads, rows, sites), 2)
    for family in range(weights.shape[0]):
        total = jnp.zeros((heads, rows, sites), F32)
        for group in range(groups):
            for end in range(2):
                part = parts[group, end * heads : (end + 1) * heads].astype(F32)
                total += jnp.where(ends[2 * group + end] == family, part, 0.0)
        total = jnp.where(site < tally_ref[family], total, -jnp.inf)
        total = jnp.exp(total - jnp.max(total, axis=-1, keepdims=True))
        total = total / jnp.sum(total, axis=-1, keepdims=True)
        weights[family] = total.astype(BF16)
    for group in range(groups):
        for end in range(2):
            chosen = weights[ends[2 * group + end]]
            out[group, end * heads : (end + 1) * heads] = chosen


def tie(parts, plan):
    groups, pairs, rows, sites = parts.shape
    _, label, _, tally = plan
    if rows % 16 == 0:
        return pl.pallas_call(
            tie_kernel,
            out_shape=jax.ShapeDtypeStruct(parts.shape, BF16),
            in_specs=[IN_SMEM] * 4 + [IN_VMEM],
            out_specs=IN_VMEM,
            scratch_shapes=[pltpu.VMEM((tally.shape[0], pairs // 2, rows, sites), BF16)],
            compiler_params=GRANT,
            name="tie",
        )(*plan, parts)
    ends = jnp.stack([label.reshape(groups, -1)[:, 0], label.reshape(groups, -1)[:, -1]], axis=1)
    parts = parts.astype(F32).reshape(groups, 2, -1, rows, sites)
    member = (ends[:, :, None] == jnp.arange(tally.shape[0])).astype(F32)
    totals = jnp.einsum("stf,sthij->fhij", member, parts, precision=lax.Precision.HIGHEST)
    return masked_softmax(totals, tally)[ends].reshape(groups, pairs, rows, sites)


def mix_kernel(me_ref, label_ref, starts_ref, tally_ref, shared, inner, values, out, weights):
    heads, sites = shared.shape[1] // 2, values.shape[2]
    lines, chips = values.shape[0], out.shape[0]
    place = sites // chips
    for index in range(2 * heads):
        weights[index] = shared[:, index].reshape(sites, sites)
    weights[2 * heads :] = inner[...]
    mixed = []
    for line in range(lines):
        slot = slot_of(label_ref, me_ref[0] * lines, lines, line)
        value = values[line]
        mixed.append(
            [
                lax.dot_general(
                    weights[slot * heads + head],
                    value[head * HEAD_SIZE : (head + 1) * HEAD_SIZE],
                    CONTRACT_LAST,
                    preferred_element_type=F32,
                )
                for head in range(heads)
            ]
        )
    pairs = [(part[0], part[1]) for part in mixed]
    pairs += [(mixed[line][2], mixed[line + lines // 2][2]) for line in range(lines // 2)]
    for index in range(0, len(pairs), 2):
        block = [
            jnp.concatenate(pair, axis=1).reshape(chips, place, 2 * HEAD_SIZE)
            for pair in pairs[index : index + 2]
        ]
        out[:, index * place : (index + 2) * place] = jnp.concatenate(block, axis=1).astype(BF16)


def mix(shared, inner, values, plan, chips):
    groups, pairs, rows, sites = shared.shape
    lines, quarter, _ = values.shape
    place = sites // chips
    if rows % 16 == 0 and place % 8 == 0:
        shape = (chips, 3 * lines * place // 2, 2 * HEAD_SIZE)
        return pl.pallas_call(
            mix_kernel,
            out_shape=jax.ShapeDtypeStruct(shape, BF16),
            in_specs=[IN_SMEM] * 4 + [IN_VMEM] * 3,
            out_specs=IN_VMEM,
            scratch_shapes=[pltpu.VMEM((pairs + inner.shape[0], sites, sites), BF16)],
            compiler_params=GRANT,
            name="mix",
        )(*plan, shared, inner, values)
    me, label = plan[:2]
    label = lax.dynamic_slice_in_dim(label, me[0] * lines, lines)
    slot = slot_of(label, 0, lines, jnp.arange(lines))
    ends = jnp.transpose(shared, (1, 0, 2, 3)).reshape(2, pairs // 2, sites, sites)
    weights = jnp.concatenate([ends, inner.reshape(-1, *ends.shape[1:])])[slot]
    values = values.reshape(lines, -1, HEAD_SIZE, sites)
    mixed = jnp.einsum("rhdj,rhij->rihd", values, weights, preferred_element_type=F32)
    mixed = mixed.astype(BF16).reshape(lines, chips, place, quarter)
    return jnp.transpose(mixed, (1, 0, 2, 3)).reshape(chips, lines * place, quarter)


def project_kernel(
    me_ref, blocks, mixing, piece, kept, sent, more, wide, first, second, semaphores
):
    chips, count, lanes = blocks.shape
    quarter, model = mixing.shape
    tokens = count * 2 // 3
    groups, own = chips // 2, tokens // 2
    chip, core = me_ref[1], me_ref[2]
    start = piece.shape[0] - quarter
    tail = quarter - lanes
    first[...] = jnp.zeros_like(first)
    second[...] = jnp.zeros_like(second)
    copies = []
    for index, (source, place, side) in enumerate(((mixing, 0, chip), (piece, start, 1 - chip))):
        spot = pl.multiple_of(side * lanes, lanes)
        end = source.at[pl.ds(place + lanes, tail)]
        moves = (
            (source.at[pl.ds(place, lanes)], wide.at[pl.ds(spot, lanes)]),
            (end, first.at[pl.ds(spot, tail)]),
            (end, second.at[pl.ds(pl.multiple_of(spot + tail, tail), tail)]),
        )
        for number, (origin, target) in enumerate(moves):
            copies.append(
                pltpu.make_async_copy(origin, target, semaphores.at[3 * index + number])
            )
    for copy in copies:
        copy.start()
    values = blocks[...].reshape(groups, 2, count, lanes)
    values = jnp.concatenate([values[:, 0], values[:, 1]], axis=-1)
    whole = values[:, :tokens].reshape(groups * tokens, 2 * lanes)
    narrow = values[:, tokens:].reshape(groups * own, 2 * lanes)
    for copy in copies:
        copy.wait()
    total = jnp.dot(whole, wide[...], preferred_element_type=F32)
    total = total.reshape(groups, tokens, model)
    ends = [
        jnp.dot(narrow, weights[...], preferred_element_type=F32).reshape(groups, own, model)
        for weights in (first, second)
    ]
    halves = [total[:, :own] + ends[0], total[:, own:] + ends[1]]
    for index in range(2):

        @pl.when(core == index)
        def _(index=index):
            kept[...] = halves[index]
            sent[...] = halves[1 - index][: groups // 2].astype(BF16)
            more[...] = halves[1 - index][groups // 2 :].astype(BF16)


def project(blocks, mixing, piece, me, lines):
    chips, count, lanes = blocks.shape
    quarter, model = mixing.shape
    groups = chips // 2
    if lanes != quarter:
        out = (groups, count // 3, model)
        return pl.pallas_call(
            project_kernel,
            out_shape=(
                jax.ShapeDtypeStruct(out, F32),
                jax.ShapeDtypeStruct((groups // 2, *out[1:]), BF16),
                jax.ShapeDtypeStruct((groups // 2, *out[1:]), BF16),
            ),
            in_specs=[IN_SMEM, IN_VMEM, IN_HBM, IN_HBM],
            out_specs=(IN_VMEM, IN_VMEM, IN_VMEM),
            scratch_shapes=[pltpu.VMEM((2 * lanes, model), BF16)] * 3
            + [pltpu.SemaphoreType.DMA((6,))],
            compiler_params=GRANT,
            name="project",
        )(me, blocks, mixing, piece)
    weights = in_order(mixing[None], piece[None, -quarter:], me[1], 0)
    values = blocks.reshape(groups, 2, 2, count // 2, quarter)
    partial = jnp.einsum("gxctd,xde->cgte", values, weights, preferred_element_type=F32)
    kept = lax.dynamic_index_in_dim(partial, me[2], 0, False)
    sent = lax.dynamic_index_in_dim(partial, 1 - me[2], 0, False)
    sent = sent.astype(BF16)
    return kept, sent[: groups // 2], sent[groups // 2 :]


def arrive_kernel(kept, got, more, blocks, normed, later, stream, tokens):
    groups, own, model = kept.shape
    places, rows, _ = stream.shape
    count, lanes = blocks.shape[1], blocks.shape[2]
    heads = blocks.shape[0] // groups
    parts = count // 3
    for group in range(groups):
        source = got if group < groups // 2 else more
        total = kept[group] + source[group % (groups // 2)].astype(F32)
        features = []
        for head in range(heads):
            block = blocks[group * heads + head].astype(F32)
            narrow = block[2 * parts :]
            narrow = jnp.concatenate([narrow[:, : lanes // 2], narrow[:, lanes // 2 :]], axis=0)
            features += [block[: 2 * parts], narrow]
        values = total + jnp.concatenate(features, axis=1)
        for index in range(tokens.shape[0]):
            lower = index * tokens.shape[2]
            part = values[:, lower : lower + tokens.shape[2]]
            tokens[index, group * own : (group + 1) * own] = part
    for place in range(places):
        values = [
            tokens[index, pl.ds(place, rows, stride=places), :] for index in range(tokens.shape[0])
        ]
        values = jnp.concatenate(values, axis=-1).astype(BF16)
        stream[place] = values
        values = values.astype(F32)
        centred = values - jnp.mean(values, axis=-1, keepdims=True)
        variance = jnp.mean(centred * centred, axis=-1, keepdims=True)
        target = normed if place < places // 2 else later
        target[place % (places // 2)] = (centred * lax.rsqrt(variance + 1e-05)).astype(BF16)


def arrive(kept, got, more, blocks, place):
    groups, own, model = kept.shape
    rows = groups * own // place
    if place % 8 == 0:
        shape = jax.ShapeDtypeStruct((place, rows, model), BF16)
        half = jax.ShapeDtypeStruct((place // 2, rows, model), BF16)
        return pl.pallas_call(
            arrive_kernel,
            out_shape=(half, half, shape),
            in_specs=[IN_VMEM] * 4,
            out_specs=(IN_VMEM, IN_VMEM, IN_VMEM),
            scratch_shapes=[pltpu.VMEM((model // 128, groups * own, 128), F32)],
            compiler_params=GRANT,
            name="arrive",
        )(kept, got, more, blocks)
    heads = blocks.shape[0] // groups
    stream = jnp.transpose(blocks.reshape(groups, heads, own, -1), (0, 2, 1, 3))
    stream = stream.reshape(groups, own, model).astype(F32) + kept
    stream += jnp.concatenate([got, more]).astype(F32)
    stream = jnp.transpose(stream.reshape(rows, place, model), (1, 0, 2)).astype(BF16)
    normed = own_norm(stream, -1)
    if place == 1:
        return normed[:, : rows // 2], normed[:, rows // 2 :], stream
    return normed[: place // 2], normed[place // 2 :], stream


def column_kernel(
    lines, me_ref, starts_ref, own, own_later, other, other_later, triple, mixing, piece, rest,
    kept, sent, normed, near, far, projected, mixed, semaphores,
):
    quarter = mixing.shape[0]
    core, pair = me_ref[2], me_ref[3]
    half = rest.shape[0] // 2

    def spot(index):
        return far.at[pl.ds(pl.multiple_of(index * half, half), half)]

    moves = (
        (triple, near.at[pl.ds(0, 3 * quarter)]),
        (mixing, near.at[pl.ds(3 * quarter, quarter)]),
        (piece.at[pl.ds(half, half)], spot(pair)),
        (rest.at[pl.ds(half, half)], spot(1 - pair)),
    )
    copies = [
        pltpu.make_async_copy(source, target, semaphores.at[index])
        for index, (source, target) in enumerate(moves)
    ]
    for copy in copies:
        copy.start()
    places, both, model = normed.shape
    rows = both // 2
    count, width = own.shape[:2]
    for index, values in enumerate((own, own_later, other, other_later)):
        start = index % 2 * count if count < places else 0
        lower = index // 2 * rows + (0 if count < places else index % 2 * width)
        normed[start : start + count, lower : lower + width] = values[...]
    flat = normed[...].reshape(places * both, model)

    def families(axis):
        shape = (both, 1) if axis == 0 else (1, both)
        index = lax.broadcasted_iota(jnp.int32, shape, axis)
        line = jnp.where(index < rows, core * lines, (1 - core) * lines)
        index = jnp.where(index < rows, index, index - rows)
        line += index // lines * (2 * lines) + index % lines
        return sum(
            (line >= starts_ref[family]).astype(jnp.int32)
            for family in range(1, starts_ref.shape[0] - 1)
        )

    same = families(0) == families(1)
    scale = HEAD_SIZE**-0.5

    def attend(weights, lower):
        projected[...] = lax.dot_general(
            weights, flat, CONTRACT_LAST, preferred_element_type=F32
        ).astype(BF16)
        heads = quarter // HEAD_SIZE
        jobs = [(place, head) for place in range(places) for head in range(heads)]
        group = min(len(jobs), max(1, 12 * 128 // both))
        for first in range(0, len(jobs), group):
            batch = jobs[first : first + group]
            scores = []
            for place, head in batch:
                lanes = slice(place * both, (place + 1) * both)
                features = slice(head * HEAD_SIZE, (head + 1) * HEAD_SIZE)
                queries = projected[:quarter, lanes][features]
                keys = projected[quarter : 2 * quarter, lanes][features]
                scores.append(
                    lax.dot_general(keys, queries, CONTRACT_FIRST, preferred_element_type=F32)
                )
            scores = [jnp.where(same, part * scale, -jnp.inf) for part in scores]
            scores = [jnp.exp(part - jnp.max(part, axis=0, keepdims=True)) for part in scores]
            totals = [jnp.sum(part, axis=0, keepdims=True) for part in scores]
            scores = [part.astype(BF16) for part in scores]
            results = []
            for (place, head), part in zip(batch, scores):
                lanes = slice(place * both, (place + 1) * both)
                features = slice(head * HEAD_SIZE, (head + 1) * HEAD_SIZE)
                values = projected[2 * quarter :, lanes][features]
                results.append(jnp.dot(values, part, preferred_element_type=F32))
            for (place, head), part, total in zip(batch, results, totals):
                lanes = slice(place * both, (place + 1) * both)
                target = slice(lower + head * HEAD_SIZE, lower + (head + 1) * HEAD_SIZE)
                mixed[target, lanes] = (part / total).astype(BF16)

    copies[0].wait()
    attend(near[: 3 * quarter], 0)
    for copy in copies[1:]:
        copy.wait()
    attend(far[: 3 * quarter], quarter)
    for place in range(places):
        lanes = slice(place * both, (place + 1) * both)
        partial = lax.dot_general(
            mixed[:quarter, lanes], near[3 * quarter :], CONTRACT_FIRST, preferred_element_type=F32
        )
        partial += lax.dot_general(
            mixed[quarter:, lanes], far[3 * quarter :], CONTRACT_FIRST, preferred_element_type=F32
        )
        kept[place] = partial[:rows]
        sent[place] = partial[rows:].astype(BF16)


def column(own, other, triple, mixing, piece, rest, plan, lines, shape):
    places, rows, model = shape
    quarter = mixing.shape[0]
    tokens = 2 * places * rows
    return pl.pallas_call(
        functools.partial(column_kernel, lines),
        out_shape=(
            jax.ShapeDtypeStruct(shape, F32),
            jax.ShapeDtypeStruct(shape, BF16),
        ),
        in_specs=[IN_SMEM] * 2 + [IN_VMEM] * 4 + [IN_HBM] * 4,
        out_specs=(IN_VMEM, IN_VMEM),
        scratch_shapes=[
            pltpu.VMEM((places, 2 * rows, model), BF16),
            pltpu.VMEM((4 * quarter, model), BF16),
            pltpu.VMEM((4 * quarter, model), BF16),
            pltpu.VMEM((3 * quarter, tokens), BF16),
            pltpu.VMEM((2 * quarter, tokens), BF16),
            pltpu.SemaphoreType.DMA((4,)),
        ],
        compiler_params=GRANT,
        name="column",
    )(plan[0], plan[2], *own, *other, triple.reshape(-1, model), mixing, piece, rest)


def finish_kernel(stream, kept, got, out):
    places, rows, model = stream.shape
    parts, wide = out.shape[1] // 3, out.shape[2]
    quarter = wide // 2 * 3
    heads = model // quarter
    groups = out.shape[0] // heads
    lines = rows // groups
    for group in range(groups):
        these = slice(group * lines, (group + 1) * lines)
        total = stream[:, these].astype(F32) + kept[:, these] + got[:, these].astype(F32)
        total = total.reshape(places * lines, model)
        for head in range(heads):
            block = total[:, head * quarter : (head + 1) * quarter]
            narrow = jnp.concatenate([block[:parts, wide:], block[parts:, wide:]], axis=1)
            block = jnp.concatenate([block[:, :wide], narrow], axis=0)
            out[group * heads + head] = block.astype(BF16)


def finish(stream, kept, got, groups, quarter):
    places, rows, model = stream.shape
    heads, lines = model // quarter, rows // groups
    parts, wide = places * lines // 2, quarter // 3 * 2
    shape = (groups * heads, 3 * parts, wide)
    if parts % 16 == 0 and lines % 8 == 0:
        return pl.pallas_call(
            finish_kernel,
            out_shape=jax.ShapeDtypeStruct(shape, BF16),
            in_specs=[IN_VMEM] * 3,
            out_specs=IN_VMEM,
            compiler_params=GRANT,
            name="finish",
        )(stream, kept, got)
    total = (stream.astype(F32) + kept + got.astype(F32)).astype(BF16)
    total = total.reshape(places, groups, lines, heads, quarter)
    total = jnp.transpose(total, (1, 3, 0, 2, 4)).reshape(-1, places * lines, quarter)
    narrow = jnp.concatenate([total[:, :parts, wide:], total[:, parts:, wide:]], axis=2)
    return jnp.concatenate([total[:, :, :wide], narrow], axis=1)


def feed_forward_kernel(
    me_ref, normed, expand, contract, piece, rest, late, out,
    near_expand, near_contract, far_expand, far_contract, hidden, semaphores,
):
    width = near_expand.shape[1]
    half, pair = rest.shape[0] // 2, me_ref[3]

    def move(source, start, count, target, place, index):
        return pltpu.make_async_copy(
            source.at[pl.ds(start, count)], target.at[pl.ds(place, count)], semaphores.at[index]
        )

    def shared(first, second):
        return [
            move(piece, 0, half, first, 0, 4),
            move(rest, 0, half, second, 0, 5),
        ]

    copies = [
        move(expand, 0, width, near_expand, 0, 0),
        move(contract, 0, width, near_contract, 0, 1),
        move(late, 0, half, far_expand, half, 2),
        move(late, half, half, far_contract, half, 3),
    ]
    for copy in copies:
        copy.start()

    @pl.when(pair == 0)
    def _():
        for copy in shared(far_expand, far_contract):
            copy.start()

    @pl.when(pair != 0)
    def _():
        for copy in shared(far_contract, far_expand):
            copy.start()

    tile = width // 3
    values = normed[...]

    def raise_by(weights, lower):
        for start in range(0, width, tile):
            up = jnp.dot(values, weights[:, start : start + tile], preferred_element_type=F32)
            up = 0.5 * up * (1.0 + lax.erf(up * 2.0**-0.5))
            hidden[:, lower + start : lower + start + tile] = up.astype(BF16)

    copies += shared(far_expand, far_contract)
    copies[0].wait()
    raise_by(near_expand, 0)
    for copy in copies[1:]:
        copy.wait()
    raise_by(far_expand, width)
    down = jnp.dot(hidden[:, :width], near_contract[...], preferred_element_type=F32)
    down += jnp.dot(hidden[:, width:], far_contract[...], preferred_element_type=F32)
    out[...] = down.astype(out.dtype)


def feed_forward(normed, expand, contract, pieces, me, kind):
    places, rows, model = normed.shape
    tokens, width = places * rows, expand.shape[1]
    result = pl.pallas_call(
        feed_forward_kernel,
        out_shape=jax.ShapeDtypeStruct((tokens, model), kind),
        in_specs=[IN_SMEM, IN_VMEM] + [IN_HBM] * 5,
        out_specs=IN_VMEM,
        scratch_shapes=[
            pltpu.VMEM((model, width), BF16),
            pltpu.VMEM((width, model), BF16),
            pltpu.VMEM((model, width), BF16),
            pltpu.VMEM((model, width), BF16),
            pltpu.VMEM((tokens, 2 * width), BF16),
            pltpu.SemaphoreType.DMA((6,)),
        ],
        compiler_params=GRANT,
        name="feed_forward",
    )(me, normed.reshape(tokens, model), expand, contract, *pieces)
    return result.reshape(normed.shape)


def core_sum(stream, kept, sent):
    return (stream.astype(F32) + kept + other_core(sent).astype(F32)).astype(BF16)


def shards(
    alignment_embedding,
    line_group_label,
    group_site_tally,
    horizontal_triple_matrix,
    horizontal_mixing_matrix,
    vertical_triple_matrix,
    vertical_mixing_matrix,
    expand_matrix,
    contract_matrix,
):
    lines, quarter, sites = alignment_embedding.shape
    row_groups = lax.axis_size(ROWS)
    own = lines // 2
    chips = 2 * row_groups
    place = sites // chips
    pair = lax.axis_index("pair")
    chip = lax.axis_index("chip")
    core = lax.axis_index("core")
    label, tally = line_group_label, group_site_tally
    families = tally.shape[0]
    starts = jnp.sum(label[:, None] < jnp.arange(families + 1), axis=0, dtype=jnp.int32)
    me = jnp.stack([lax.axis_index(ROWS), chip, core, pair]).astype(jnp.int32)

    across = other_chip(alignment_embedding)
    near = other_core(alignment_embedding)
    pack, late = pack_weights(
        me,
        horizontal_mixing_matrix,
        vertical_triple_matrix,
        vertical_mixing_matrix,
        expand_matrix,
        contract_matrix,
    )
    stream, pack, late = lax.optimization_barrier((alignment_embedding, pack, late))
    stream = spread(stream, chips)
    stream = lax.all_to_all(stream, ROWS + ("chip", "core"), 0, 0, tiled=True)
    across, near, pack, late, starts, me = lax.optimization_barrier(
        (across, near, pack, late, starts, me)
    )
    plan = (me, label, starts, tally)
    piece = other_chip(pack)

    shared, inner_weights, values = row_front(
        (alignment_embedding, near, across, other_core(across)),
        horizontal_triple_matrix,
        plan,
        2 + max(min(families, lines) - 2, 1),
        row_groups,
    )
    shared, stream = lax.optimization_barrier((shared, stream))
    parts = lax.all_to_all(shared, ROWS, 0, 0, tiled=True)
    shared = lax.all_to_all(tie(parts, plan), ROWS, 0, 0, tiled=True)
    blocks = mix(shared, inner_weights, values, plan, chips)

    blocks, piece, late = lax.optimization_barrier((blocks, piece, late))
    half = expand_matrix.shape[0] // 2
    rest = other_pair(piece[: 2 * half])
    late = other_chip(late)
    blocks = lax.all_to_all(blocks, ROWS + ("chip",), 0, 0, tiled=True)
    kept, *sent = project(blocks, horizontal_mixing_matrix, piece, me, lines)
    got = [other_core(part) for part in sent]
    *normed, after_row = arrive(kept, *got, stream, place)
    other = [other_core(part) for part in normed]
    other, rest, late = lax.optimization_barrier((other, rest, late))

    kept, sent = column(
        normed,
        other,
        vertical_triple_matrix,
        vertical_mixing_matrix,
        piece,
        rest,
        plan,
        own,
        after_row.shape,
    )
    after_col = core_sum(after_row, kept, sent)

    normed = own_norm(after_col, -1)
    weights = (expand_matrix, contract_matrix, (piece, rest, late), me)
    kept = feed_forward(normed, *weights, F32)
    sent = feed_forward(other_core(normed), *weights, BF16)
    blocks = finish(after_col, kept, other_core(sent), row_groups, quarter)

    blocks = lax.all_to_all(blocks, ROWS + ("chip", "core"), 0, 0, tiled=True)
    parts, wide = own * place // 2, quarter // 3 * 2
    narrow = blocks[:, 2 * parts :]
    narrow = jnp.concatenate([narrow[:, :, : wide // 2], narrow[:, :, wide // 2 :]], axis=1)
    finished = jnp.concatenate([blocks[:, : 2 * parts], narrow], axis=2)
    finished = finished.reshape(chips, 2, place, own, quarter)
    finished = jnp.transpose(finished, (1, 3, 4, 0, 2))
    return finished.reshape(lines, quarter, sites)


def solution(mesh):
    planes = mesh.shape["rows"] // 2
    split = Mesh(mesh.devices.reshape(planes, 2, 2, 2), ROWS + ("chip", "core"))
    heads = ("chip", "core")
    placed = (
        P(ROWS, heads, None),
        P(),
        P(),
        P(None, heads, None),
        P(heads, None),
        P(None, heads, None),
        P(heads, None),
        P(None, heads),
        P(heads, None),
    )
    return jax.shard_map(
        shards, mesh=split, in_specs=placed, out_specs=P(ROWS, heads, None), check_vma=False
    )
```

```python
import functools

import jax
import jax.numpy as jnp
from jax import lax
from jax.experimental import pallas as pl
from jax.experimental.pallas import tpu as pltpu
from jax.sharding import Mesh, PartitionSpec as P

HEAD_SIZE = 64
SWAP = [(0, 1), (1, 0)]
ROWS = ("far", "plane", "pair")
PARTS = 4
BF16 = jnp.bfloat16
F32 = jnp.float32


def other_chip(value):
    return lax.ppermute(value, "chip", SWAP)


def other_pair(value):
    return lax.ppermute(value, "pair", SWAP)


def other_plane(value):
    return lax.ppermute(value, "plane", SWAP)


def other_core(value):
    return lax.ppermute(value, "core", SWAP)


def in_order(first, second, index, axis):
    forward = jnp.concatenate([first, second], axis=axis)
    backward = jnp.concatenate([second, first], axis=axis)
    return jnp.where(index == 0, forward, backward)


def half_rows(value, index):
    rows = value.shape[0] // 2
    return lax.dynamic_slice_in_dim(value, index * rows, rows)


def own_norm(values, axis):
    values = values.astype(F32)
    average = jnp.mean(values, axis=axis, keepdims=True)
    centred = values - average
    variance = jnp.mean(centred * centred, axis=axis, keepdims=True)
    return (centred * lax.rsqrt(variance + 1e-05)).astype(BF16)


def masked_softmax(tables, tally):
    live = jnp.arange(tables.shape[-1])[None, :] < tally[:, None]
    tables = jnp.where(live[:, None, None, :], tables, -jnp.inf)
    return jax.nn.softmax(tables, axis=-1).astype(BF16)


CONTRACT_FIRST = (((0,), (0,)), ((), ()))
CONTRACT_LAST = (((1,), (1,)), ((), ()))
IN_VMEM = pl.BlockSpec(memory_space=pltpu.VMEM)
IN_SMEM = pl.BlockSpec(memory_space=pltpu.SMEM)
IN_HBM = pl.BlockSpec(memory_space=pltpu.HBM)
GRANT = pltpu.CompilerParams(vmem_limit_bytes=40 * 2**20)


def slot_of(label_ref, start, lines, line):
    first, last = label_ref[start], label_ref[start + lines - 1]
    family = label_ref[start + line]
    return jnp.where(family == first, 0, jnp.where(family == last, 1, family - first + 1))


def quarter_spots(me_ref):
    chip, core = me_ref[1], me_ref[2]
    return (
        2 * chip + core, 2 * chip + 1 - core, 2 * (1 - chip) + core, 2 * (1 - chip) + 1 - core
    )


def pack_kernel(me_ref, mixing, triple, vertical, expand, contract, pack, late, semaphores):
    quarter = mixing.shape[0]
    half, pair, plane = 2 * quarter, me_ref[3], me_ref[4]

    def move(index, source, start, count, target, place):
        return pltpu.make_async_copy(
            source.at[pl.ds(start, count)], target.at[pl.ds(place, count)], semaphores.at[index]
        )

    fixed = [
        move(0, mixing, 0, quarter, pack, 2 * half),
        move(1, expand, half, half, late, 0),
        move(2, contract, half, half, late, half),
    ]
    by_pair = (
        [
            move(3, expand, 0, quarter, pack, 0),
            move(4, triple, 0, quarter, pack, half),
            move(5, triple, quarter, quarter, pack, half + quarter),
        ],
        [
            move(3, contract, 0, quarter, pack, 0),
            move(4, triple, half, quarter, pack, half),
            move(5, vertical, 0, quarter, pack, half + quarter),
        ],
    )
    by_plane = (
        [move(6, expand, quarter, quarter, pack, quarter)],
        [move(6, contract, quarter, quarter, pack, quarter)],
    )
    for copy in fixed:
        copy.start()
    for index in range(2):
        for place, options in ((pair, by_pair), (plane, by_plane)):

            @pl.when(place == index)
            def _(copies=options[index]):
                for copy in copies:
                    copy.start()

    for copy in fixed + by_pair[0] + by_plane[0]:
        copy.wait()


def pack_weights(me, mixing, triple, vertical, expand, contract):
    quarter, model = mixing.shape
    return pl.pallas_call(
        pack_kernel,
        out_shape=(
            jax.ShapeDtypeStruct((5 * quarter, model), BF16),
            jax.ShapeDtypeStruct((4 * quarter, model), BF16),
        ),
        in_specs=[IN_SMEM] + [IN_HBM] * 5,
        out_specs=(IN_HBM, IN_HBM),
        scratch_shapes=[pltpu.SemaphoreType.DMA((7,))],
        compiler_params=GRANT,
        name="pack",
    )(me, mixing, triple.reshape(-1, model), vertical, expand, contract)


def spread_kernel(stream, out):
    lines, quarter, sites = stream.shape
    chips = out.shape[0] // 2
    place, own = sites // chips, lines // 2
    wide = out.shape[2]
    for core in range(2):
        values = [stream[core * own + line].astype(F32).T for line in range(own)]
        values = [value.reshape(chips, place, quarter) for value in values]
        values = jnp.concatenate(values, axis=1)
        parts = own * place // 2
        narrow = jnp.concatenate([values[:, :parts, wide:], values[:, parts:, wide:]], axis=2)
        values = jnp.concatenate([values[:, :, :wide], narrow], axis=1).astype(BF16)
        for chip in range(chips):
            out[2 * chip + core] = values[chip]


def spread(stream, chips):
    lines, quarter, sites = stream.shape
    place, own = sites // chips, lines // 2
    if place % 8 == 0:
        shape = (2 * chips, 3 * own * place // 2, quarter // 3 * 2)
        return pl.pallas_call(
            spread_kernel,
            out_shape=jax.ShapeDtypeStruct(shape, BF16),
            in_specs=[IN_VMEM],
            out_specs=IN_VMEM,
            compiler_params=GRANT,
            name="spread",
        )(stream)
    stream = jnp.transpose(stream.reshape(2, own, quarter, chips, place), (3, 0, 1, 4, 2))
    return stream.reshape(2 * chips, own * place, quarter)


def row_front_kernel(
    lines, me_ref, label_ref, starts_ref, tally_ref, own, near, far, diagonal, triple,
    table_ref, inner_ref, value_ref, tables, normed,
):
    step = pl.program_id(0)
    group, quarter, sites = own.shape
    heads = quarter // HEAD_SIZE

    @pl.when(step == 0)
    def _():
        tables[...] = jnp.zeros_like(tables)

    pieces = []
    for ref in (own, near, far, diagonal):
        lanes = jnp.concatenate([ref[line] for line in range(group)], axis=-1)
        pieces.append(lanes.astype(F32))
    size = 4 * quarter
    average = sum(jnp.sum(piece, axis=0, keepdims=True) for piece in pieces) / size
    pieces = [piece - average for piece in pieces]
    variance = sum(jnp.sum(piece * piece, axis=0, keepdims=True) for piece in pieces) / size
    inverse = lax.rsqrt(variance + 1e-05)
    for spot, piece in zip(quarter_spots(me_ref), pieces):
        spot = pl.multiple_of(spot * quarter, quarter)
        normed[pl.ds(spot, quarter), :] = (piece * inverse).astype(BF16)
    projected = jnp.dot(triple[...], normed[...], preferred_element_type=F32).astype(BF16)
    base = me_ref[0] * lines
    jobs = []
    for line in range(group):
        part = projected[:, line * sites : (line + 1) * sites]
        value_ref[line] = part[2 * quarter :]
        place = step * group + line
        slot = slot_of(label_ref, base, lines, place)
        family = label_ref[base + place]
        members = jnp.full((1, sites), starts_ref[family + 1] - starts_ref[family], jnp.int32)
        scale = HEAD_SIZE**-0.5 * lax.rsqrt(members.astype(F32))
        for head in range(heads):
            lower = head * HEAD_SIZE
            queries = part[lower : lower + HEAD_SIZE]
            keys = part[quarter + lower : quarter + lower + HEAD_SIZE]
            logits = lax.dot_general(queries, keys, CONTRACT_FIRST, preferred_element_type=F32)
            jobs.append((slot * heads + head, logits, scale))
    for index, logits, scale in jobs:
        tables[index] += logits * scale

    @pl.when(step == pl.num_programs(0) - 1)
    def _():
        for index in range(2 * heads):
            table = tables[index].astype(BF16)
            if len(table_ref.shape) == 4:
                groups, _, rows, _ = table_ref.shape
                table_ref[:, index] = table.reshape(groups, rows, sites)
            else:
                table_ref[index] = table
        site = lax.broadcasted_iota(jnp.int32, (sites, sites), 1)

        def inner(index, carry):
            table = tables[2 * heads + index]
            family = label_ref[base] + 1 + index // heads
            family = jnp.minimum(family, tally_ref.shape[0] - 1)
            table = jnp.where(site < tally_ref[family], table, -jnp.inf)
            table = jnp.exp(table - jnp.max(table, axis=-1, keepdims=True))
            table = table / jnp.sum(table, axis=-1, keepdims=True)
            inner_ref[index] = table.astype(BF16)
            return carry

        lax.fori_loop(0, inner_ref.shape[0], inner, 0)


def row_front(pieces, triple, plan, slots, row_groups):
    lines, quarter, sites = pieces[0].shape
    group = 4
    heads = quarter // HEAD_SIZE
    inner = slots - 2
    rows = sites // row_groups
    shape = (row_groups, 2 * heads, rows, sites) if rows % 16 == 0 else (2 * heads, sites, sites)
    block = pl.BlockSpec((group, quarter, sites), lambda step: (step, 0, 0))

    def whole(shape):
        return pl.BlockSpec(shape, lambda step: (0,) * len(shape))

    tables, inner_weights, values = pl.pallas_call(
        functools.partial(row_front_kernel, lines),
        grid=(lines // group,),
        out_shape=(
            jax.ShapeDtypeStruct(shape, BF16),
            jax.ShapeDtypeStruct((inner * heads, sites, sites), BF16),
            jax.ShapeDtypeStruct((lines, quarter, sites), BF16),
        ),
        in_specs=[IN_SMEM] * 4 + [block] * 4 + [whole((3 * quarter, 4 * quarter))],
        out_specs=(whole(shape), whole((inner * heads, sites, sites)), block),
        scratch_shapes=[
            pltpu.VMEM((slots * heads, sites, sites), F32),
            pltpu.VMEM((4 * quarter, group * sites), BF16),
        ],
        compiler_params=GRANT,
        name="row_front",
    )(*plan, *pieces, triple.reshape(3 * quarter, 4 * quarter))
    if rows % 16:
        tables = jnp.transpose(tables.reshape(-1, row_groups, rows, sites), (1, 0, 2, 3))
    return tables, inner_weights, values


def tie_kernel(me_ref, label_ref, starts_ref, tally_ref, parts, out, weights):
    groups, pairs, rows, sites = parts.shape
    lines = label_ref.shape[0] // groups
    ends = [label_ref[g * lines + e * (lines - 1)] for g in range(groups) for e in range(2)]
    heads = pairs // 2
    site = lax.broadcasted_iota(jnp.int32, (heads, rows, sites), 2)
    for family in range(weights.shape[0]):
        total = jnp.zeros((heads, rows, sites), F32)
        for group in range(groups):
            for end in range(2):
                part = parts[group, end * heads : (end + 1) * heads].astype(F32)
                total += jnp.where(ends[2 * group + end] == family, part, 0.0)
        total = jnp.where(site < tally_ref[family], total, -jnp.inf)
        total = jnp.exp(total - jnp.max(total, axis=-1, keepdims=True))
        total = total / jnp.sum(total, axis=-1, keepdims=True)
        weights[family] = total.astype(BF16)
    for group in range(groups):
        for end in range(2):
            chosen = weights[ends[2 * group + end]]
            out[group, end * heads : (end + 1) * heads] = chosen


def tie(parts, plan):
    groups, pairs, rows, sites = parts.shape
    _, label, _, tally = plan
    if rows % 16 == 0:
        return pl.pallas_call(
            tie_kernel,
            out_shape=jax.ShapeDtypeStruct(parts.shape, BF16),
            in_specs=[IN_SMEM] * 4 + [IN_VMEM],
            out_specs=IN_VMEM,
            scratch_shapes=[pltpu.VMEM((tally.shape[0], pairs // 2, rows, sites), BF16)],
            compiler_params=GRANT,
            name="tie",
        )(*plan, parts)
    ends = jnp.stack([label.reshape(groups, -1)[:, 0], label.reshape(groups, -1)[:, -1]], axis=1)
    parts = parts.astype(F32).reshape(groups, 2, -1, rows, sites)
    member = (ends[:, :, None] == jnp.arange(tally.shape[0])).astype(F32)
    totals = jnp.einsum("stf,sthij->fhij", member, parts, precision=lax.Precision.HIGHEST)
    return masked_softmax(totals, tally)[ends].reshape(groups, pairs, rows, sites)


def mix_kernel(me_ref, label_ref, starts_ref, tally_ref, shared, inner, values, out, weights):
    heads, sites = shared.shape[1] // 2, values.shape[2]
    lines, chips = values.shape[0], out.shape[0]
    place = sites // chips
    for index in range(2 * heads):
        weights[index] = shared[:, index].reshape(sites, sites)
    weights[2 * heads :] = inner[...]
    mixed = []
    for line in range(lines):
        slot = slot_of(label_ref, me_ref[0] * lines, lines, line)
        value = values[line]
        mixed.append(
            [
                lax.dot_general(
                    weights[slot * heads + head],
                    value[head * HEAD_SIZE : (head + 1) * HEAD_SIZE],
                    CONTRACT_LAST,
                    preferred_element_type=F32,
                )
                for head in range(heads)
            ]
        )
    pairs = [(part[0], part[1]) for part in mixed]
    pairs += [(mixed[line][2], mixed[line + lines // 2][2]) for line in range(lines // 2)]
    for index in range(0, len(pairs), 2):
        block = [
            jnp.concatenate(pair, axis=1).reshape(chips, place, 2 * HEAD_SIZE)
            for pair in pairs[index : index + 2]
        ]
        out[:, index * place : (index + 2) * place] = jnp.concatenate(block, axis=1).astype(BF16)


def mix(shared, inner, values, plan, chips):
    groups, pairs, rows, sites = shared.shape
    lines, quarter, _ = values.shape
    place = sites // chips
    if rows % 16 == 0 and place % 8 == 0:
        shape = (chips, 3 * lines * place // 2, 2 * HEAD_SIZE)
        return pl.pallas_call(
            mix_kernel,
            out_shape=jax.ShapeDtypeStruct(shape, BF16),
            in_specs=[IN_SMEM] * 4 + [IN_VMEM] * 3,
            out_specs=IN_VMEM,
            scratch_shapes=[pltpu.VMEM((pairs + inner.shape[0], sites, sites), BF16)],
            compiler_params=GRANT,
            name="mix",
        )(*plan, shared, inner, values)
    me, label = plan[:2]
    label = lax.dynamic_slice_in_dim(label, me[0] * lines, lines)
    slot = slot_of(label, 0, lines, jnp.arange(lines))
    ends = jnp.transpose(shared, (1, 0, 2, 3)).reshape(2, pairs // 2, sites, sites)
    weights = jnp.concatenate([ends, inner.reshape(-1, *ends.shape[1:])])[slot]
    values = values.reshape(lines, -1, HEAD_SIZE, sites)
    mixed = jnp.einsum("rhdj,rhij->rihd", values, weights, preferred_element_type=F32)
    mixed = mixed.astype(BF16).reshape(lines, chips, place, quarter)
    return jnp.transpose(mixed, (1, 0, 2, 3)).reshape(chips, lines * place, quarter)


def project_kernel(me_ref, blocks, mixing, piece, kept, *refs):
    sent = refs[:PARTS]
    wide, first, second, semaphores = refs[PARTS:]
    chips, count, lanes = blocks.shape
    quarter, model = mixing.shape
    tokens = count * 2 // 3
    groups, own = chips // 2, tokens // 2
    chip, core = me_ref[1], me_ref[2]
    start = piece.shape[0] - quarter
    tail = quarter - lanes
    first[...] = jnp.zeros_like(first)
    second[...] = jnp.zeros_like(second)
    copies = []
    for index, (source, place, side) in enumerate(((mixing, 0, chip), (piece, start, 1 - chip))):
        spot = pl.multiple_of(side * lanes, lanes)
        end = source.at[pl.ds(place + lanes, tail)]
        moves = (
            (source.at[pl.ds(place, lanes)], wide.at[pl.ds(spot, lanes)]),
            (end, first.at[pl.ds(spot, tail)]),
            (end, second.at[pl.ds(pl.multiple_of(spot + tail, tail), tail)]),
        )
        for number, (origin, target) in enumerate(moves):
            copies.append(
                pltpu.make_async_copy(origin, target, semaphores.at[3 * index + number])
            )
    for copy in copies:
        copy.start()
    values = blocks[...].reshape(groups, 2, count, lanes)
    values = jnp.concatenate([values[:, 0], values[:, 1]], axis=-1)
    whole = values[:, :tokens].reshape(groups * tokens, 2 * lanes)
    narrow = values[:, tokens:].reshape(groups * own, 2 * lanes)
    for copy in copies:
        copy.wait()
    total = jnp.dot(whole, wide[...], preferred_element_type=F32)
    total = total.reshape(groups, tokens, model)
    ends = [
        jnp.dot(narrow, weights[...], preferred_element_type=F32).reshape(groups, own, model)
        for weights in (first, second)
    ]
    halves = [total[:, :own] + ends[0], total[:, own:] + ends[1]]
    for index in range(2):

        @pl.when(core == index)
        def _(index=index):
            kept[...] = halves[index]
            for number, part in enumerate(sent):
                lower = number * groups // PARTS
                part[...] = halves[1 - index][lower : lower + groups // PARTS].astype(BF16)


def project(blocks, mixing, piece, me, lines):
    chips, count, lanes = blocks.shape
    quarter, model = mixing.shape
    groups = chips // 2
    if lanes != quarter:
        out = (groups, count // 3, model)
        return pl.pallas_call(
            project_kernel,
            out_shape=(jax.ShapeDtypeStruct(out, F32),)
            + (jax.ShapeDtypeStruct((groups // PARTS, *out[1:]), BF16),) * PARTS,
            in_specs=[IN_SMEM, IN_VMEM, IN_HBM, IN_HBM],
            out_specs=(IN_VMEM,) * (1 + PARTS),
            scratch_shapes=[pltpu.VMEM((2 * lanes, model), BF16)] * 3
            + [pltpu.SemaphoreType.DMA((6,))],
            compiler_params=GRANT,
            name="project",
        )(me, blocks, mixing, piece)
    weights = in_order(mixing[None], piece[None, -quarter:], me[1], 0)
    values = blocks.reshape(groups, 2, 2, count // 2, quarter)
    partial = jnp.einsum("gxctd,xde->cgte", values, weights, preferred_element_type=F32)
    kept = lax.dynamic_index_in_dim(partial, me[2], 0, False)
    sent = lax.dynamic_index_in_dim(partial, 1 - me[2], 0, False)
    return kept, *jnp.split(sent.astype(BF16), PARTS)


def arrive_kernel(kept, *refs):
    got, blocks = refs[:PARTS], refs[PARTS]
    normed, (stream, tokens) = refs[PARTS + 1 : 2 * PARTS + 1], refs[2 * PARTS + 1 :]
    groups, own, model = kept.shape
    places, rows, _ = stream.shape
    count, lanes = blocks.shape[1], blocks.shape[2]
    heads = blocks.shape[0] // groups
    parts = count // 3
    for group in range(groups):
        each = groups // PARTS
        total = kept[group] + got[group // each][group % each].astype(F32)
        features = []
        for head in range(heads):
            block = blocks[group * heads + head].astype(F32)
            narrow = block[2 * parts :]
            narrow = jnp.concatenate([narrow[:, : lanes // 2], narrow[:, lanes // 2 :]], axis=0)
            features += [block[: 2 * parts], narrow]
        values = total + jnp.concatenate(features, axis=1)
        for index in range(tokens.shape[0]):
            lower = index * tokens.shape[2]
            part = values[:, lower : lower + tokens.shape[2]]
            tokens[index, group * own : (group + 1) * own] = part
    for place in range(places):
        values = [
            tokens[index, pl.ds(place, rows, stride=places), :] for index in range(tokens.shape[0])
        ]
        values = jnp.concatenate(values, axis=-1).astype(BF16)
        stream[place] = values
        values = values.astype(F32)
        centred = values - jnp.mean(values, axis=-1, keepdims=True)
        variance = jnp.mean(centred * centred, axis=-1, keepdims=True)
        each = places // PARTS
        normed[place // each][place % each] = (centred * lax.rsqrt(variance + 1e-05)).astype(BF16)


def arrive(kept, got, blocks, place):
    groups, own, model = kept.shape
    rows = groups * own // place
    if place % 8 == 0:
        shape = jax.ShapeDtypeStruct((place, rows, model), BF16)
        part = jax.ShapeDtypeStruct((place // PARTS, rows, model), BF16)
        return pl.pallas_call(
            arrive_kernel,
            out_shape=(part,) * PARTS + (shape,),
            in_specs=[IN_VMEM] * (2 + PARTS),
            out_specs=(IN_VMEM,) * (1 + PARTS),
            scratch_shapes=[pltpu.VMEM((model // 128, groups * own, 128), F32)],
            compiler_params=GRANT,
            name="arrive",
        )(kept, *got, blocks)
    heads = blocks.shape[0] // groups
    stream = jnp.transpose(blocks.reshape(groups, heads, own, -1), (0, 2, 1, 3))
    stream = stream.reshape(groups, own, model).astype(F32) + kept
    stream += jnp.concatenate(got).astype(F32)
    stream = jnp.transpose(stream.reshape(rows, place, model), (1, 0, 2)).astype(BF16)
    normed = own_norm(stream, -1)
    return *jnp.split(normed, PARTS, axis=0 if place % PARTS == 0 else 1), stream


def column_kernel(
    lines, me_ref, starts_ref, *refs
):
    tokens = refs[: 2 * PARTS]
    triple, mixing, piece, rest, kept, sent = refs[2 * PARTS : 2 * PARTS + 6]
    normed, near, far, projected, mixed, semaphores = refs[2 * PARTS + 6 :]
    quarter = mixing.shape[0]
    core, pair = me_ref[2], me_ref[3]
    half = rest.shape[0]

    def spot(index):
        return far.at[pl.ds(pl.multiple_of(index * half, half), half)]

    moves = (
        (triple, near.at[pl.ds(0, 3 * quarter)]),
        (mixing, near.at[pl.ds(3 * quarter, quarter)]),
        (piece.at[pl.ds(half, half)], spot(pair)),
        (rest, spot(1 - pair)),
    )
    copies = [
        pltpu.make_async_copy(source, target, semaphores.at[index])
        for index, (source, target) in enumerate(moves)
    ]
    for copy in copies:
        copy.start()
    places, both, model = normed.shape
    rows = both // 2
    count, width = tokens[0].shape[:2]
    for index, values in enumerate(tokens):
        part, lower = index % PARTS, index // PARTS * rows
        start = part * count if count < places else 0
        lower += 0 if count < places else part * width
        normed[start : start + count, lower : lower + width] = values[...]
    flat = normed[...].reshape(places * both, model)

    def families(axis):
        shape = (both, 1) if axis == 0 else (1, both)
        index = lax.broadcasted_iota(jnp.int32, shape, axis)
        line = jnp.where(index < rows, core * lines, (1 - core) * lines)
        index = jnp.where(index < rows, index, index - rows)
        line += index // lines * (2 * lines) + index % lines
        return sum(
            (line >= starts_ref[family]).astype(jnp.int32)
            for family in range(1, starts_ref.shape[0] - 1)
        )

    same = families(0) == families(1)
    scale = HEAD_SIZE**-0.5

    def attend(weights, lower):
        projected[...] = lax.dot_general(
            weights, flat, CONTRACT_LAST, preferred_element_type=F32
        ).astype(BF16)
        heads = quarter // HEAD_SIZE
        jobs = [(place, head) for place in range(places) for head in range(heads)]
        group = min(len(jobs), max(1, 12 * 128 // both))
        for first in range(0, len(jobs), group):
            batch = jobs[first : first + group]
            scores = []
            for place, head in batch:
                lanes = slice(place * both, (place + 1) * both)
                features = slice(head * HEAD_SIZE, (head + 1) * HEAD_SIZE)
                queries = projected[:quarter, lanes][features]
                keys = projected[quarter : 2 * quarter, lanes][features]
                scores.append(
                    lax.dot_general(keys, queries, CONTRACT_FIRST, preferred_element_type=F32)
                )
            scores = [jnp.where(same, part * scale, -jnp.inf) for part in scores]
            scores = [jnp.exp(part - jnp.max(part, axis=0, keepdims=True)) for part in scores]
            totals = [jnp.sum(part, axis=0, keepdims=True) for part in scores]
            scores = [part.astype(BF16) for part in scores]
            results = []
            for (place, head), part in zip(batch, scores):
                lanes = slice(place * both, (place + 1) * both)
                features = slice(head * HEAD_SIZE, (head + 1) * HEAD_SIZE)
                values = projected[2 * quarter :, lanes][features]
                results.append(jnp.dot(values, part, preferred_element_type=F32))
            for (place, head), part, total in zip(batch, results, totals):
                lanes = slice(place * both, (place + 1) * both)
                target = slice(lower + head * HEAD_SIZE, lower + (head + 1) * HEAD_SIZE)
                mixed[target, lanes] = (part / total).astype(BF16)

    copies[0].wait()
    attend(near[: 3 * quarter], 0)
    for copy in copies[1:]:
        copy.wait()
    attend(far[: 3 * quarter], quarter)
    for place in range(places):
        lanes = slice(place * both, (place + 1) * both)
        partial = lax.dot_general(
            mixed[:quarter, lanes], near[3 * quarter :], CONTRACT_FIRST, preferred_element_type=F32
        )
        partial += lax.dot_general(
            mixed[quarter:, lanes], far[3 * quarter :], CONTRACT_FIRST, preferred_element_type=F32
        )
        kept[place] = partial[:rows]
        sent[place] = partial[rows:].astype(BF16)


def column(own, other, triple, mixing, piece, rest, plan, lines, shape):
    places, rows, model = shape
    quarter = mixing.shape[0]
    tokens = 2 * places * rows
    return pl.pallas_call(
        functools.partial(column_kernel, lines),
        out_shape=(
            jax.ShapeDtypeStruct(shape, F32),
            jax.ShapeDtypeStruct(shape, BF16),
        ),
        in_specs=[IN_SMEM] * 2 + [IN_VMEM] * (2 * PARTS) + [IN_HBM] * 4,
        out_specs=(IN_VMEM, IN_VMEM),
        scratch_shapes=[
            pltpu.VMEM((places, 2 * rows, model), BF16),
            pltpu.VMEM((4 * quarter, model), BF16),
            pltpu.VMEM((4 * quarter, model), BF16),
            pltpu.VMEM((3 * quarter, tokens), BF16),
            pltpu.VMEM((2 * quarter, tokens), BF16),
            pltpu.SemaphoreType.DMA((4,)),
        ],
        compiler_params=GRANT,
        name="column",
    )(plan[0], plan[2], *own, *other, triple.reshape(-1, model), mixing, piece, rest)


def finish_kernel(stream, kept, got, out):
    places, rows, model = stream.shape
    parts, wide = out.shape[1] // 3, out.shape[2]
    quarter = wide // 2 * 3
    heads = model // quarter
    groups = out.shape[0] // heads
    lines = rows // groups
    for group in range(groups):
        these = slice(group * lines, (group + 1) * lines)
        total = stream[:, these].astype(F32) + kept[:, these] + got[:, these].astype(F32)
        total = total.reshape(places * lines, model)
        for head in range(heads):
            block = total[:, head * quarter : (head + 1) * quarter]
            narrow = jnp.concatenate([block[:parts, wide:], block[parts:, wide:]], axis=1)
            block = jnp.concatenate([block[:, :wide], narrow], axis=0)
            out[group * heads + head] = block.astype(BF16)


def finish(stream, kept, got, groups, quarter):
    places, rows, model = stream.shape
    heads, lines = model // quarter, rows // groups
    parts, wide = places * lines // 2, quarter // 3 * 2
    shape = (groups * heads, 3 * parts, wide)
    if parts % 16 == 0 and lines % 8 == 0:
        return pl.pallas_call(
            finish_kernel,
            out_shape=jax.ShapeDtypeStruct(shape, BF16),
            in_specs=[IN_VMEM] * 3,
            out_specs=IN_VMEM,
            compiler_params=GRANT,
            name="finish",
        )(stream, kept, got)
    total = (stream.astype(F32) + kept + got.astype(F32)).astype(BF16)
    total = total.reshape(places, groups, lines, heads, quarter)
    total = jnp.transpose(total, (1, 3, 0, 2, 4)).reshape(-1, places * lines, quarter)
    narrow = jnp.concatenate([total[:, :parts, wide:], total[:, parts:, wide:]], axis=2)
    return jnp.concatenate([total[:, :, :wide], narrow], axis=1)


def feed_forward_kernel(
    me_ref, normed, expand, contract, piece, pair_rest, plane_rest, late, out,
    near_expand, near_contract, far_expand, far_contract, hidden, semaphores,
):
    width = near_expand.shape[1]
    count, half = pair_rest.shape[0], width // 2
    pair, plane = me_ref[3], me_ref[4]

    def move(source, start, count, target, place, index):
        return pltpu.make_async_copy(
            source.at[pl.ds(start, count)], target.at[pl.ds(place, count)], semaphores.at[index]
        )

    def by_pair(first, second):
        return [
            move(piece, 0, count, first, 0, 4),
            move(pair_rest, 0, count, second, 0, 5),
        ]

    def by_plane(first, second):
        return [
            move(piece, count, count, first, count, 6),
            move(plane_rest, 0, count, second, count, 7),
        ]

    copies = [
        move(expand, 0, width, near_expand, 0, 0),
        move(contract, 0, width, near_contract, 0, 1),
        move(late, 0, half, far_expand, half, 2),
        move(late, half, half, far_contract, half, 3),
    ]
    for copy in copies:
        copy.start()
    for place, moves in ((pair, by_pair), (plane, by_plane)):

        @pl.when(place == 0)
        def _(moves=moves):
            for copy in moves(far_expand, far_contract):
                copy.start()

        @pl.when(place != 0)
        def _(moves=moves):
            for copy in moves(far_contract, far_expand):
                copy.start()

    tile = width // 3
    values = normed[...]

    def raise_by(weights, lower):
        for start in range(0, width, tile):
            up = jnp.dot(values, weights[:, start : start + tile], preferred_element_type=F32)
            up = 0.5 * up * (1.0 + lax.erf(up * 2.0**-0.5))
            hidden[:, lower + start : lower + start + tile] = up.astype(BF16)

    copies += by_pair(far_expand, far_contract) + by_plane(far_expand, far_contract)
    copies[0].wait()
    raise_by(near_expand, 0)
    for copy in copies[1:]:
        copy.wait()
    raise_by(far_expand, width)
    down = jnp.dot(hidden[:, :width], near_contract[...], preferred_element_type=F32)
    down += jnp.dot(hidden[:, width:], far_contract[...], preferred_element_type=F32)
    out[...] = down.astype(out.dtype)


def feed_forward(normed, expand, contract, pieces, me, kind):
    places, rows, model = normed.shape
    tokens, width = places * rows, expand.shape[1]
    result = pl.pallas_call(
        feed_forward_kernel,
        out_shape=jax.ShapeDtypeStruct((tokens, model), kind),
        in_specs=[IN_SMEM, IN_VMEM] + [IN_HBM] * 6,
        out_specs=IN_VMEM,
        scratch_shapes=[
            pltpu.VMEM((model, width), BF16),
            pltpu.VMEM((width, model), BF16),
            pltpu.VMEM((model, width), BF16),
            pltpu.VMEM((model, width), BF16),
            pltpu.VMEM((tokens, 2 * width), BF16),
            pltpu.SemaphoreType.DMA((8,)),
        ],
        compiler_params=GRANT,
        name="feed_forward",
    )(me, normed.reshape(tokens, model), expand, contract, *pieces)
    return result.reshape(normed.shape)


def core_sum(stream, kept, sent):
    return (stream.astype(F32) + kept + other_core(sent).astype(F32)).astype(BF16)


def shards(
    alignment_embedding,
    line_group_label,
    group_site_tally,
    horizontal_triple_matrix,
    horizontal_mixing_matrix,
    vertical_triple_matrix,
    vertical_mixing_matrix,
    expand_matrix,
    contract_matrix,
):
    lines, quarter, sites = alignment_embedding.shape
    row_groups = lax.axis_size(ROWS)
    own = lines // 2
    chips = 2 * row_groups
    place = sites // chips
    pair = lax.axis_index("pair")
    chip = lax.axis_index("chip")
    core = lax.axis_index("core")
    label, tally = line_group_label, group_site_tally
    families = tally.shape[0]
    starts = jnp.sum(label[:, None] < jnp.arange(families + 1), axis=0, dtype=jnp.int32)
    plane = lax.axis_index("plane")
    me = jnp.stack([lax.axis_index(ROWS), chip, core, pair, plane]).astype(jnp.int32)

    across = other_chip(alignment_embedding)
    near = other_core(alignment_embedding)
    pack, late = pack_weights(
        me,
        horizontal_mixing_matrix,
        vertical_triple_matrix,
        vertical_mixing_matrix,
        expand_matrix,
        contract_matrix,
    )
    stream, pack, late = lax.optimization_barrier((alignment_embedding, pack, late))
    stream = spread(stream, chips)
    stream = lax.all_to_all(stream, ROWS + ("chip", "core"), 0, 0, tiled=True)
    across, near, pack, late, starts, me = lax.optimization_barrier(
        (across, near, pack, late, starts, me)
    )
    plan = (me, label, starts, tally)
    piece = other_chip(pack)

    shared, inner_weights, values = row_front(
        (alignment_embedding, near, across, other_core(across)),
        horizontal_triple_matrix,
        plan,
        2 + max(min(families, lines) - 2, 1),
        row_groups,
    )
    shared, stream = lax.optimization_barrier((shared, stream))
    parts = lax.all_to_all(shared, ROWS, 0, 0, tiled=True)
    shared = lax.all_to_all(tie(parts, plan), ROWS, 0, 0, tiled=True)
    blocks = mix(shared, inner_weights, values, plan, chips)

    blocks, piece, late = lax.optimization_barrier((blocks, piece, late))
    half = expand_matrix.shape[0] // 2
    column_rest = other_pair(piece[half : 2 * half])
    feed_rest = (other_pair(piece[:quarter]), other_plane(piece[quarter:half]))
    late = other_chip(late)
    blocks = lax.all_to_all(blocks, ROWS + ("chip",), 0, 0, tiled=True)
    kept, *sent = project(blocks, horizontal_mixing_matrix, piece, me, lines)
    got = [other_core(part) for part in sent]
    got, column_rest = lax.optimization_barrier((got, column_rest))
    *normed, after_row = arrive(kept, got, stream, place)
    other = [other_core(part) for part in normed]

    kept, sent = column(
        normed,
        other,
        vertical_triple_matrix,
        vertical_mixing_matrix,
        piece,
        column_rest,
        plan,
        own,
        after_row.shape,
    )
    sent, feed_rest, late = lax.optimization_barrier((sent, feed_rest, late))
    after_col = core_sum(after_row, kept, sent)

    normed = own_norm(after_col, -1)
    weights = (expand_matrix, contract_matrix, (piece, *feed_rest, late), me)
    kept = feed_forward(normed, *weights, F32)
    sent = feed_forward(other_core(normed), *weights, BF16)
    blocks = finish(after_col, kept, other_core(sent), row_groups, quarter)

    blocks = lax.all_to_all(blocks, ROWS + ("chip", "core"), 0, 0, tiled=True)
    parts, wide = own * place // 2, quarter // 3 * 2
    narrow = blocks[:, 2 * parts :]
    narrow = jnp.concatenate([narrow[:, :, : wide // 2], narrow[:, :, wide // 2 :]], axis=1)
    finished = jnp.concatenate([blocks[:, : 2 * parts], narrow], axis=2)
    finished = finished.reshape(chips, 2, place, own, quarter)
    finished = jnp.transpose(finished, (1, 3, 4, 0, 2))
    return finished.reshape(lines, quarter, sites)


def solution(mesh):
    far = mesh.shape["rows"] // 4
    split = Mesh(mesh.devices.reshape(far, 2, 2, 2, 2), ROWS + ("chip", "core"))
    heads = ("chip", "core")
    placed = (
        P(ROWS, heads, None),
        P(),
        P(),
        P(None, heads, None),
        P(heads, None),
        P(None, heads, None),
        P(heads, None),
        P(None, heads),
        P(heads, None),
    )
    return jax.shard_map(
        shards, mesh=split, in_specs=placed, out_specs=P(ROWS, heads, None), check_vma=False
    )
```

```python
import functools

import jax
import jax.numpy as jnp
from jax import lax
from jax.experimental import pallas as pl
from jax.experimental.pallas import tpu as pltpu
from jax.sharding import Mesh, PartitionSpec as P

HEAD_SIZE = 64
SWAP = [(0, 1), (1, 0)]
ROWS = ("far", "plane", "pair")
PARTS = 4
BF16 = jnp.bfloat16
F32 = jnp.float32


def other_chip(value):
    return lax.ppermute(value, "chip", SWAP)


def other_pair(value):
    return lax.ppermute(value, "pair", SWAP)


def other_plane(value):
    return lax.ppermute(value, "plane", SWAP)


def other_core(value):
    return lax.ppermute(value, "core", SWAP)


def in_order(first, second, index, axis):
    forward = jnp.concatenate([first, second], axis=axis)
    backward = jnp.concatenate([second, first], axis=axis)
    return jnp.where(index == 0, forward, backward)


def half_rows(value, index):
    rows = value.shape[0] // 2
    return lax.dynamic_slice_in_dim(value, index * rows, rows)


def own_norm(values, axis):
    values = values.astype(F32)
    average = jnp.mean(values, axis=axis, keepdims=True)
    centred = values - average
    variance = jnp.mean(centred * centred, axis=axis, keepdims=True)
    return (centred * lax.rsqrt(variance + 1e-05)).astype(BF16)


def masked_softmax(tables, tally):
    live = jnp.arange(tables.shape[-1])[None, :] < tally[:, None]
    tables = jnp.where(live[:, None, None, :], tables, -jnp.inf)
    return jax.nn.softmax(tables, axis=-1).astype(BF16)


CONTRACT_FIRST = (((0,), (0,)), ((), ()))
CONTRACT_LAST = (((1,), (1,)), ((), ()))
IN_VMEM = pl.BlockSpec(memory_space=pltpu.VMEM)
IN_SMEM = pl.BlockSpec(memory_space=pltpu.SMEM)
IN_HBM = pl.BlockSpec(memory_space=pltpu.HBM)
GRANT = pltpu.CompilerParams(vmem_limit_bytes=40 * 2**20)


def slot_of(label_ref, start, lines, line):
    first, last = label_ref[start], label_ref[start + lines - 1]
    family = label_ref[start + line]
    return jnp.where(family == first, 0, jnp.where(family == last, 1, family - first + 1))


def quarter_spots(me_ref):
    chip, core = me_ref[1], me_ref[2]
    return (
        2 * chip + core, 2 * chip + 1 - core, 2 * (1 - chip) + core, 2 * (1 - chip) + 1 - core
    )


def pack_kernel(me_ref, mixing, triple, vertical, expand, contract, pack, late, semaphores):
    quarter = mixing.shape[0]
    half, pair, plane = 2 * quarter, me_ref[3], me_ref[4]

    def move(index, source, start, count, target, place):
        return pltpu.make_async_copy(
            source.at[pl.ds(start, count)], target.at[pl.ds(place, count)], semaphores.at[index]
        )

    fixed = [
        move(0, mixing, 0, quarter, pack, 2 * half),
        move(1, expand, half, half, late, 0),
        move(2, contract, half, half, late, half),
    ]
    by_pair = (
        [
            move(3, expand, 0, quarter, pack, 0),
            move(4, triple, 0, quarter, pack, half),
            move(5, triple, quarter, quarter, pack, half + quarter),
        ],
        [
            move(3, contract, 0, quarter, pack, 0),
            move(4, triple, half, quarter, pack, half),
            move(5, vertical, 0, quarter, pack, half + quarter),
        ],
    )
    by_plane = (
        [move(6, expand, quarter, quarter, pack, quarter)],
        [move(6, contract, quarter, quarter, pack, quarter)],
    )
    for copy in fixed:
        copy.start()
    for index in range(2):
        for place, options in ((pair, by_pair), (plane, by_plane)):

            @pl.when(place == index)
            def _(copies=options[index]):
                for copy in copies:
                    copy.start()

    for copy in fixed + by_pair[0] + by_plane[0]:
        copy.wait()


def pack_weights(me, mixing, triple, vertical, expand, contract):
    quarter, model = mixing.shape
    return pl.pallas_call(
        pack_kernel,
        out_shape=(
            jax.ShapeDtypeStruct((5 * quarter, model), BF16),
            jax.ShapeDtypeStruct((4 * quarter, model), BF16),
        ),
        in_specs=[IN_SMEM] + [IN_HBM] * 5,
        out_specs=(IN_HBM, IN_HBM),
        scratch_shapes=[pltpu.SemaphoreType.DMA((7,))],
        compiler_params=GRANT,
        name="pack",
    )(me, mixing, triple.reshape(-1, model), vertical, expand, contract)


def spread_kernel(stream, out):
    lines, quarter, sites = stream.shape
    chips = out.shape[0] // 2
    place, own = sites // chips, lines // 2
    wide = out.shape[2]
    for core in range(2):
        values = [stream[core * own + line].astype(F32).T for line in range(own)]
        values = [value.reshape(chips, place, quarter) for value in values]
        values = jnp.concatenate(values, axis=1)
        parts = own * place // 2
        narrow = jnp.concatenate([values[:, :parts, wide:], values[:, parts:, wide:]], axis=2)
        values = jnp.concatenate([values[:, :, :wide], narrow], axis=1).astype(BF16)
        for chip in range(chips):
            out[2 * chip + core] = values[chip]


def spread(stream, chips):
    lines, quarter, sites = stream.shape
    place, own = sites // chips, lines // 2
    if place % 8 == 0:
        shape = (2 * chips, 3 * own * place // 2, quarter // 3 * 2)
        return pl.pallas_call(
            spread_kernel,
            out_shape=jax.ShapeDtypeStruct(shape, BF16),
            in_specs=[IN_VMEM],
            out_specs=IN_VMEM,
            compiler_params=GRANT,
            name="spread",
        )(stream)
    stream = jnp.transpose(stream.reshape(2, own, quarter, chips, place), (3, 0, 1, 4, 2))
    return stream.reshape(2 * chips, own * place, quarter)


def row_front_kernel(
    lines, me_ref, label_ref, starts_ref, tally_ref, own, near, far, diagonal, triple,
    table_ref, inner_ref, value_ref, tables, normed,
):
    step = pl.program_id(0)
    group, quarter, sites = own.shape
    heads = quarter // HEAD_SIZE

    @pl.when(step == 0)
    def _():
        tables[...] = jnp.zeros_like(tables)

    pieces = []
    for ref in (own, near, far, diagonal):
        lanes = jnp.concatenate([ref[line] for line in range(group)], axis=-1)
        pieces.append(lanes.astype(F32))
    size = 4 * quarter
    average = sum(jnp.sum(piece, axis=0, keepdims=True) for piece in pieces) / size
    pieces = [piece - average for piece in pieces]
    variance = sum(jnp.sum(piece * piece, axis=0, keepdims=True) for piece in pieces) / size
    inverse = lax.rsqrt(variance + 1e-05)
    for spot, piece in zip(quarter_spots(me_ref), pieces):
        spot = pl.multiple_of(spot * quarter, quarter)
        normed[pl.ds(spot, quarter), :] = (piece * inverse).astype(BF16)
    projected = jnp.dot(triple[...], normed[...], preferred_element_type=F32).astype(BF16)
    base = me_ref[0] * lines
    jobs = []
    for line in range(group):
        part = projected[:, line * sites : (line + 1) * sites]
        value_ref[line] = part[2 * quarter :]
        place = step * group + line
        slot = slot_of(label_ref, base, lines, place)
        family = label_ref[base + place]
        members = jnp.full((1, sites), starts_ref[family + 1] - starts_ref[family], jnp.int32)
        scale = HEAD_SIZE**-0.5 * lax.rsqrt(members.astype(F32))
        for head in range(heads):
            lower = head * HEAD_SIZE
            queries = part[lower : lower + HEAD_SIZE]
            keys = part[quarter + lower : quarter + lower + HEAD_SIZE]
            logits = lax.dot_general(queries, keys, CONTRACT_FIRST, preferred_element_type=F32)
            jobs.append((slot * heads + head, logits, scale))
    for index, logits, scale in jobs:
        tables[index] += logits * scale

    @pl.when(step == pl.num_programs(0) - 1)
    def _():
        for index in range(2 * heads):
            table = tables[index].astype(BF16)
            if len(table_ref.shape) == 4:
                groups, _, rows, _ = table_ref.shape
                table_ref[:, index] = table.reshape(groups, rows, sites)
            else:
                table_ref[index] = table
        site = lax.broadcasted_iota(jnp.int32, (sites, sites), 1)

        def inner(index, carry):
            table = tables[2 * heads + index]
            family = label_ref[base] + 1 + index // heads
            family = jnp.minimum(family, tally_ref.shape[0] - 1)
            table = jnp.where(site < tally_ref[family], table, -jnp.inf)
            table = jnp.exp(table - jnp.max(table, axis=-1, keepdims=True))
            table = table / jnp.sum(table, axis=-1, keepdims=True)
            inner_ref[index] = table.astype(BF16)
            return carry

        lax.fori_loop(0, inner_ref.shape[0], inner, 0)


def row_front(pieces, triple, plan, slots, row_groups):
    lines, quarter, sites = pieces[0].shape
    group = 4
    heads = quarter // HEAD_SIZE
    inner = slots - 2
    rows = sites // row_groups
    shape = (row_groups, 2 * heads, rows, sites) if rows % 16 == 0 else (2 * heads, sites, sites)
    block = pl.BlockSpec((group, quarter, sites), lambda step: (step, 0, 0))

    def whole(shape):
        return pl.BlockSpec(shape, lambda step: (0,) * len(shape))

    tables, inner_weights, values = pl.pallas_call(
        functools.partial(row_front_kernel, lines),
        grid=(lines // group,),
        out_shape=(
            jax.ShapeDtypeStruct(shape, BF16),
            jax.ShapeDtypeStruct((inner * heads, sites, sites), BF16),
            jax.ShapeDtypeStruct((lines, quarter, sites), BF16),
        ),
        in_specs=[IN_SMEM] * 4 + [block] * 4 + [whole((3 * quarter, 4 * quarter))],
        out_specs=(whole(shape), whole((inner * heads, sites, sites)), block),
        scratch_shapes=[
            pltpu.VMEM((slots * heads, sites, sites), F32),
            pltpu.VMEM((4 * quarter, group * sites), BF16),
        ],
        compiler_params=GRANT,
        name="row_front",
    )(*plan, *pieces, triple.reshape(3 * quarter, 4 * quarter))
    if rows % 16:
        tables = jnp.transpose(tables.reshape(-1, row_groups, rows, sites), (1, 0, 2, 3))
    return tables, inner_weights, values


def tie_kernel(me_ref, label_ref, starts_ref, tally_ref, parts, out, weights):
    groups, pairs, rows, sites = parts.shape
    lines = label_ref.shape[0] // groups
    ends = [label_ref[g * lines + e * (lines - 1)] for g in range(groups) for e in range(2)]
    heads = pairs // 2
    site = lax.broadcasted_iota(jnp.int32, (heads, rows, sites), 2)
    for family in range(weights.shape[0]):
        total = jnp.zeros((heads, rows, sites), F32)
        for group in range(groups):
            for end in range(2):
                part = parts[group, end * heads : (end + 1) * heads].astype(F32)
                total += jnp.where(ends[2 * group + end] == family, part, 0.0)
        total = jnp.where(site < tally_ref[family], total, -jnp.inf)
        total = jnp.exp(total - jnp.max(total, axis=-1, keepdims=True))
        total = total / jnp.sum(total, axis=-1, keepdims=True)
        weights[family] = total.astype(BF16)
    for group in range(groups):
        for end in range(2):
            chosen = weights[ends[2 * group + end]]
            out[group, end * heads : (end + 1) * heads] = chosen


def tie(parts, plan):
    groups, pairs, rows, sites = parts.shape
    _, label, _, tally = plan
    if rows % 16 == 0:
        return pl.pallas_call(
            tie_kernel,
            out_shape=jax.ShapeDtypeStruct(parts.shape, BF16),
            in_specs=[IN_SMEM] * 4 + [IN_VMEM],
            out_specs=IN_VMEM,
            scratch_shapes=[pltpu.VMEM((tally.shape[0], pairs // 2, rows, sites), BF16)],
            compiler_params=GRANT,
            name="tie",
        )(*plan, parts)
    ends = jnp.stack([label.reshape(groups, -1)[:, 0], label.reshape(groups, -1)[:, -1]], axis=1)
    parts = parts.astype(F32).reshape(groups, 2, -1, rows, sites)
    member = (ends[:, :, None] == jnp.arange(tally.shape[0])).astype(F32)
    totals = jnp.einsum("stf,sthij->fhij", member, parts, precision=lax.Precision.HIGHEST)
    return masked_softmax(totals, tally)[ends].reshape(groups, pairs, rows, sites)


def mix_kernel(me_ref, label_ref, starts_ref, tally_ref, shared, inner, values, out, weights):
    heads, sites = shared.shape[1] // 2, values.shape[2]
    lines, chips = values.shape[0], out.shape[0]
    place = sites // chips
    for index in range(2 * heads):
        weights[index] = shared[:, index].reshape(sites, sites)
    weights[2 * heads :] = inner[...]
    mixed = []
    for line in range(lines):
        slot = slot_of(label_ref, me_ref[0] * lines, lines, line)
        value = values[line]
        mixed.append(
            [
                lax.dot_general(
                    weights[slot * heads + head],
                    value[head * HEAD_SIZE : (head + 1) * HEAD_SIZE],
                    CONTRACT_LAST,
                    preferred_element_type=F32,
                )
                for head in range(heads)
            ]
        )
    pairs = [(part[0], part[1]) for part in mixed]
    pairs += [(mixed[line][2], mixed[line + lines // 2][2]) for line in range(lines // 2)]
    for index in range(0, len(pairs), 2):
        block = [
            jnp.concatenate(pair, axis=1).reshape(chips, place, 2 * HEAD_SIZE)
            for pair in pairs[index : index + 2]
        ]
        out[:, index * place : (index + 2) * place] = jnp.concatenate(block, axis=1).astype(BF16)


def mix(shared, inner, values, plan, chips):
    groups, pairs, rows, sites = shared.shape
    lines, quarter, _ = values.shape
    place = sites // chips
    if rows % 16 == 0 and place % 8 == 0:
        shape = (chips, 3 * lines * place // 2, 2 * HEAD_SIZE)
        return pl.pallas_call(
            mix_kernel,
            out_shape=jax.ShapeDtypeStruct(shape, BF16),
            in_specs=[IN_SMEM] * 4 + [IN_VMEM] * 3,
            out_specs=IN_VMEM,
            scratch_shapes=[pltpu.VMEM((pairs + inner.shape[0], sites, sites), BF16)],
            compiler_params=GRANT,
            name="mix",
        )(*plan, shared, inner, values)
    me, label = plan[:2]
    label = lax.dynamic_slice_in_dim(label, me[0] * lines, lines)
    slot = slot_of(label, 0, lines, jnp.arange(lines))
    ends = jnp.transpose(shared, (1, 0, 2, 3)).reshape(2, pairs // 2, sites, sites)
    weights = jnp.concatenate([ends, inner.reshape(-1, *ends.shape[1:])])[slot]
    values = values.reshape(lines, -1, HEAD_SIZE, sites)
    mixed = jnp.einsum("rhdj,rhij->rihd", values, weights, preferred_element_type=F32)
    mixed = mixed.astype(BF16).reshape(lines, chips, place, quarter)
    return jnp.transpose(mixed, (1, 0, 2, 3)).reshape(chips, lines * place, quarter)


def project_kernel(me_ref, blocks, mixing, piece, kept, *refs):
    sent = refs[:PARTS]
    wide, first, second, semaphores = refs[PARTS:]
    chips, count, lanes = blocks.shape
    quarter, model = mixing.shape
    tokens = count * 2 // 3
    groups, own = chips // 2, tokens // 2
    chip, core = me_ref[1], me_ref[2]
    start = piece.shape[0] - quarter
    tail = quarter - lanes
    first[...] = jnp.zeros_like(first)
    second[...] = jnp.zeros_like(second)
    copies = []
    for index, (source, place, side) in enumerate(((mixing, 0, chip), (piece, start, 1 - chip))):
        spot = pl.multiple_of(side * lanes, lanes)
        end = source.at[pl.ds(place + lanes, tail)]
        moves = (
            (source.at[pl.ds(place, lanes)], wide.at[pl.ds(spot, lanes)]),
            (end, first.at[pl.ds(spot, tail)]),
            (end, second.at[pl.ds(pl.multiple_of(spot + tail, tail), tail)]),
        )
        for number, (origin, target) in enumerate(moves):
            copies.append(
                pltpu.make_async_copy(origin, target, semaphores.at[3 * index + number])
            )
    for copy in copies:
        copy.start()
    values = blocks[...].reshape(groups, 2, count, lanes)
    values = jnp.concatenate([values[:, 0], values[:, 1]], axis=-1)
    whole = values[:, :tokens].reshape(groups * tokens, 2 * lanes)
    narrow = values[:, tokens:].reshape(groups * own, 2 * lanes)
    for copy in copies:
        copy.wait()
    total = jnp.dot(whole, wide[...], preferred_element_type=F32)
    total = total.reshape(groups, tokens, model)
    ends = [
        jnp.dot(narrow, weights[...], preferred_element_type=F32).reshape(groups, own, model)
        for weights in (first, second)
    ]
    halves = [total[:, :own] + ends[0], total[:, own:] + ends[1]]
    for index in range(2):

        @pl.when(core == index)
        def _(index=index):
            kept[...] = halves[index]
            for number, part in enumerate(sent):
                lower = number * groups // PARTS
                part[...] = halves[1 - index][lower : lower + groups // PARTS].astype(BF16)


def project(blocks, mixing, piece, me, lines):
    chips, count, lanes = blocks.shape
    quarter, model = mixing.shape
    groups = chips // 2
    if lanes != quarter:
        out = (groups, count // 3, model)
        return pl.pallas_call(
            project_kernel,
            out_shape=(jax.ShapeDtypeStruct(out, F32),)
            + (jax.ShapeDtypeStruct((groups // PARTS, *out[1:]), BF16),) * PARTS,
            in_specs=[IN_SMEM, IN_VMEM, IN_HBM, IN_HBM],
            out_specs=(IN_VMEM,) * (1 + PARTS),
            scratch_shapes=[pltpu.VMEM((2 * lanes, model), BF16)] * 3
            + [pltpu.SemaphoreType.DMA((6,))],
            compiler_params=GRANT,
            name="project",
        )(me, blocks, mixing, piece)
    weights = in_order(mixing[None], piece[None, -quarter:], me[1], 0)
    values = blocks.reshape(groups, 2, 2, count // 2, quarter)
    partial = jnp.einsum("gxctd,xde->cgte", values, weights, preferred_element_type=F32)
    kept = lax.dynamic_index_in_dim(partial, me[2], 0, False)
    sent = lax.dynamic_index_in_dim(partial, 1 - me[2], 0, False)
    return kept, *jnp.split(sent.astype(BF16), PARTS)


def arrive_kernel(kept, *refs):
    got, blocks = refs[:PARTS], refs[PARTS]
    normed, (stream, tokens) = refs[PARTS + 1 : 2 * PARTS + 1], refs[2 * PARTS + 1 :]
    groups, own, model = kept.shape
    places, rows, _ = stream.shape
    count, lanes = blocks.shape[1], blocks.shape[2]
    heads = blocks.shape[0] // groups
    parts = count // 3
    for group in range(groups):
        each = groups // PARTS
        total = kept[group] + got[group // each][group % each].astype(F32)
        features = []
        for head in range(heads):
            block = blocks[group * heads + head].astype(F32)
            narrow = block[2 * parts :]
            narrow = jnp.concatenate([narrow[:, : lanes // 2], narrow[:, lanes // 2 :]], axis=0)
            features += [block[: 2 * parts], narrow]
        values = total + jnp.concatenate(features, axis=1)
        for index in range(tokens.shape[0]):
            lower = index * tokens.shape[2]
            part = values[:, lower : lower + tokens.shape[2]]
            tokens[index, group * own : (group + 1) * own] = part
    for place in range(places):
        values = [
            tokens[index, pl.ds(place, rows, stride=places), :] for index in range(tokens.shape[0])
        ]
        values = jnp.concatenate(values, axis=-1).astype(BF16)
        stream[place] = values
        values = values.astype(F32)
        centred = values - jnp.mean(values, axis=-1, keepdims=True)
        variance = jnp.mean(centred * centred, axis=-1, keepdims=True)
        each = places // PARTS
        normed[place // each][place % each] = (centred * lax.rsqrt(variance + 1e-05)).astype(BF16)


def arrive(kept, got, blocks, place):
    groups, own, model = kept.shape
    rows = groups * own // place
    if place % 8 == 0:
        shape = jax.ShapeDtypeStruct((place, rows, model), BF16)
        part = jax.ShapeDtypeStruct((place // PARTS, rows, model), BF16)
        return pl.pallas_call(
            arrive_kernel,
            out_shape=(part,) * PARTS + (shape,),
            in_specs=[IN_VMEM] * (2 + PARTS),
            out_specs=(IN_VMEM,) * (1 + PARTS),
            scratch_shapes=[pltpu.VMEM((model // 128, groups * own, 128), F32)],
            compiler_params=GRANT,
            name="arrive",
        )(kept, *got, blocks)
    heads = blocks.shape[0] // groups
    stream = jnp.transpose(blocks.reshape(groups, heads, own, -1), (0, 2, 1, 3))
    stream = stream.reshape(groups, own, model).astype(F32) + kept
    stream += jnp.concatenate(got).astype(F32)
    stream = jnp.transpose(stream.reshape(rows, place, model), (1, 0, 2)).astype(BF16)
    normed = own_norm(stream, -1)
    return *jnp.split(normed, PARTS, axis=0 if place % PARTS == 0 else 1), stream


def column_kernel(
    lines, me_ref, starts_ref, *refs
):
    tokens = refs[: 2 * PARTS]
    triple, mixing, piece, rest, kept, sent = refs[2 * PARTS : 2 * PARTS + 6]
    normed, far, projected, mixed, semaphores = refs[2 * PARTS + 6 :]
    quarter = mixing.shape[0]
    core, pair = me_ref[2], me_ref[3]
    half = rest.shape[0]

    def spot(index):
        return far.at[pl.ds(pl.multiple_of(index * half, half), half)]

    moves = (
        (piece.at[pl.ds(half, half)], spot(pair)),
        (rest, spot(1 - pair)),
    )
    copies = [
        pltpu.make_async_copy(source, target, semaphores.at[index])
        for index, (source, target) in enumerate(moves)
    ]
    for copy in copies:
        copy.start()
    places, both, model = normed.shape
    rows = both // 2
    count, width = tokens[0].shape[:2]
    for index, values in enumerate(tokens):
        part, lower = index % PARTS, index // PARTS * rows
        start = part * count if count < places else 0
        lower += 0 if count < places else part * width
        normed[start : start + count, lower : lower + width] = values[...]
    flat = normed[...].reshape(places * both, model)

    def families(axis):
        shape = (both, 1) if axis == 0 else (1, both)
        index = lax.broadcasted_iota(jnp.int32, shape, axis)
        line = jnp.where(index < rows, core * lines, (1 - core) * lines)
        index = jnp.where(index < rows, index, index - rows)
        line += index // lines * (2 * lines) + index % lines
        return sum(
            (line >= starts_ref[family]).astype(jnp.int32)
            for family in range(1, starts_ref.shape[0] - 1)
        )

    same = families(0) == families(1)
    scale = HEAD_SIZE**-0.5

    def attend(weights, lower):
        projected[...] = lax.dot_general(
            weights, flat, CONTRACT_LAST, preferred_element_type=F32
        ).astype(BF16)
        heads = quarter // HEAD_SIZE
        jobs = [(place, head) for place in range(places) for head in range(heads)]
        group = min(len(jobs), max(1, 12 * 128 // both))
        for first in range(0, len(jobs), group):
            batch = jobs[first : first + group]
            scores = []
            for place, head in batch:
                lanes = slice(place * both, (place + 1) * both)
                features = slice(head * HEAD_SIZE, (head + 1) * HEAD_SIZE)
                queries = projected[:quarter, lanes][features]
                keys = projected[quarter : 2 * quarter, lanes][features]
                scores.append(
                    lax.dot_general(keys, queries, CONTRACT_FIRST, preferred_element_type=F32)
                )
            scores = [jnp.where(same, part * scale, -jnp.inf) for part in scores]
            scores = [jnp.exp(part - jnp.max(part, axis=0, keepdims=True)) for part in scores]
            totals = [jnp.sum(part, axis=0, keepdims=True) for part in scores]
            scores = [part.astype(BF16) for part in scores]
            results = []
            for (place, head), part in zip(batch, scores):
                lanes = slice(place * both, (place + 1) * both)
                features = slice(head * HEAD_SIZE, (head + 1) * HEAD_SIZE)
                values = projected[2 * quarter :, lanes][features]
                results.append(jnp.dot(values, part, preferred_element_type=F32))
            for (place, head), part, total in zip(batch, results, totals):
                lanes = slice(place * both, (place + 1) * both)
                target = slice(lower + head * HEAD_SIZE, lower + (head + 1) * HEAD_SIZE)
                mixed[target, lanes] = (part / total).astype(BF16)

    attend(triple[...], 0)
    for copy in copies:
        copy.wait()
    attend(far[: 3 * quarter], quarter)
    for place in range(places):
        lanes = slice(place * both, (place + 1) * both)
        partial = lax.dot_general(
            mixed[:quarter, lanes], mixing[...], CONTRACT_FIRST, preferred_element_type=F32
        )
        partial += lax.dot_general(
            mixed[quarter:, lanes], far[3 * quarter :], CONTRACT_FIRST, preferred_element_type=F32
        )
        kept[place] = partial[:rows]
        sent[place] = partial[rows:].astype(BF16)


def column(own, other, triple, mixing, piece, rest, plan, lines, shape):
    places, rows, model = shape
    quarter = mixing.shape[0]
    tokens = 2 * places * rows
    return pl.pallas_call(
        functools.partial(column_kernel, lines),
        out_shape=(
            jax.ShapeDtypeStruct(shape, F32),
            jax.ShapeDtypeStruct(shape, BF16),
        ),
        in_specs=[IN_SMEM] * 2 + [IN_VMEM] * (2 * PARTS + 2) + [IN_HBM] * 2,
        out_specs=(IN_VMEM, IN_VMEM),
        scratch_shapes=[
            pltpu.VMEM((places, 2 * rows, model), BF16),
            pltpu.VMEM((4 * quarter, model), BF16),
            pltpu.VMEM((3 * quarter, tokens), BF16),
            pltpu.VMEM((2 * quarter, tokens), BF16),
            pltpu.SemaphoreType.DMA((2,)),
        ],
        compiler_params=GRANT,
        name="column",
    )(plan[0], plan[2], *own, *other, triple.reshape(-1, model), mixing, piece, rest)


def finish_kernel(stream, kept, got, out):
    places, rows, model = stream.shape
    parts, wide = out.shape[1] // 3, out.shape[2]
    quarter = wide // 2 * 3
    heads = model // quarter
    groups = out.shape[0] // heads
    lines = rows // groups
    for group in range(groups):
        these = slice(group * lines, (group + 1) * lines)
        total = stream[:, these].astype(F32) + kept[:, these] + got[:, these].astype(F32)
        total = total.reshape(places * lines, model)
        for head in range(heads):
            block = total[:, head * quarter : (head + 1) * quarter]
            narrow = jnp.concatenate([block[:parts, wide:], block[parts:, wide:]], axis=1)
            block = jnp.concatenate([block[:, :wide], narrow], axis=0)
            out[group * heads + head] = block.astype(BF16)


def finish(stream, kept, got, groups, quarter):
    places, rows, model = stream.shape
    heads, lines = model // quarter, rows // groups
    parts, wide = places * lines // 2, quarter // 3 * 2
    shape = (groups * heads, 3 * parts, wide)
    if parts % 16 == 0 and lines % 8 == 0:
        return pl.pallas_call(
            finish_kernel,
            out_shape=jax.ShapeDtypeStruct(shape, BF16),
            in_specs=[IN_VMEM] * 3,
            out_specs=IN_VMEM,
            compiler_params=GRANT,
            name="finish",
        )(stream, kept, got)
    total = (stream.astype(F32) + kept + got.astype(F32)).astype(BF16)
    total = total.reshape(places, groups, lines, heads, quarter)
    total = jnp.transpose(total, (1, 3, 0, 2, 4)).reshape(-1, places * lines, quarter)
    narrow = jnp.concatenate([total[:, :parts, wide:], total[:, parts:, wide:]], axis=2)
    return jnp.concatenate([total[:, :, :wide], narrow], axis=1)


def feed_forward_kernel(
    me_ref, normed, expand, contract, piece, pair_rest, plane_rest, late, out,
    far_expand, far_contract, hidden, semaphores,
):
    width = expand.shape[1]
    count, half = pair_rest.shape[0], width // 2
    pair, plane = me_ref[3], me_ref[4]

    def move(source, start, count, target, place, index):
        return pltpu.make_async_copy(
            source.at[pl.ds(start, count)], target.at[pl.ds(place, count)], semaphores.at[index]
        )

    def by_pair(first, second):
        return [
            move(piece, 0, count, first, 0, 2),
            move(pair_rest, 0, count, second, 0, 3),
        ]

    def by_plane(first, second):
        return [
            move(piece, count, count, first, count, 4),
            move(plane_rest, 0, count, second, count, 5),
        ]

    copies = [
        move(late, 0, half, far_expand, half, 0),
        move(late, half, half, far_contract, half, 1),
    ]
    for copy in copies:
        copy.start()
    for place, moves in ((pair, by_pair), (plane, by_plane)):

        @pl.when(place == 0)
        def _(moves=moves):
            for copy in moves(far_expand, far_contract):
                copy.start()

        @pl.when(place != 0)
        def _(moves=moves):
            for copy in moves(far_contract, far_expand):
                copy.start()

    tile = width // 3
    values = normed[...]

    def raise_by(weights, lower):
        for start in range(0, width, tile):
            up = jnp.dot(values, weights[:, start : start + tile], preferred_element_type=F32)
            up = 0.5 * up * (1.0 + lax.erf(up * 2.0**-0.5))
            hidden[:, lower + start : lower + start + tile] = up.astype(BF16)

    copies += by_pair(far_expand, far_contract) + by_plane(far_expand, far_contract)
    raise_by(expand, 0)
    for copy in copies:
        copy.wait()
    raise_by(far_expand, width)
    down = jnp.dot(hidden[:, :width], contract[...], preferred_element_type=F32)
    down += jnp.dot(hidden[:, width:], far_contract[...], preferred_element_type=F32)
    out[...] = down.astype(out.dtype)


def feed_forward(normed, expand, contract, pieces, me, kind):
    places, rows, model = normed.shape
    tokens, width = places * rows, expand.shape[1]
    result = pl.pallas_call(
        feed_forward_kernel,
        out_shape=jax.ShapeDtypeStruct((tokens, model), kind),
        in_specs=[IN_SMEM] + [IN_VMEM] * 3 + [IN_HBM] * 4,
        out_specs=IN_VMEM,
        scratch_shapes=[
            pltpu.VMEM((model, width), BF16),
            pltpu.VMEM((width, model), BF16),
            pltpu.VMEM((tokens, 2 * width), BF16),
            pltpu.SemaphoreType.DMA((6,)),
        ],
        compiler_params=GRANT,
        name="feed_forward",
    )(me, normed.reshape(tokens, model), expand, contract, *pieces)
    return result.reshape(normed.shape)


def renew_kernel(stream, kept, got, after, normed):
    total = (stream[...].astype(F32) + kept[...] + got[...].astype(F32)).astype(BF16)
    after[...] = total
    values = total.astype(F32)
    centred = values - jnp.mean(values, axis=-1, keepdims=True)
    variance = jnp.mean(centred * centred, axis=-1, keepdims=True)
    normed[...] = (centred * lax.rsqrt(variance + 1e-05)).astype(BF16)


def renew(stream, kept, got):
    return pl.pallas_call(
        renew_kernel,
        out_shape=(jax.ShapeDtypeStruct(stream.shape, BF16),) * 2,
        in_specs=[IN_VMEM] * 3,
        out_specs=(IN_VMEM, IN_VMEM),
        compiler_params=GRANT,
        name="renew",
    )(stream, kept, got)


def shards(
    alignment_embedding,
    line_group_label,
    group_site_tally,
    horizontal_triple_matrix,
    horizontal_mixing_matrix,
    vertical_triple_matrix,
    vertical_mixing_matrix,
    expand_matrix,
    contract_matrix,
):
    lines, quarter, sites = alignment_embedding.shape
    row_groups = lax.axis_size(ROWS)
    own = lines // 2
    chips = 2 * row_groups
    place = sites // chips
    pair = lax.axis_index("pair")
    chip = lax.axis_index("chip")
    core = lax.axis_index("core")
    label, tally = line_group_label, group_site_tally
    families = tally.shape[0]
    starts = jnp.sum(label[:, None] < jnp.arange(families + 1), axis=0, dtype=jnp.int32)
    plane = lax.axis_index("plane")
    me = jnp.stack([lax.axis_index(ROWS), chip, core, pair, plane]).astype(jnp.int32)

    across = other_chip(alignment_embedding)
    near = other_core(alignment_embedding)
    pack, late = pack_weights(
        me,
        horizontal_mixing_matrix,
        vertical_triple_matrix,
        vertical_mixing_matrix,
        expand_matrix,
        contract_matrix,
    )
    stream, pack, late = lax.optimization_barrier((alignment_embedding, pack, late))
    stream = spread(stream, chips)
    stream = lax.all_to_all(stream, ROWS + ("chip", "core"), 0, 0, tiled=True)
    across, near, pack, late, starts, me = lax.optimization_barrier(
        (across, near, pack, late, starts, me)
    )
    plan = (me, label, starts, tally)
    piece = other_chip(pack)

    shared, inner_weights, values = row_front(
        (alignment_embedding, near, across, other_core(across)),
        horizontal_triple_matrix,
        plan,
        2 + max(min(families, lines) - 2, 1),
        row_groups,
    )
    shared, stream = lax.optimization_barrier((shared, stream))
    parts = lax.all_to_all(shared, ROWS, 0, 0, tiled=True)
    shared = lax.all_to_all(tie(parts, plan), ROWS, 0, 0, tiled=True)
    blocks = mix(shared, inner_weights, values, plan, chips)

    blocks, piece, late = lax.optimization_barrier((blocks, piece, late))
    half = expand_matrix.shape[0] // 2
    column_rest = other_pair(piece[half : 2 * half])
    feed_rest = (other_pair(piece[:quarter]), other_plane(piece[quarter:half]))
    late = other_chip(late)
    blocks = lax.all_to_all(blocks, ROWS + ("chip",), 0, 0, tiled=True)
    kept, *sent = project(blocks, horizontal_mixing_matrix, piece, me, lines)
    got = [other_core(part) for part in sent]
    got, column_rest = lax.optimization_barrier((got, column_rest))
    *normed, after_row = arrive(kept, got, stream, place)
    other = [other_core(part) for part in normed]

    kept, sent = column(
        normed,
        other,
        vertical_triple_matrix,
        vertical_mixing_matrix,
        piece,
        column_rest,
        plan,
        own,
        after_row.shape,
    )
    sent, feed_rest, late = lax.optimization_barrier((sent, feed_rest, late))
    after_col, normed = renew(after_row, kept, other_core(sent))

    weights = (expand_matrix, contract_matrix, (piece, *feed_rest, late), me)
    kept = feed_forward(normed, *weights, F32)
    sent = feed_forward(other_core(normed), *weights, BF16)
    blocks = finish(after_col, kept, other_core(sent), row_groups, quarter)

    blocks = lax.all_to_all(blocks, ROWS + ("chip", "core"), 0, 0, tiled=True)
    parts, wide = own * place // 2, quarter // 3 * 2
    narrow = blocks[:, 2 * parts :]
    narrow = jnp.concatenate([narrow[:, :, : wide // 2], narrow[:, :, wide // 2 :]], axis=1)
    finished = jnp.concatenate([blocks[:, : 2 * parts], narrow], axis=2)
    finished = finished.reshape(chips, 2, place, own, quarter)
    finished = jnp.transpose(finished, (1, 3, 4, 0, 2))
    return finished.reshape(lines, quarter, sites)


def solution(mesh):
    far = mesh.shape["rows"] // 4
    split = Mesh(mesh.devices.reshape(far, 2, 2, 2, 2), ROWS + ("chip", "core"))
    heads = ("chip", "core")
    placed = (
        P(ROWS, heads, None),
        P(),
        P(),
        P(None, heads, None),
        P(heads, None),
        P(None, heads, None),
        P(heads, None),
        P(None, heads),
        P(heads, None),
    )
    return jax.shard_map(
        shards, mesh=split, in_specs=placed, out_specs=P(ROWS, heads, None), check_vma=False
    )
```

```python
import functools

import jax
import jax.numpy as jnp
from jax import lax
from jax.experimental import pallas as pl
from jax.experimental.pallas import tpu as pltpu
from jax.sharding import Mesh, PartitionSpec as P

HEAD_SIZE = 64
SWAP = [(0, 1), (1, 0)]
ROWS = ("far", "plane", "pair")
PARTS = 4
BF16 = jnp.bfloat16
F32 = jnp.float32


def other_chip(value):
    return lax.ppermute(value, "chip", SWAP)


def other_pair(value):
    return lax.ppermute(value, "pair", SWAP)


def other_plane(value):
    return lax.ppermute(value, "plane", SWAP)


def other_core(value):
    return lax.ppermute(value, "core", SWAP)


def in_order(first, second, index, axis):
    forward = jnp.concatenate([first, second], axis=axis)
    backward = jnp.concatenate([second, first], axis=axis)
    return jnp.where(index == 0, forward, backward)


def half_rows(value, index):
    rows = value.shape[0] // 2
    return lax.dynamic_slice_in_dim(value, index * rows, rows)


def own_norm(values, axis):
    values = values.astype(F32)
    average = jnp.mean(values, axis=axis, keepdims=True)
    centred = values - average
    variance = jnp.mean(centred * centred, axis=axis, keepdims=True)
    return (centred * lax.rsqrt(variance + 1e-05)).astype(BF16)


def masked_softmax(tables, tally):
    live = jnp.arange(tables.shape[-1])[None, :] < tally[:, None]
    tables = jnp.where(live[:, None, None, :], tables, -jnp.inf)
    return jax.nn.softmax(tables, axis=-1).astype(BF16)


CONTRACT_FIRST = (((0,), (0,)), ((), ()))
CONTRACT_LAST = (((1,), (1,)), ((), ()))
IN_VMEM = pl.BlockSpec(memory_space=pltpu.VMEM)
IN_SMEM = pl.BlockSpec(memory_space=pltpu.SMEM)
IN_HBM = pl.BlockSpec(memory_space=pltpu.HBM)
GRANT = pltpu.CompilerParams(vmem_limit_bytes=40 * 2**20)


def slot_of(label_ref, start, lines, line):
    first, last = label_ref[start], label_ref[start + lines - 1]
    family = label_ref[start + line]
    return jnp.where(family == first, 0, jnp.where(family == last, 1, family - first + 1))


def quarter_spots(me_ref):
    chip, core = me_ref[1], me_ref[2]
    return (
        2 * chip + core, 2 * chip + 1 - core, 2 * (1 - chip) + core, 2 * (1 - chip) + 1 - core
    )


def pack_kernel(me_ref, mixing, triple, vertical, expand, contract, pack, late, semaphores):
    quarter = mixing.shape[0]
    half, pair, plane = 2 * quarter, me_ref[3], me_ref[4]

    def move(index, source, start, count, target, place):
        return pltpu.make_async_copy(
            source.at[pl.ds(start, count)], target.at[pl.ds(place, count)], semaphores.at[index]
        )

    fixed = [
        move(0, mixing, 0, quarter, pack, 2 * half),
        move(1, expand, half, half, late, 0),
        move(2, contract, half, half, late, half),
    ]
    by_pair = (
        [
            move(3, expand, 0, quarter, pack, 0),
            move(4, triple, 0, quarter, pack, half),
            move(5, triple, quarter, quarter, pack, half + quarter),
        ],
        [
            move(3, contract, 0, quarter, pack, 0),
            move(4, triple, half, quarter, pack, half),
            move(5, vertical, 0, quarter, pack, half + quarter),
        ],
    )
    by_plane = (
        [move(6, expand, quarter, quarter, pack, quarter)],
        [move(6, contract, quarter, quarter, pack, quarter)],
    )
    for copy in fixed:
        copy.start()
    for index in range(2):
        for place, options in ((pair, by_pair), (plane, by_plane)):

            @pl.when(place == index)
            def _(copies=options[index]):
                for copy in copies:
                    copy.start()

    for copy in fixed + by_pair[0] + by_plane[0]:
        copy.wait()


def pack_weights(me, mixing, triple, vertical, expand, contract):
    quarter, model = mixing.shape
    return pl.pallas_call(
        pack_kernel,
        out_shape=(
            jax.ShapeDtypeStruct((5 * quarter, model), BF16),
            jax.ShapeDtypeStruct((4 * quarter, model), BF16),
        ),
        in_specs=[IN_SMEM] + [IN_HBM] * 5,
        out_specs=(IN_HBM, IN_HBM),
        scratch_shapes=[pltpu.SemaphoreType.DMA((7,))],
        compiler_params=GRANT,
        name="pack",
    )(me, mixing, triple.reshape(-1, model), vertical, expand, contract)


def spread_kernel(stream, out):
    lines, quarter, sites = stream.shape
    chips = out.shape[0] // 2
    place, own = sites // chips, lines // 2
    wide = out.shape[2]
    for core in range(2):
        values = [stream[core * own + line].astype(F32).T for line in range(own)]
        values = [value.reshape(chips, place, quarter) for value in values]
        values = jnp.concatenate(values, axis=1)
        parts = own * place // 2
        narrow = jnp.concatenate([values[:, :parts, wide:], values[:, parts:, wide:]], axis=2)
        values = jnp.concatenate([values[:, :, :wide], narrow], axis=1).astype(BF16)
        for chip in range(chips):
            out[2 * chip + core] = values[chip]


def spread(stream, chips):
    lines, quarter, sites = stream.shape
    place, own = sites // chips, lines // 2
    if place % 8 == 0:
        shape = (2 * chips, 3 * own * place // 2, quarter // 3 * 2)
        return pl.pallas_call(
            spread_kernel,
            out_shape=jax.ShapeDtypeStruct(shape, BF16),
            in_specs=[IN_VMEM],
            out_specs=IN_VMEM,
            compiler_params=GRANT,
            name="spread",
        )(stream)
    stream = jnp.transpose(stream.reshape(2, own, quarter, chips, place), (3, 0, 1, 4, 2))
    return stream.reshape(2 * chips, own * place, quarter)


def row_front_kernel(
    lines, me_ref, label_ref, starts_ref, tally_ref, own, near, far, diagonal, triple,
    table_ref, inner_ref, value_ref, tables, normed,
):
    step = pl.program_id(0)
    group, quarter, sites = own.shape
    heads = quarter // HEAD_SIZE

    @pl.when(step == 0)
    def _():
        tables[...] = jnp.zeros_like(tables)

    pieces = []
    for ref in (own, near, far, diagonal):
        lanes = jnp.concatenate([ref[line] for line in range(group)], axis=-1)
        pieces.append(lanes.astype(F32))
    size = 4 * quarter
    average = sum(jnp.sum(piece, axis=0, keepdims=True) for piece in pieces) / size
    pieces = [piece - average for piece in pieces]
    variance = sum(jnp.sum(piece * piece, axis=0, keepdims=True) for piece in pieces) / size
    inverse = lax.rsqrt(variance + 1e-05)
    for spot, piece in zip(quarter_spots(me_ref), pieces):
        spot = pl.multiple_of(spot * quarter, quarter)
        normed[pl.ds(spot, quarter), :] = (piece * inverse).astype(BF16)
    projected = jnp.dot(triple[...], normed[...], preferred_element_type=F32).astype(BF16)
    base = me_ref[0] * lines
    jobs = []
    for line in range(group):
        part = projected[:, line * sites : (line + 1) * sites]
        value_ref[line] = part[2 * quarter :]
        place = step * group + line
        slot = slot_of(label_ref, base, lines, place)
        family = label_ref[base + place]
        members = jnp.full((1, sites), starts_ref[family + 1] - starts_ref[family], jnp.int32)
        scale = HEAD_SIZE**-0.5 * lax.rsqrt(members.astype(F32))
        for head in range(heads):
            lower = head * HEAD_SIZE
            queries = part[lower : lower + HEAD_SIZE]
            keys = part[quarter + lower : quarter + lower + HEAD_SIZE]
            logits = lax.dot_general(queries, keys, CONTRACT_FIRST, preferred_element_type=F32)
            jobs.append((slot * heads + head, logits, scale))
    for index, logits, scale in jobs:
        tables[index] += logits * scale

    @pl.when(step == pl.num_programs(0) - 1)
    def _():
        for index in range(2 * heads):
            table = tables[index].astype(BF16)
            if len(table_ref.shape) == 4:
                groups, _, rows, _ = table_ref.shape
                table_ref[:, index] = table.reshape(groups, rows, sites)
            else:
                table_ref[index] = table
        site = lax.broadcasted_iota(jnp.int32, (sites, sites), 1)

        def inner(index, carry):
            table = tables[2 * heads + index]
            family = label_ref[base] + 1 + index // heads
            family = jnp.minimum(family, tally_ref.shape[0] - 1)
            table = jnp.where(site < tally_ref[family], table, -jnp.inf)
            table = jnp.exp(table - jnp.max(table, axis=-1, keepdims=True))
            table = table / jnp.sum(table, axis=-1, keepdims=True)
            inner_ref[index] = table.astype(BF16)
            return carry

        lax.fori_loop(0, inner_ref.shape[0], inner, 0)


def row_front(pieces, triple, plan, slots, row_groups):
    lines, quarter, sites = pieces[0].shape
    group = 4
    heads = quarter // HEAD_SIZE
    inner = slots - 2
    rows = sites // row_groups
    shape = (row_groups, 2 * heads, rows, sites) if rows % 16 == 0 else (2 * heads, sites, sites)
    block = pl.BlockSpec((group, quarter, sites), lambda step: (step, 0, 0))

    def whole(shape):
        return pl.BlockSpec(shape, lambda step: (0,) * len(shape))

    tables, inner_weights, values = pl.pallas_call(
        functools.partial(row_front_kernel, lines),
        grid=(lines // group,),
        out_shape=(
            jax.ShapeDtypeStruct(shape, BF16),
            jax.ShapeDtypeStruct((inner * heads, sites, sites), BF16),
            jax.ShapeDtypeStruct((lines, quarter, sites), BF16),
        ),
        in_specs=[IN_SMEM] * 4 + [block] * 4 + [whole((3 * quarter, 4 * quarter))],
        out_specs=(whole(shape), whole((inner * heads, sites, sites)), block),
        scratch_shapes=[
            pltpu.VMEM((slots * heads, sites, sites), F32),
            pltpu.VMEM((4 * quarter, group * sites), BF16),
        ],
        compiler_params=GRANT,
        name="row_front",
    )(*plan, *pieces, triple.reshape(3 * quarter, 4 * quarter))
    if rows % 16:
        tables = jnp.transpose(tables.reshape(-1, row_groups, rows, sites), (1, 0, 2, 3))
    return tables, inner_weights, values


def tie_kernel(me_ref, label_ref, starts_ref, tally_ref, parts, out, weights):
    groups, pairs, rows, sites = parts.shape
    lines = label_ref.shape[0] // groups
    ends = [label_ref[g * lines + e * (lines - 1)] for g in range(groups) for e in range(2)]
    heads = pairs // 2
    site = lax.broadcasted_iota(jnp.int32, (heads, rows, sites), 2)
    for family in range(weights.shape[0]):
        total = jnp.zeros((heads, rows, sites), F32)
        for group in range(groups):
            for end in range(2):
                part = parts[group, end * heads : (end + 1) * heads].astype(F32)
                total += jnp.where(ends[2 * group + end] == family, part, 0.0)
        total = jnp.where(site < tally_ref[family], total, -jnp.inf)
        total = jnp.exp(total - jnp.max(total, axis=-1, keepdims=True))
        total = total / jnp.sum(total, axis=-1, keepdims=True)
        weights[family] = total.astype(BF16)
    for group in range(groups):
        for end in range(2):
            chosen = weights[ends[2 * group + end]]
            out[group, end * heads : (end + 1) * heads] = chosen


def tie(parts, plan):
    groups, pairs, rows, sites = parts.shape
    _, label, _, tally = plan
    if rows % 16 == 0:
        return pl.pallas_call(
            tie_kernel,
            out_shape=jax.ShapeDtypeStruct(parts.shape, BF16),
            in_specs=[IN_SMEM] * 4 + [IN_VMEM],
            out_specs=IN_VMEM,
            scratch_shapes=[pltpu.VMEM((tally.shape[0], pairs // 2, rows, sites), BF16)],
            compiler_params=GRANT,
            name="tie",
        )(*plan, parts)
    ends = jnp.stack([label.reshape(groups, -1)[:, 0], label.reshape(groups, -1)[:, -1]], axis=1)
    parts = parts.astype(F32).reshape(groups, 2, -1, rows, sites)
    member = (ends[:, :, None] == jnp.arange(tally.shape[0])).astype(F32)
    totals = jnp.einsum("stf,sthij->fhij", member, parts, precision=lax.Precision.HIGHEST)
    return masked_softmax(totals, tally)[ends].reshape(groups, pairs, rows, sites)


def mix_kernel(me_ref, label_ref, starts_ref, tally_ref, shared, inner, values, out, weights):
    heads, sites = shared.shape[1] // 2, values.shape[2]
    lines, chips = values.shape[0], out.shape[0]
    place = sites // chips
    for index in range(2 * heads):
        weights[index] = shared[:, index].reshape(sites, sites)
    weights[2 * heads :] = inner[...]
    mixed = []
    for line in range(lines):
        slot = slot_of(label_ref, me_ref[0] * lines, lines, line)
        value = values[line]
        mixed.append(
            [
                lax.dot_general(
                    weights[slot * heads + head],
                    value[head * HEAD_SIZE : (head + 1) * HEAD_SIZE],
                    CONTRACT_LAST,
                    preferred_element_type=F32,
                )
                for head in range(heads)
            ]
        )
    pairs = [(part[0], part[1]) for part in mixed]
    pairs += [(mixed[line][2], mixed[line + lines // 2][2]) for line in range(lines // 2)]
    for index in range(0, len(pairs), 2):
        block = [
            jnp.concatenate(pair, axis=1).reshape(chips, place, 2 * HEAD_SIZE)
            for pair in pairs[index : index + 2]
        ]
        out[:, index * place : (index + 2) * place] = jnp.concatenate(block, axis=1).astype(BF16)


def mix(shared, inner, values, plan, chips):
    groups, pairs, rows, sites = shared.shape
    lines, quarter, _ = values.shape
    place = sites // chips
    if rows % 16 == 0 and place % 8 == 0:
        shape = (chips, 3 * lines * place // 2, 2 * HEAD_SIZE)
        return pl.pallas_call(
            mix_kernel,
            out_shape=jax.ShapeDtypeStruct(shape, BF16),
            in_specs=[IN_SMEM] * 4 + [IN_VMEM] * 3,
            out_specs=IN_VMEM,
            scratch_shapes=[pltpu.VMEM((pairs + inner.shape[0], sites, sites), BF16)],
            compiler_params=GRANT,
            name="mix",
        )(*plan, shared, inner, values)
    me, label = plan[:2]
    label = lax.dynamic_slice_in_dim(label, me[0] * lines, lines)
    slot = slot_of(label, 0, lines, jnp.arange(lines))
    ends = jnp.transpose(shared, (1, 0, 2, 3)).reshape(2, pairs // 2, sites, sites)
    weights = jnp.concatenate([ends, inner.reshape(-1, *ends.shape[1:])])[slot]
    values = values.reshape(lines, -1, HEAD_SIZE, sites)
    mixed = jnp.einsum("rhdj,rhij->rihd", values, weights, preferred_element_type=F32)
    mixed = mixed.astype(BF16).reshape(lines, chips, place, quarter)
    return jnp.transpose(mixed, (1, 0, 2, 3)).reshape(chips, lines * place, quarter)


def project_kernel(me_ref, blocks, mixing, piece, kept, *refs):
    sent = refs[:PARTS]
    wide, first, second, semaphores = refs[PARTS:]
    chips, count, lanes = blocks.shape
    quarter, model = mixing.shape
    tokens = count * 2 // 3
    groups, own = chips // 2, tokens // 2
    chip, core = me_ref[1], me_ref[2]
    start = piece.shape[0] - quarter
    tail = quarter - lanes
    first[...] = jnp.zeros_like(first)
    second[...] = jnp.zeros_like(second)
    copies = []
    for index, (source, place, side) in enumerate(((mixing, 0, chip), (piece, start, 1 - chip))):
        spot = pl.multiple_of(side * lanes, lanes)
        end = source.at[pl.ds(place + lanes, tail)]
        moves = (
            (source.at[pl.ds(place, lanes)], wide.at[pl.ds(spot, lanes)]),
            (end, first.at[pl.ds(spot, tail)]),
            (end, second.at[pl.ds(pl.multiple_of(spot + tail, tail), tail)]),
        )
        for number, (origin, target) in enumerate(moves):
            copies.append(
                pltpu.make_async_copy(origin, target, semaphores.at[3 * index + number])
            )
    for copy in copies:
        copy.start()
    values = blocks[...].reshape(groups, 2, count, lanes)
    values = jnp.concatenate([values[:, 0], values[:, 1]], axis=-1)
    whole = values[:, :tokens].reshape(groups * tokens, 2 * lanes)
    narrow = values[:, tokens:].reshape(groups * own, 2 * lanes)
    for copy in copies:
        copy.wait()
    total = jnp.dot(whole, wide[...], preferred_element_type=F32)
    total = total.reshape(groups, tokens, model)
    ends = [
        jnp.dot(narrow, weights[...], preferred_element_type=F32).reshape(groups, own, model)
        for weights in (first, second)
    ]
    halves = [total[:, :own] + ends[0], total[:, own:] + ends[1]]
    for index in range(2):

        @pl.when(core == index)
        def _(index=index):
            kept[...] = halves[index]
            for number, part in enumerate(sent):
                lower = number * groups // PARTS
                part[...] = halves[1 - index][lower : lower + groups // PARTS].astype(BF16)


def project(blocks, mixing, piece, me, lines):
    chips, count, lanes = blocks.shape
    quarter, model = mixing.shape
    groups = chips // 2
    if lanes != quarter:
        out = (groups, count // 3, model)
        return pl.pallas_call(
            project_kernel,
            out_shape=(jax.ShapeDtypeStruct(out, F32),)
            + (jax.ShapeDtypeStruct((groups // PARTS, *out[1:]), BF16),) * PARTS,
            in_specs=[IN_SMEM, IN_VMEM, IN_HBM, IN_HBM],
            out_specs=(IN_VMEM,) * (1 + PARTS),
            scratch_shapes=[pltpu.VMEM((2 * lanes, model), BF16)] * 3
            + [pltpu.SemaphoreType.DMA((6,))],
            compiler_params=GRANT,
            name="project",
        )(me, blocks, mixing, piece)
    weights = in_order(mixing[None], piece[None, -quarter:], me[1], 0)
    values = blocks.reshape(groups, 2, 2, count // 2, quarter)
    partial = jnp.einsum("gxctd,xde->cgte", values, weights, preferred_element_type=F32)
    kept = lax.dynamic_index_in_dim(partial, me[2], 0, False)
    sent = lax.dynamic_index_in_dim(partial, 1 - me[2], 0, False)
    return kept, *jnp.split(sent.astype(BF16), PARTS)


def arrive_kernel(kept, *refs):
    got, blocks = refs[:PARTS], refs[PARTS]
    normed, (stream, tokens) = refs[PARTS + 1 : 2 * PARTS + 1], refs[2 * PARTS + 1 :]
    groups, own, model = kept.shape
    places, rows, _ = stream.shape
    count, lanes = blocks.shape[1], blocks.shape[2]
    heads = blocks.shape[0] // groups
    parts = count // 3
    for group in range(groups):
        each = groups // PARTS
        total = kept[group] + got[group // each][group % each].astype(F32)
        features = []
        for head in range(heads):
            block = blocks[group * heads + head].astype(F32)
            narrow = block[2 * parts :]
            narrow = jnp.concatenate([narrow[:, : lanes // 2], narrow[:, lanes // 2 :]], axis=0)
            features += [block[: 2 * parts], narrow]
        values = total + jnp.concatenate(features, axis=1)
        for index in range(tokens.shape[0]):
            lower = index * tokens.shape[2]
            part = values[:, lower : lower + tokens.shape[2]]
            tokens[index, group * own : (group + 1) * own] = part
    for place in range(places):
        values = [
            tokens[index, pl.ds(place, rows, stride=places), :] for index in range(tokens.shape[0])
        ]
        values = jnp.concatenate(values, axis=-1).astype(BF16)
        stream[place] = values
        values = values.astype(F32)
        centred = values - jnp.mean(values, axis=-1, keepdims=True)
        variance = jnp.mean(centred * centred, axis=-1, keepdims=True)
        each = places // PARTS
        normed[place // each][place % each] = (centred * lax.rsqrt(variance + 1e-05)).astype(BF16)


def arrive(kept, got, blocks, place):
    groups, own, model = kept.shape
    rows = groups * own // place
    if place % 8 == 0:
        shape = jax.ShapeDtypeStruct((place, rows, model), BF16)
        part = jax.ShapeDtypeStruct((place // PARTS, rows, model), BF16)
        return pl.pallas_call(
            arrive_kernel,
            out_shape=(part,) * PARTS + (shape,),
            in_specs=[IN_VMEM] * (2 + PARTS),
            out_specs=(IN_VMEM,) * (1 + PARTS),
            scratch_shapes=[pltpu.VMEM((model // 128, groups * own + place, 128), F32)],
            compiler_params=GRANT,
            name="arrive",
        )(kept, *got, blocks)
    heads = blocks.shape[0] // groups
    stream = jnp.transpose(blocks.reshape(groups, heads, own, -1), (0, 2, 1, 3))
    stream = stream.reshape(groups, own, model).astype(F32) + kept
    stream += jnp.concatenate(got).astype(F32)
    stream = jnp.transpose(stream.reshape(rows, place, model), (1, 0, 2)).astype(BF16)
    normed = own_norm(stream, -1)
    return *jnp.split(normed, PARTS, axis=0 if place % PARTS == 0 else 1), stream


def column_kernel(
    lines, me_ref, starts_ref, *refs
):
    tokens = refs[: 2 * PARTS]
    triple, mixing, piece, rest, kept, sent = refs[2 * PARTS : 2 * PARTS + 6]
    normed, far, projected, mixed, semaphores = refs[2 * PARTS + 6 :]
    quarter = mixing.shape[0]
    core, pair = me_ref[2], me_ref[3]
    half = rest.shape[0]

    def spot(index):
        return far.at[pl.ds(pl.multiple_of(index * half, half), half)]

    moves = (
        (piece.at[pl.ds(half, half)], spot(pair)),
        (rest, spot(1 - pair)),
    )
    copies = [
        pltpu.make_async_copy(source, target, semaphores.at[index])
        for index, (source, target) in enumerate(moves)
    ]
    for copy in copies:
        copy.start()
    places, both, model = normed.shape
    rows = both // 2
    count, width = tokens[0].shape[:2]
    for index, values in enumerate(tokens):
        part, lower = index % PARTS, index // PARTS * rows
        start = part * count if count < places else 0
        lower += 0 if count < places else part * width
        normed[start : start + count, lower : lower + width] = values[...]
    flat = normed[...].reshape(places * both, model)

    def families(axis):
        shape = (both, 1) if axis == 0 else (1, both)
        index = lax.broadcasted_iota(jnp.int32, shape, axis)
        line = jnp.where(index < rows, core * lines, (1 - core) * lines)
        index = jnp.where(index < rows, index, index - rows)
        line += index // lines * (2 * lines) + index % lines
        return sum(
            (line >= starts_ref[family]).astype(jnp.int32)
            for family in range(1, starts_ref.shape[0] - 1)
        )

    same = families(0) == families(1)
    scale = HEAD_SIZE**-0.5

    def attend(weights, lower):
        projected[...] = lax.dot_general(
            weights, flat, CONTRACT_LAST, preferred_element_type=F32
        ).astype(BF16)
        heads = quarter // HEAD_SIZE
        jobs = [(place, head) for place in range(places) for head in range(heads)]
        group = min(len(jobs), max(1, 12 * 128 // both))
        for first in range(0, len(jobs), group):
            batch = jobs[first : first + group]
            scores = []
            for place, head in batch:
                lanes = slice(place * both, (place + 1) * both)
                features = slice(head * HEAD_SIZE, (head + 1) * HEAD_SIZE)
                queries = projected[:quarter, lanes][features]
                keys = projected[quarter : 2 * quarter, lanes][features]
                scores.append(
                    lax.dot_general(keys, queries, CONTRACT_FIRST, preferred_element_type=F32)
                )
            scores = [jnp.where(same, part * scale, -jnp.inf) for part in scores]
            scores = [jnp.exp(part - jnp.max(part, axis=0, keepdims=True)) for part in scores]
            totals = [jnp.sum(part, axis=0, keepdims=True) for part in scores]
            scores = [part.astype(BF16) for part in scores]
            results = []
            for (place, head), part in zip(batch, scores):
                lanes = slice(place * both, (place + 1) * both)
                features = slice(head * HEAD_SIZE, (head + 1) * HEAD_SIZE)
                values = projected[2 * quarter :, lanes][features]
                results.append(jnp.dot(values, part, preferred_element_type=F32))
            for (place, head), part, total in zip(batch, results, totals):
                lanes = slice(place * both, (place + 1) * both)
                target = slice(lower + head * HEAD_SIZE, lower + (head + 1) * HEAD_SIZE)
                mixed[target, lanes] = (part / total).astype(BF16)

    attend(triple[...], 0)
    for copy in copies:
        copy.wait()
    attend(far[: 3 * quarter], quarter)
    for place in range(places):
        lanes = slice(place * both, (place + 1) * both)
        partial = lax.dot_general(
            mixed[:quarter, lanes], mixing[...], CONTRACT_FIRST, preferred_element_type=F32
        )
        partial += lax.dot_general(
            mixed[quarter:, lanes], far[3 * quarter :], CONTRACT_FIRST, preferred_element_type=F32
        )
        kept[place] = partial[:rows]
        sent[place] = partial[rows:].astype(BF16)


def column(own, other, triple, mixing, piece, rest, plan, lines, shape):
    places, rows, model = shape
    quarter = mixing.shape[0]
    tokens = 2 * places * rows
    return pl.pallas_call(
        functools.partial(column_kernel, lines),
        out_shape=(
            jax.ShapeDtypeStruct(shape, F32),
            jax.ShapeDtypeStruct(shape, BF16),
        ),
        in_specs=[IN_SMEM] * 2 + [IN_VMEM] * (2 * PARTS + 2) + [IN_HBM] * 2,
        out_specs=(IN_VMEM, IN_VMEM),
        scratch_shapes=[
            pltpu.VMEM((places, 2 * rows, model), BF16),
            pltpu.VMEM((4 * quarter, model), BF16),
            pltpu.VMEM((3 * quarter, tokens), BF16),
            pltpu.VMEM((2 * quarter, tokens), BF16),
            pltpu.SemaphoreType.DMA((2,)),
        ],
        compiler_params=GRANT,
        name="column",
    )(plan[0], plan[2], *own, *other, triple.reshape(-1, model), mixing, piece, rest)


def finish_kernel(stream, first, second, got, out):
    places, rows, model = stream.shape
    parts, wide = out.shape[1] // 3, out.shape[2]
    quarter = wide // 2 * 3
    heads = model // quarter
    groups = out.shape[0] // heads
    lines = rows // groups
    for group in range(groups):
        these = slice(group * lines, (group + 1) * lines)
        total = jnp.concatenate([first[:, these], second[:, these]], axis=0)
        total += stream[:, these].astype(F32) + got[:, these].astype(F32)
        total = total.reshape(places * lines, model)
        for head in range(heads):
            block = total[:, head * quarter : (head + 1) * quarter]
            narrow = jnp.concatenate([block[:parts, wide:], block[parts:, wide:]], axis=1)
            block = jnp.concatenate([block[:, :wide], narrow], axis=0)
            out[group * heads + head] = block.astype(BF16)


def finish(stream, first, second, got, groups, quarter):
    places, rows, model = stream.shape
    heads, lines = model // quarter, rows // groups
    parts, wide = places * lines // 2, quarter // 3 * 2
    shape = (groups * heads, 3 * parts, wide)
    got = got.reshape(stream.shape)
    if parts % 16 == 0 and lines % 8 == 0 and places % 2 == 0:
        half = (places // 2, rows, model)
        first, second = first.reshape(half), second.reshape(half)
        return pl.pallas_call(
            finish_kernel,
            out_shape=jax.ShapeDtypeStruct(shape, BF16),
            in_specs=[IN_VMEM] * 4,
            out_specs=IN_VMEM,
            compiler_params=GRANT,
            name="finish",
        )(stream, first, second, got)
    kept = jnp.concatenate([first, second]).reshape(stream.shape)
    total = (stream.astype(F32) + kept + got.astype(F32)).astype(BF16)
    total = total.reshape(places, groups, lines, heads, quarter)
    total = jnp.transpose(total, (1, 3, 0, 2, 4)).reshape(-1, places * lines, quarter)
    narrow = jnp.concatenate([total[:, :parts, wide:], total[:, parts:, wide:]], axis=2)
    return jnp.concatenate([total[:, :, :wide], narrow], axis=1)


def feed_forward_kernel(
    me_ref, normed, expand, contract, piece, pair_rest, plane_rest, late, out,
    far_expand, far_contract, hidden, semaphores,
):
    width = expand.shape[1]
    count, half = pair_rest.shape[0], width // 2
    pair, plane = me_ref[3], me_ref[4]

    def move(source, start, count, target, place, index):
        return pltpu.make_async_copy(
            source.at[pl.ds(start, count)], target.at[pl.ds(place, count)], semaphores.at[index]
        )

    def by_pair(first, second):
        return [
            move(piece, 0, count, first, 0, 2),
            move(pair_rest, 0, count, second, 0, 3),
        ]

    def by_plane(first, second):
        return [
            move(piece, count, count, first, count, 4),
            move(plane_rest, 0, count, second, count, 5),
        ]

    copies = [
        move(late, 0, half, far_expand, half, 0),
        move(late, half, half, far_contract, half, 1),
    ]
    for copy in copies:
        copy.start()
    for place, moves in ((pair, by_pair), (plane, by_plane)):

        @pl.when(place == 0)
        def _(moves=moves):
            for copy in moves(far_expand, far_contract):
                copy.start()

        @pl.when(place != 0)
        def _(moves=moves):
            for copy in moves(far_contract, far_expand):
                copy.start()

    tile = width // 3
    values = normed[...]

    def raise_by(weights, lower):
        for start in range(0, width, tile):
            up = jnp.dot(values, weights[:, start : start + tile], preferred_element_type=F32)
            up = 0.5 * up * (1.0 + lax.erf(up * 2.0**-0.5))
            hidden[:, lower + start : lower + start + tile] = up.astype(BF16)

    copies += by_pair(far_expand, far_contract) + by_plane(far_expand, far_contract)
    raise_by(expand, 0)
    for copy in copies:
        copy.wait()
    raise_by(far_expand, width)
    down = jnp.dot(hidden[:, :width], contract[...], preferred_element_type=F32)
    down += jnp.dot(hidden[:, width:], far_contract[...], preferred_element_type=F32)
    out[...] = down.astype(out.dtype)


def feed_forward(normed, expand, contract, pieces, me, kind):
    tokens, model = normed.shape
    width = expand.shape[1]
    return pl.pallas_call(
        feed_forward_kernel,
        out_shape=jax.ShapeDtypeStruct((tokens, model), kind),
        in_specs=[IN_SMEM] + [IN_VMEM] * 3 + [IN_HBM] * 4,
        out_specs=IN_VMEM,
        scratch_shapes=[
            pltpu.VMEM((model, width), BF16),
            pltpu.VMEM((width, model), BF16),
            pltpu.VMEM((tokens, 2 * width), BF16),
            pltpu.SemaphoreType.DMA((6,)),
        ],
        compiler_params=GRANT,
        name="feed_forward",
    )(me, normed, expand, contract, *pieces)


def renew_kernel(stream, kept, got, after, normed, first, second):
    total = (stream[...].astype(F32) + kept[...] + got[...].astype(F32)).astype(BF16)
    after[...] = total
    values = total.astype(F32)
    centred = values - jnp.mean(values, axis=-1, keepdims=True)
    variance = jnp.mean(centred * centred, axis=-1, keepdims=True)
    values = (centred * lax.rsqrt(variance + 1e-05)).astype(BF16)
    normed[...] = values
    values = values.reshape(2 * first.shape[0], first.shape[1])
    first[...] = values[: first.shape[0]]
    second[...] = values[first.shape[0] :]


def renew(stream, kept, got):
    half = (stream.shape[0] * stream.shape[1] // 2, stream.shape[2])
    return pl.pallas_call(
        renew_kernel,
        out_shape=(jax.ShapeDtypeStruct(stream.shape, BF16),) * 2
        + (jax.ShapeDtypeStruct(half, BF16),) * 2,
        in_specs=[IN_VMEM] * 3,
        out_specs=(IN_VMEM,) * 4,
        compiler_params=GRANT,
        name="renew",
    )(stream, kept, got)


def shards(
    alignment_embedding,
    line_group_label,
    group_site_tally,
    horizontal_triple_matrix,
    horizontal_mixing_matrix,
    vertical_triple_matrix,
    vertical_mixing_matrix,
    expand_matrix,
    contract_matrix,
):
    lines, quarter, sites = alignment_embedding.shape
    row_groups = lax.axis_size(ROWS)
    own = lines // 2
    chips = 2 * row_groups
    place = sites // chips
    pair = lax.axis_index("pair")
    chip = lax.axis_index("chip")
    core = lax.axis_index("core")
    label, tally = line_group_label, group_site_tally
    families = tally.shape[0]
    starts = jnp.sum(label[:, None] < jnp.arange(families + 1), axis=0, dtype=jnp.int32)
    plane = lax.axis_index("plane")
    me = jnp.stack([lax.axis_index(ROWS), chip, core, pair, plane]).astype(jnp.int32)

    across = other_chip(alignment_embedding)
    near = other_core(alignment_embedding)
    pack, late = pack_weights(
        me,
        horizontal_mixing_matrix,
        vertical_triple_matrix,
        vertical_mixing_matrix,
        expand_matrix,
        contract_matrix,
    )
    stream, pack, late = lax.optimization_barrier((alignment_embedding, pack, late))
    stream = spread(stream, chips)
    stream = lax.all_to_all(stream, ROWS + ("chip", "core"), 0, 0, tiled=True)
    across, near, pack, late, starts, me = lax.optimization_barrier(
        (across, near, pack, late, starts, me)
    )
    plan = (me, label, starts, tally)
    piece = other_chip(pack)

    shared, inner_weights, values = row_front(
        (alignment_embedding, near, across, other_core(across)),
        horizontal_triple_matrix,
        plan,
        2 + max(min(families, lines) - 2, 1),
        row_groups,
    )
    shared, stream = lax.optimization_barrier((shared, stream))
    parts = lax.all_to_all(shared, ROWS, 0, 0, tiled=True)
    shared = lax.all_to_all(tie(parts, plan), ROWS, 0, 0, tiled=True)
    blocks = mix(shared, inner_weights, values, plan, chips)

    blocks, piece, late = lax.optimization_barrier((blocks, piece, late))
    half = expand_matrix.shape[0] // 2
    column_rest = other_pair(piece[half : 2 * half])
    feed_rest = (other_pair(piece[:quarter]), other_plane(piece[quarter:half]))
    late = other_chip(late)
    blocks = lax.all_to_all(blocks, ROWS + ("chip",), 0, 0, tiled=True)
    kept, *sent = project(blocks, horizontal_mixing_matrix, piece, me, lines)
    got = [other_core(part) for part in sent]
    got, column_rest = lax.optimization_barrier((got, column_rest))
    *normed, after_row = arrive(kept, got, stream, place)
    other = [other_core(part) for part in normed]

    kept, sent = column(
        normed,
        other,
        vertical_triple_matrix,
        vertical_mixing_matrix,
        piece,
        column_rest,
        plan,
        own,
        after_row.shape,
    )
    sent, feed_rest, late = lax.optimization_barrier((sent, feed_rest, late))
    after_col, normed, first, second = renew(after_row, kept, other_core(sent))

    weights = (expand_matrix, contract_matrix, (piece, *feed_rest, late), me)
    first = feed_forward(first, *weights, F32)
    other = other_core(normed).reshape(-1, normed.shape[-1])
    other, first = lax.optimization_barrier((other, first))
    sent = feed_forward(other, *weights, BF16)
    second = feed_forward(second, *weights, F32)
    blocks = finish(after_col, first, second, other_core(sent), row_groups, quarter)

    blocks = lax.all_to_all(blocks, ROWS + ("chip", "core"), 0, 0, tiled=True)
    parts, wide = own * place // 2, quarter // 3 * 2
    narrow = blocks[:, 2 * parts :]
    narrow = jnp.concatenate([narrow[:, :, : wide // 2], narrow[:, :, wide // 2 :]], axis=1)
    finished = jnp.concatenate([blocks[:, : 2 * parts], narrow], axis=2)
    finished = finished.reshape(chips, 2, place, own, quarter)
    finished = jnp.transpose(finished, (1, 3, 4, 0, 2))
    return finished.reshape(lines, quarter, sites)


def solution(mesh):
    far = mesh.shape["rows"] // 4
    split = Mesh(mesh.devices.reshape(far, 2, 2, 2, 2), ROWS + ("chip", "core"))
    heads = ("chip", "core")
    placed = (
        P(ROWS, heads, None),
        P(),
        P(),
        P(None, heads, None),
        P(heads, None),
        P(None, heads, None),
        P(heads, None),
        P(None, heads),
        P(heads, None),
    )
    return jax.shard_map(
        shards, mesh=split, in_specs=placed, out_specs=P(ROWS, heads, None), check_vma=False
    )
```
